32 devices in a mesh: gx: 4 (over z), gy: 4 (over x, core), gz: 2 (over y).
Axes of the slice: x: 2, y: 2, z: 4, core: 2. Of those that a mesh axis runs over, the one named last changes fastest.
Arguments:
- positions: float32 [4, 4, 2, 3, 256], P('gx', 'gy', 'gz'), may hold values from 0 to 1
- species: int32 [4, 4, 2, 256], P('gx', 'gy', 'gz'), may hold values from 0 to 1
- start_block: float32 [4, 4, 2, 4, 3, 256], P('gx', 'gy', 'gz'), may hold values from -560 to 560
- neighbors: int32 [4, 4, 2, 6, 256], P('gx', 'gy', 'gz'), may hold values from 0 to 1151, as said below
- ghost_lists: int32 [8, 8, 4, 16], P('gx', 'gy', 'gz'), may hold values from 0 to 255
- embedding: float32 [2, 64], replicated, may hold values from 0.5 to 1.5
- radial_in: float32 [8, 128], replicated, may hold values from -2 to 2
- radial_out: float32 [128, 64], replicated, may hold values from -0.5 to 0.5
- readout: float32 [64], replicated, may hold values from -0.75 to 0.75
Outputs:
- next_block: float32 [4, 4, 2, 4, 3, 256], P('gx', 'gy', 'gz')
- diagonal_blocks: float32 [2, 4, 4], replicated
- offdiagonal_blocks: float32 [2, 4, 4], replicated
The draws below stay inside these ranges and needn't reach their ends.
Inputs may be any that keep to these rules, and one draw needn't show every extreme that they name: `neighbors`: about two thirds of the slots name the device's own atoms, the rest ghost entries.
All inputs are finite; a program needn't handle non-finite values.
Results may differ from the reference program's by a relative error of at most 0.0003.
Values sent between devices are 32-bit elements; how exact they have to be, the bound alone decides.
No kernel may reach another device: no remote copies, remote signals or barrier semaphores. Data moves between devices by JAX's collectives and lax.ppermute only.
A program may use at most 192 MiB of HBM per device.

```python
import math
import jax
import jax.numpy as jnp
import numpy as np
from jax import lax

ATOMS_DEV = 256
NEIGHBORS = 6
CHANNELS = 64
RADIAL_HIDDEN = 128
BASIS = 8
SPECIES = 2
VECTORS = 4
PRODUCTS = 2
GHOSTS = 16
N_GX = 4
N_GY = 4
N_GZ = 2


def draw_start_block(key, part):
    base_key = jax.random.fold_in(key, 7)
    subkeys = jax.random.split(base_key, 3)
    shape_full = (N_GX, N_GY, N_GZ, VECTORS, 3, ATOMS_DEV)
    entries = jax.random.truncated_normal(subkeys[0], -4.0, 4.0, shape_full, jnp.float32)
    atom_scale = jnp.exp(jax.random.uniform(subkeys[1], (N_GX, N_GY, N_GZ, 1, 1, ATOMS_DEV), jnp.float32, 0.0, math.log(10.0)))
    column_scale = jnp.exp(jax.random.uniform(subkeys[2], (1, 1, 1, VECTORS, 1, 1), jnp.float32, 0.0, math.log(10.0)))
    return entries * atom_scale * column_scale


def draw_neighbors(key, part):
    base_key = jax.random.fold_in(key, 11)
    subkeys = jax.random.split(base_key, 3)
    shape_full = (N_GX, N_GY, N_GZ, NEIGHBORS, ATOMS_DEV)
    own_pick = jax.random.randint(subkeys[0], shape_full, 0, ATOMS_DEV, jnp.int32)
    ghost_pick = jax.random.randint(subkeys[1], shape_full, ATOMS_DEV, ATOMS_DEV + 56 * GHOSTS, jnp.int32)
    select = jax.random.randint(subkeys[2], shape_full, 0, 100, jnp.int32)
    combined_output = jnp.where(select < 35, ghost_pick, own_pick)
    combined_output = combined_output.at[:, :, :, 0, 0].set(0)
    combined_output = combined_output.at[:, :, :, 0, 1].set(ATOMS_DEV + 56 * GHOSTS - 1)
    return combined_output


def set_ends(drawn, stream_key, low, top_value):
    dims = drawn.shape
    place = [jax.random.randint(jax.random.fold_in(stream_key, axis), (), 0, dims[axis]) for axis in range(len(dims))]
    drawn = drawn.at[tuple(place)].set(low)
    longest = dims.index(max(dims))
    place[longest] = (place[longest] + 1) % dims[longest]
    return drawn.at[tuple(place)].set(top_value)


def shard_levels(own_key, dims, cuts, least, high):
    loudness, own = 1.0, jax.random.fold_in(own_key, 6)
    for dim, blocks in cuts:
        draws = jnp.exp(jax.random.uniform(jax.random.fold_in(own, dim), (blocks,), jnp.float32, least / len(cuts), high / len(cuts)))
        loudness = loudness * jnp.repeat(draws, dims[dim] // blocks).reshape([-1 if axis == dim else 1 for axis in range(len(dims))])
    return loudness


def scatter_about(key, shape, scale, most, kind=jnp.bfloat16):
    values = jax.random.normal(key, shape, jnp.float32) * scale
    return jnp.minimum(jnp.maximum(values, -most), most).astype(kind)


def setup_inputs(seed: int = 0) -> dict:
    key_list = jax.random.split(jax.random.key(seed), 10)
    positions = jnp.clip(1.0 * jax.random.uniform(key_list[0], (N_GX, N_GY, N_GZ, 3, ATOMS_DEV), jnp.float32) ** shard_levels(key_list[0], (N_GX, N_GY, N_GZ, 3, ATOMS_DEV), ((0, 4), (1, 4), (2, 2)), -0.2, 0.2), 0.0, 1.0)
    species = set_ends(jax.random.randint(key_list[1], (N_GX, N_GY, N_GZ, ATOMS_DEV), 0, SPECIES), jax.random.fold_in(key_list[1], 1), 0, SPECIES - 1).astype(jnp.int32)
    start_block = draw_start_block(jax.random.fold_in(key_list[9], 71), 0)
    neighbors = draw_neighbors(jax.random.fold_in(key_list[9], 71), 0)
    ghost_lists = set_ends(jax.random.randint(key_list[4], (2 * N_GX, 2 * N_GY, 2 * N_GZ, GHOSTS), 0, ATOMS_DEV), jax.random.fold_in(key_list[4], 1), 0, ATOMS_DEV - 1).astype(jnp.int32)
    embedding = jnp.clip(jax.random.uniform(key_list[5], (SPECIES, CHANNELS), jnp.float32, 0.5, 1.5), 0.5, 1.5)
    radial_in = scatter_about(key_list[6], (BASIS, RADIAL_HIDDEN), BASIS ** -0.5, 2.0, jnp.float32)
    radial_out = scatter_about(key_list[7], (RADIAL_HIDDEN, CHANNELS), RADIAL_HIDDEN ** -0.5, 0.5, jnp.float32)
    readout = scatter_about(key_list[8], (CHANNELS,), CHANNELS ** -0.5, 0.75, jnp.float32)
    return dict(positions=positions, species=species, start_block=start_block, neighbors=neighbors, ghost_lists=ghost_lists, embedding=embedding, radial_in=radial_in, radial_out=radial_out, readout=readout)


SOFTEN = 0.25
CUTOFF = 4.0
HIGHEST = lax.Precision.HIGHEST

def ghost_layout():
    chosen = []
    moves = []
    octants = []
    for number in range(64):
        coords = (number // 16, number // 4 % 4, number % 4)
        if all((member in (1, 2) for member in coords)):
            continue
        chosen.append(number)
        moves.append([int(member == 3) - int(member == 0) for member in coords])
        octants.append([(member + 1) % 2 for member in coords])
    return (np.array(chosen), np.array(moves), np.array(octants))

def block_energy(atom_table, embed_table, centers, neighbor, radial_in, radial_out, readout):
    fanout = neighbor.shape[0]
    width_block = neighbor.shape[1]
    flat_neighbor = neighbor.reshape(-1)
    center_coords = jnp.take(atom_table, centers, axis=1)
    neighbor_coords = jnp.take(atom_table, flat_neighbor, axis=1).reshape(3, fanout, width_block)
    displace = neighbor_coords - center_coords[:, None, :]
    distance = jnp.sqrt(lax.optimization_barrier(jnp.sum(displace * displace, axis=0)) + SOFTEN)
    direction = displace / distance[None]
    envelope = (1.0 - (distance / CUTOFF) ** 2) ** 2
    orders = jnp.arange(1, radial_in.shape[0] + 1).astype(jnp.float32)
    flat_distance = distance.reshape(-1)
    bessel = jnp.sin(orders[:, None] * (jnp.pi / CUTOFF) * flat_distance[None, :]) / flat_distance[None, :]
    hidden = jax.nn.silu(jnp.dot(radial_in.T, bessel, precision=HIGHEST))
    radial = jnp.dot(radial_out.T, hidden, precision=HIGHEST).reshape(-1, fanout, width_block)
    pairing = jnp.take(embed_table, centers, axis=1)[:, None, :] * jnp.take(embed_table, flat_neighbor, axis=1).reshape(-1, fanout, width_block)
    feature = radial * envelope[None] * pairing
    harmonic = jnp.concatenate([jnp.ones((1, fanout, width_block), jnp.float32), direction], axis=0)
    environ = jnp.einsum('ckb,mkb->cmb', feature, harmonic, precision=HIGHEST) / fanout
    project = jnp.einsum('cmb,mkb->ckb', environ, harmonic, precision=HIGHEST)
    mixed_feature = feature * project
    return jnp.sum(readout[:, None, None] * jax.nn.silu(mixed_feature))

def table_hessian(atom_table, embed_table, centers, neighbor, tangents, radial_in, radial_out, readout):

    def energy(coords):
        return block_energy(coords, embed_table, centers, neighbor, radial_in, radial_out, readout)
    forces = jax.grad(energy)

    def apply_one(tangent):
        return jax.jvp(forces, (atom_table,), (tangent,))[1]
    return jax.vmap(apply_one)(tangents)

def gather_cells(packets, moves, octants):
    pieces = []
    for cell_number in range(moves.shape[0]):
        shift_by = tuple((int(-member) for member in moves[cell_number]))
        rolled = jnp.roll(packets, shift_by, axis=(0, 1, 2))
        first, second, third = (int(member) for member in octants[cell_number])
        pieces.append(rolled[:, :, :, :, first, second, third, :])
    return jnp.stack(pieces, axis=4)

def return_cells(contrib, moves, octants):
    full_shape = contrib.shape
    running = jnp.zeros(full_shape[:4] + (2, 2, 2, full_shape[5]), jnp.float32)
    for cell_number in range(moves.shape[0]):
        shift_by = tuple((int(member) for member in moves[cell_number]))
        shifted = jnp.roll(contrib[:, :, :, :, cell_number], shift_by, axis=(0, 1, 2))
        first, second, third = (int(member) for member in octants[cell_number])
        running = running.at[:, :, :, :, first, second, third, :].add(shifted)
    return running

def reference(positions, species, start_block, neighbors, ghost_lists, embedding, radial_in, radial_out, readout):
    chosen, moves, octants = ghost_layout()
    count_dev = N_GX * N_GY * N_GZ
    atoms_dev = positions.shape[-1]
    ghosts = ghost_lists.shape[-1]
    octant_index_lists = ghost_lists.reshape(N_GX, 2, N_GY, 2, N_GZ, 2, ghosts).transpose(0, 2, 4, 1, 3, 5, 6).reshape(count_dev, 8 * ghosts)

    def pack_octants(values):
        selected = jax.vmap(lambda source_rows, gather_index: jnp.take(source_rows, gather_index, axis=1))(values, octant_index_lists)
        return selected.reshape(N_GX, N_GY, N_GZ, values.shape[1], 2, 2, 2, ghosts)
    flat_coords = positions.reshape(count_dev, 3, atoms_dev)
    flat_species = species.reshape(count_dev, 1, atoms_dev)
    offsets = jnp.asarray(moves.T, jnp.float32)
    ghost_coords = gather_cells(pack_octants(flat_coords), moves, octants) + offsets[None, None, None, :, :, None]
    ghost_species = gather_cells(pack_octants(flat_species), moves, octants)
    atom_tables = jnp.concatenate([flat_coords, ghost_coords.reshape(count_dev, 3, -1)], axis=2)
    species_tables = jnp.concatenate([flat_species[:, 0], ghost_species.reshape(count_dev, -1)], axis=1)
    embed_tables = jnp.swapaxes(jnp.take(embedding, species_tables, axis=0), 1, 2)
    neighbor_dev = neighbors.reshape(count_dev, neighbors.shape[3], atoms_dev)
    centers = jnp.arange(atoms_dev, dtype=jnp.int32)

    def apply_hessian(block):
        flat_block = block.reshape(count_dev, 3 * VECTORS, atoms_dev)
        ghost_tangent = gather_cells(pack_octants(flat_block), moves, octants)
        tangent_tables = jnp.concatenate([flat_block, ghost_tangent.reshape(count_dev, 3 * VECTORS, -1)], axis=2)
        tangent_tables = tangent_tables.reshape(count_dev, VECTORS, 3, -1)

        def one_device(inputs):
            atom_table, embed_table, neighbor, tangents = inputs
            return table_hessian(atom_table, embed_table, centers, neighbor, tangents, radial_in, radial_out, readout)
        images = lax.map(one_device, (atom_tables, embed_tables, neighbor_dev, tangent_tables))
        images = images.reshape(count_dev, 3 * VECTORS, -1)
        local_portion = images[:, :, :atoms_dev]
        ghost_part = images[:, :, atoms_dev:].reshape(N_GX, N_GY, N_GZ, 3 * VECTORS, chosen.shape[0], ghosts)
        octant_partial_sums = return_cells(ghost_part, moves, octants).reshape(count_dev, 3 * VECTORS, 8 * ghosts)
        combined_output = jax.vmap(lambda local_rows, partial_terms, gather_index: local_rows.at[:, gather_index].add(partial_terms))(local_portion, octant_partial_sums, octant_index_lists)
        return combined_output.reshape(count_dev, VECTORS, 3, atoms_dev)
    scale_ip = 1.0 / (3.0 * atoms_dev * count_dev)

    def mean_product(left_block, right_block):
        return jnp.einsum('dkca,dlca->kl', left_block, right_block, precision=HIGHEST) * scale_ip

    def combine(weights, block):
        return jnp.einsum('ij,dica->djca', weights, block, precision=HIGHEST)

    def solve_rows(factor, block):
        matrix = jnp.moveaxis(block, 1, 0).reshape(VECTORS, -1)
        solved = jax.scipy.linalg.solve_triangular(factor, matrix, lower=True)
        return jnp.moveaxis(solved.reshape(VECTORS, count_dev, 3, atoms_dev), 0, 1)
    initial = start_block.reshape(count_dev, VECTORS, 3, atoms_dev)
    factor = jnp.linalg.cholesky(mean_product(initial, initial))
    current = solve_rows(factor, initial)
    previous = jnp.zeros_like(current)
    diagonals = []
    couplings = []
    for step_number in range(PRODUCTS):
        product_block = apply_hessian(current)
        proj_current = mean_product(current, product_block)
        proj_previous = mean_product(previous, product_block)
        residue = product_block - combine(proj_current, current) - combine(proj_previous, previous)
        factor = jnp.linalg.cholesky(mean_product(residue, residue))
        previous, current = (current, solve_rows(factor, residue))
        diagonals.append(proj_current)
        couplings.append(factor.T)
    return (current.reshape(N_GX, N_GY, N_GZ, VECTORS, 3, atoms_dev), jnp.stack(diagonals), jnp.stack(couplings))
```

```python
import functools

import jax
import jax.numpy as jnp
import numpy as np
from jax import lax
from jax.experimental import pallas as pl
from jax.experimental.pallas import tpu as pltpu
from jax.sharding import PartitionSpec as P

SOFTEN = 0.25
CUTOFF = 4.0
HIGHEST = lax.Precision.HIGHEST
LANES = 128
GROUP = 8
AXES = ("gx", "gy", "gz")
VMEM_BYTES = 48 * 1024 * 1024


def swap_pairs(size, distance):
    return [(i, (i + distance) % size) for i in range(size)]


def octant_bit(shape, bit, ghosts):
    lane = lax.broadcasted_iota(jnp.int32, shape, 1) % (8 * ghosts)
    return (lane // ghosts // (4 >> bit)) % 2 == 1


def fetch_ghosts(x, bit, ghosts):
    axis = AXES[bit]
    size = lax.axis_size(axis)
    if size == 1:
        return x
    if size == 2:
        return lax.ppermute(x, axis, swap_pairs(2, 1))
    below = lax.ppermute(x, axis, swap_pairs(size, 1))
    above = lax.ppermute(x, axis, swap_pairs(size, -1))
    return jnp.where(octant_bit(x.shape, bit, ghosts), below, above)


def return_ghosts(x, bit, ghosts):
    axis = AXES[bit]
    size = lax.axis_size(axis)
    if size == 1:
        return x
    if size == 2:
        return lax.ppermute(x, axis, swap_pairs(2, 1))
    above = lax.ppermute(x, axis, swap_pairs(size, -1))
    below = lax.ppermute(x, axis, swap_pairs(size, 1))
    return jnp.where(octant_bit(x.shape, bit, ghosts), above, below)


def halo(octants, ghosts):
    first = fetch_ghosts(octants, 0, ghosts)
    level = jnp.concatenate([octants, first], axis=1)
    second = fetch_ghosts(level, 1, ghosts)
    level = jnp.concatenate([level, second], axis=1)
    third = fetch_ghosts(level, 2, ghosts)
    return first, second, third


def halo_back(first, second, third, ghosts):
    width = first.shape[1]
    got = return_ghosts(third, 2, ghosts)
    zero_part = got[:, :width]
    first = first + got[:, width : 2 * width]
    second = second + got[:, 2 * width :]
    got = return_ghosts(second, 1, ghosts)
    zero_part = zero_part + got[:, :width]
    first = first + got[:, width:]
    return zero_part + return_ghosts(first, 0, ghosts)


def sum_everywhere(x):
    for axis in AXES:
        size = lax.axis_size(axis)
        if size & (size - 1):
            x = lax.psum(x, axis)
            continue
        step = 1
        while step < size:
            x = x + lax.ppermute(x, axis, [(i, i ^ step) for i in range(size)])
            step *= 2
    return x


def rows(a):
    return slice(GROUP * a, GROUP * (a + 1))


def gather_lanes(table, index_row, group):
    lane = jnp.broadcast_to(index_row % LANES, (GROUP, LANES))
    tile = jnp.broadcast_to(index_row // LANES, (GROUP, LANES))
    out = None
    for number in range(table.shape[1] // LANES):
        source = table[rows(group), number * LANES : (number + 1) * LANES]
        picked = jnp.take_along_axis(source, lane, axis=1, mode="promise_in_bounds")
        out = picked if out is None else jnp.where(tile == number, picked, out)
    return out


def split_rows(y, vectors):
    high = y.astype(jnp.bfloat16).astype(jnp.float32)
    return high + pltpu.roll(y - high, vectors, 0)


def join_rows(y, vectors):
    return y + pltpu.roll(y, GROUP - vectors, 0)


def pack_kernel(pos_ref, spec_ref, block_ref, list_ref, own_ref, oct_ref):
    vectors = block_ref.shape[3]
    atoms = pos_ref.shape[-1]
    for a in range(3):
        parts = [block_ref[0, 0, 0, :, a, :], pos_ref[0, 0, 0, a : a + 1, :]]
        used = vectors + 1
        if a == 0:
            parts.append(spec_ref[0, 0].astype(jnp.float32))
            used += 1
        parts.append(jnp.zeros((GROUP - used, atoms), jnp.float32))
        own_ref[rows(a), :] = jnp.concatenate(parts, axis=0)
    pick_octants(own_ref, list_ref, oct_ref)


def pick_octants(own_ref, list_ref, oct_ref):
    for j in range(list_ref.shape[1] // LANES):
        cut = slice(j * LANES, (j + 1) * LANES)
        for a in range(3):
            oct_ref[rows(a), cut] = gather_lanes(own_ref, list_ref[:, cut], a)


def add_octants(own, octants, lists, vectors):
    atoms = own.shape[1]
    width = lists.shape[1]
    keep = lax.broadcasted_iota(jnp.int32, octants.shape, 0) < vectors
    packed = split_rows(jnp.where(keep, octants, 0.0), vectors).astype(jnp.bfloat16)
    onehot = lax.broadcasted_iota(jnp.int32, (atoms, width), 0) == lists
    spread = lax.dot_general(
        packed,
        jnp.where(onehot, 1.0, 0.0).astype(jnp.bfloat16),
        (((1,), (1,)), ((), ())),
        preferred_element_type=jnp.float32,
    )
    return own + join_rows(spread, vectors)


def fill_table(table, own_ref, ghost_refs, vectors, ghosts, shifted):
    atoms = own_ref.shape[1]
    table[:, :atoms] = own_ref[...]
    width = 8 * ghosts
    base = atoms
    kind = 1
    for ref in ghost_refs:
        for j in range(ref.shape[1] // width):
            part = ref[:, j * width : (j + 1) * width]
            if shifted:
                row = lax.broadcasted_iota(jnp.int32, part.shape, 0)
                for a in range(3):
                    if (kind >> a) & 1:
                        move = jnp.where(octant_bit(part.shape, a, ghosts), -1.0, 1.0)
                        part = part + jnp.where(row == GROUP * a + vectors, move, 0.0)
            table[:, base : base + width] = part
            base += width
            kind += 1


def gather_slot(table, idx_ref, k, atoms):
    pieces = [[] for _ in range(3)]
    for j in range(atoms // LANES):
        index_row = idx_ref[:, pl.ds(pl.multiple_of(k * atoms + j * LANES, LANES), LANES)]
        for a in range(3):
            pieces[a].append(gather_lanes(table, index_row, a))
    return [jnp.concatenate(p, axis=1) for p in pieces]


def slot_tangents(diff, unit, inv, tn, tdiff, lanes, vectors):
    tau = sum(unit[a] * diff[a] for a in range(3))
    nus = [(diff[a] - unit[a] * tau) * inv for a in range(3)]
    shape = tau.shape
    for v in range(vectors):
        for m, value in enumerate([tau] + nus):
            start = (v * 4 + m) * GROUP
            tn[start : start + GROUP, lanes] = jnp.broadcast_to(value[v : v + 1, :], shape)
    for a in range(3):
        tdiff[rows(a), lanes] = diff[a]
    tdiff[rows(3), lanes] = tau


def channel_products(f, f1, q, rp, rpp, unit, env, tn, acc, half, atoms, fanout, vectors):
    share = 1.0 / fanout
    rpf = [rp[k] * f[k] for k in range(fanout)]
    for v in range(vectors):

        def get(m, k):
            start = (v * 4 + m) * GROUP
            return tn[start : start + GROUP, pl.ds(k * atoms + half, LANES)]

        phi = [f1[k] * get(0, k) for k in range(fanout)]
        de = [share * sum(phi)]
        for a in range(3):
            de.append(
                share * sum(phi[k] * unit(a, k) + f[k] * get(1 + a, k) for k in range(fanout))
            )
        y = []
        hde = []
        for k in range(fanout):
            turn = de[0] + sum(unit(a, k) * de[1 + a] for a in range(3))
            hde.append(turn)
            bend = turn + sum(get(1 + a, k) * env[1 + a] for a in range(3))
            y.append(rpp[k] * (phi[k] * q[k] + f[k] * bend))
        w = [y[k] * f[k] + rp[k] * phi[k] for k in range(fanout)]
        total = [share * sum(w)]
        for a in range(3):
            total.append(
                share * sum(w[k] * unit(a, k) + rpf[k] * get(1 + a, k) for k in range(fanout))
            )
        for k in range(fanout):
            along = total[0] + sum(unit(a, k) * total[1 + a] for a in range(3))
            terms = [f1[k] * (y[k] * q[k] + rp[k] * hde[k] + along)]
            for a in range(3):
                terms.append(f[k] * (y[k] * env[1 + a] + rp[k] * de[1 + a] + total[1 + a]))
            for m in range(4):
                start = (v * 4 + m) * GROUP
                acc[start : start + GROUP, pl.ds(k * atoms + half, LANES)] += terms[m]


def finish_product(
    idx_ref, unit_ref, inv_ref, bend_ref, acc, tdiff, scat, center, own_out, ghost_out, vectors
):
    atoms = center.shape[1]
    fanout = idx_ref.shape[1] // atoms
    tiles = scat.shape[0] // (3 * GROUP)
    scat[...] = jnp.zeros_like(scat)
    center[...] = jnp.zeros_like(center)

    def slot(k, carry):
        lanes = pl.ds(pl.multiple_of(k * atoms, LANES), atoms)
        row = lax.broadcasted_iota(jnp.int32, (GROUP, atoms), 0)
        outs = []
        for m in range(4):
            value = jnp.zeros((GROUP, atoms), jnp.float32)
            for v in range(vectors):
                start = (v * 4 + m) * GROUP
                part = jnp.sum(acc[start : start + GROUP, lanes], axis=0, keepdims=True)
                value = jnp.where(row == v, part, value)
            outs.append(value)
        unit = [unit_ref[rows(a), lanes] for a in range(3)]
        inv = inv_ref[:, lanes]
        diff = [tdiff[rows(a), lanes] for a in range(3)]
        tau = tdiff[rows(3), lanes]
        bend = bend_ref[:, lanes]
        stretch, turn = bend[0:1], bend[1:2]
        mix = [bend[2 + a : 3 + a] for a in range(3)]
        inner = sum(unit[a] * outs[1 + a] for a in range(3))
        along = (
            outs[0]
            - inner * inv
            + (stretch - turn) * tau
            + sum(mix[a] * diff[a] for a in range(3))
        )
        packed = []
        for a in range(3):
            y = along * unit[a] + outs[1 + a] * inv + turn * diff[a] + mix[a] * tau
            y = jnp.where(row < vectors, y, 0.0)
            center[rows(a), :] -= y
            packed.append(split_rows(y, vectors))
        packed = jnp.concatenate(packed, axis=0)
        index_row = idx_ref[:, lanes]
        tile = index_row // LANES
        low = lax.broadcasted_iota(jnp.int32, (LANES, atoms), 0) == index_row % LANES
        left = jnp.concatenate(
            [jnp.where(tile == number, packed, 0.0) for number in range(tiles)], axis=0
        ).astype(jnp.bfloat16)
        right = jnp.where(low, 1.0, 0.0).astype(jnp.bfloat16)
        scat[...] += lax.dot_general(
            left, right, (((1,), (1,)), ((), ())), preferred_element_type=jnp.float32
        )
        return carry

    lax.fori_loop(0, fanout, slot, 0)
    own_tiles = atoms // LANES
    for number in range(tiles):
        for a in range(3):
            start = (number * 3 + a) * GROUP
            value = join_rows(scat[start : start + GROUP, :], vectors)
            if number < own_tiles:
                cut = slice(number * LANES, (number + 1) * LANES)
                own_out[rows(a), cut] = value + center[rows(a), cut]
            else:
                cut = number - own_tiles
                ghost_out[rows(a), cut * LANES : (cut + 1) * LANES] = value


def first_kernel(
    ghosts,
    vectors,
    idx_ref,
    own_ref,
    g1_ref,
    g2_ref,
    g3_ref,
    emb_ref,
    rin_ref,
    rout_ref,
    read_ref,
    own_out,
    ghost_out,
    unit_ref,
    inv_ref,
    bend_ref,
    f_ref,
    f1_ref,
    q_ref,
    rp_ref,
    rpp_ref,
    env_ref,
    table,
    f2_ref,
    tn,
    tdiff,
    acc,
    acc2,
    scat,
    center,
):
    atoms = own_ref.shape[1]
    fanout = idx_ref.shape[1] // atoms
    channels, species = emb_ref.shape
    basis = rin_ref.shape[1]
    fill_table(table, own_ref, (g1_ref, g2_ref, g3_ref), vectors, ghosts, True)

    def embed(kind):
        value = emb_ref[:, 0:1]
        for s in range(1, species):
            value = jnp.where(kind == float(s), emb_ref[:, s : s + 1], value)
        return value

    own_embed = embed(own_ref[vectors + 1 : vectors + 2, :])

    def slot(k, carry):
        lanes = pl.ds(pl.multiple_of(k * atoms, LANES), atoms)
        near = gather_slot(table, idx_ref, k, atoms)
        diff = [near[a] - own_ref[rows(a), :] for a in range(3)]
        delta = [
            jnp.broadcast_to(diff[a][vectors : vectors + 1, :], (GROUP, atoms)) for a in range(3)
        ]
        dist = jnp.sqrt(delta[0] * delta[0] + delta[1] * delta[1] + delta[2] * delta[2] + SOFTEN)
        inv = 1.0 / dist
        unit = [delta[a] * inv for a in range(3)]
        for a in range(3):
            unit_ref[rows(a), lanes] = unit[a]
        inv_ref[:, lanes] = inv
        slot_tangents(diff, unit, inv, tn, tdiff, lanes, vectors)
        one = dist[0:1]
        inv_one = inv[0:1]
        order = (lax.broadcasted_iota(jnp.int32, (basis, atoms), 0) + 1).astype(jnp.float32)
        turns = order * (one * (1.0 / CUTOFF))
        whole = jnp.floor(turns + 0.5)
        rest = turns - whole
        odd = whole - 2.0 * jnp.floor(whole * 0.5)
        sign = 1.0 - 2.0 * odd
        x = rest * np.float32(np.pi)
        x2 = x * x
        sine = x * (
            1.0
            + x2
            * (
                -1.0 / 6
                + x2
                * (1.0 / 120 + x2 * (-1.0 / 5040 + x2 * (1.0 / 362880 + x2 * (-1.0 / 39916800))))
            )
        )
        cosine = 1.0 + x2 * (
            -0.5
            + x2
            * (
                1.0 / 24
                + x2
                * (
                    -1.0 / 720
                    + x2 * (1.0 / 40320 + x2 * (-1.0 / 3628800 + x2 * (1.0 / 479001600)))
                )
            )
        )
        sine = sine * sign
        cosine = cosine * sign
        omega = order * np.float32(np.pi / CUTOFF)
        b0 = sine * inv_one
        b1 = (omega * cosine - b0) * inv_one
        b2 = -(omega * omega * sine + 2.0 * b1) * inv_one
        z = jnp.dot(
            rin_ref[...],
            jnp.concatenate([b0, b1, b2], axis=1),
            precision=HIGHEST,
            preferred_element_type=jnp.float32,
        )
        z0, z1, z2 = z[:, :atoms], z[:, atoms : 2 * atoms], z[:, 2 * atoms :]
        sig = 1.0 / (1.0 + jnp.exp(-z0))
        anti = 1.0 - sig
        slope = sig * (1.0 + z0 * anti)
        curve = sig * anti * (2.0 + z0 * (anti - sig))
        hidden = jnp.concatenate(
            [z0 * sig, slope * z1, curve * z1 * z1 + slope * z2], axis=1
        )
        radial = jnp.dot(
            rout_ref[...], hidden, precision=HIGHEST, preferred_element_type=jnp.float32
        )
        r0, r1, r2 = radial[:, :atoms], radial[:, atoms : 2 * atoms], radial[:, 2 * atoms :]
        square = one * one
        base = 1.0 - square * (1.0 / CUTOFF**2)
        v0 = base * base
        v1 = base * one * (-4.0 / CUTOFF**2)
        v2 = -4.0 / CUTOFF**2 + square * (12.0 / CUTOFF**4)
        pair = own_embed * embed(near[0][vectors + 1 : vectors + 2, :])
        f_ref[:, lanes] = pair * (r0 * v0)
        f1_ref[:, lanes] = pair * (r1 * v0 + r0 * v1)
        f2_ref[:, lanes] = pair * (r2 * v0 + 2.0 * (r1 * v1) + r0 * v2)
        return carry

    lax.fori_loop(0, fanout, slot, 0)
    acc[...] = jnp.zeros_like(acc)
    acc2[...] = jnp.zeros_like(acc2)
    halves = atoms // LANES
    share = 1.0 / fanout

    def tile(number, carry):
        start = pl.multiple_of((number // halves) * GROUP, GROUP)
        half = pl.multiple_of((number % halves) * LANES, LANES)
        here = pl.ds(start, GROUP)

        def cut(k):
            return pl.ds(pl.multiple_of(k * atoms + half, LANES), LANES)

        def unit(a, k):
            return unit_ref[rows(a), cut(k)]

        slots = range(fanout)
        f = [f_ref[here, cut(k)] for k in slots]
        f1 = [f1_ref[here, cut(k)] for k in slots]
        read = jnp.broadcast_to(read_ref[here, :], (GROUP, LANES))
        env = [share * sum(f)]
        for a in range(3):
            env.append(share * sum(f[k] * unit(a, k) for k in slots))
        q, rp, rpp = [], [], []
        for k in slots:
            project = env[0] + sum(unit(a, k) * env[1 + a] for a in range(3))
            x = f[k] * project
            sig = 1.0 / (1.0 + jnp.exp(-x))
            anti = 1.0 - sig
            q.append(project)
            rp.append(read * (sig * (1.0 + x * anti)))
            rpp.append(read * (sig * anti * (2.0 + x * (anti - sig))))
            q_ref[here, cut(k)] = q[k]
            rp_ref[here, cut(k)] = rp[k]
            rpp_ref[here, cut(k)] = rpp[k]
        for m in range(4):
            env_ref[pl.ds(m * channels + start, GROUP), pl.ds(half, LANES)] = env[m]
        rpf = [rp[k] * f[k] for k in slots]
        total = [share * sum(rpf)]
        for a in range(3):
            total.append(share * sum(rpf[k] * unit(a, k) for k in slots))
        for k in slots:
            g = [rp[k] * env[m] + total[m] for m in range(4)]
            gamma = g[0] + sum(unit(a, k) * g[1 + a] for a in range(3))
            terms = [f2_ref[here, cut(k)] * gamma, f1[k] * g[0]]
            terms += [f1[k] * g[1 + a] for a in range(3)]
            terms += [f[k] * g[1 + a] for a in range(3)]
            for m, term in enumerate(terms):
                acc2[m * GROUP : (m + 1) * GROUP, cut(k)] += term
        channel_products(
            f, f1, q, rp, rpp, unit, env, tn, acc, half, atoms, fanout, vectors
        )
        return carry

    lax.fori_loop(0, (channels // GROUP) * halves, tile, 0)

    def bend_slot(k, carry):
        lanes = pl.ds(pl.multiple_of(k * atoms, LANES), atoms)
        sums = [
            jnp.sum(acc2[m * GROUP : (m + 1) * GROUP, lanes], axis=0, keepdims=True)
            for m in range(8)
        ]
        inv = inv_ref[0:1, lanes]
        unit = [unit_ref[GROUP * a : GROUP * a + 1, lanes] for a in range(3)]
        up = sum(unit[a] * sums[2 + a] for a in range(3))
        uw = sum(unit[a] * sums[5 + a] for a in range(3))
        turn = (sums[1] + up - uw * inv) * inv
        mix = [
            ((sums[2 + a] - unit[a] * up) - (sums[5 + a] - unit[a] * uw) * inv) * inv
            for a in range(3)
        ]
        pad = jnp.zeros((GROUP - 5, atoms), jnp.float32)
        bend_ref[:, lanes] = jnp.concatenate([sums[0], turn] + mix + [pad], axis=0)
        return carry

    lax.fori_loop(0, fanout, bend_slot, 0)
    finish_product(
        idx_ref, unit_ref, inv_ref, bend_ref, acc, tdiff, scat, center, own_out, ghost_out, vectors
    )


def second_kernel(
    ghosts,
    vectors,
    idx_ref,
    own_ref,
    g1_ref,
    g2_ref,
    g3_ref,
    unit_ref,
    inv_ref,
    bend_ref,
    f_ref,
    f1_ref,
    q_ref,
    rp_ref,
    rpp_ref,
    env_ref,
    own_out,
    ghost_out,
    table,
    tn,
    tdiff,
    acc,
    scat,
    center,
):
    atoms = own_ref.shape[1]
    fanout = idx_ref.shape[1] // atoms
    channels = f_ref.shape[0]
    fill_table(table, own_ref, (g1_ref, g2_ref, g3_ref), vectors, ghosts, False)

    def slot(k, carry):
        lanes = pl.ds(pl.multiple_of(k * atoms, LANES), atoms)
        near = gather_slot(table, idx_ref, k, atoms)
        diff = [near[a] - own_ref[rows(a), :] for a in range(3)]
        unit = [unit_ref[rows(a), lanes] for a in range(3)]
        slot_tangents(diff, unit, inv_ref[:, lanes], tn, tdiff, lanes, vectors)
        return carry

    lax.fori_loop(0, fanout, slot, 0)
    acc[...] = jnp.zeros_like(acc)
    halves = atoms // LANES

    def tile(number, carry):
        start = pl.multiple_of((number // halves) * GROUP, GROUP)
        half = pl.multiple_of((number % halves) * LANES, LANES)
        here = pl.ds(start, GROUP)

        def cut(k):
            return pl.ds(pl.multiple_of(k * atoms + half, LANES), LANES)

        def unit(a, k):
            return unit_ref[rows(a), cut(k)]

        def load(ref):
            return [ref[here, cut(k)] for k in range(fanout)]

        env = [
            env_ref[pl.ds(m * channels + start, GROUP), pl.ds(half, LANES)] for m in range(4)
        ]
        channel_products(
            load(f_ref),
            load(f1_ref),
            load(q_ref),
            load(rp_ref),
            load(rpp_ref),
            unit,
            env,
            tn,
            acc,
            half,
            atoms,
            fanout,
            vectors,
        )
        return carry

    lax.fori_loop(0, (channels // GROUP) * halves, tile, 0)
    finish_product(
        idx_ref, unit_ref, inv_ref, bend_ref, acc, tdiff, scat, center, own_out, ghost_out, vectors
    )


def middle_kernel(vectors, own_ref, sums_ref, list_ref, full_ref, oct_ref):
    for a in range(3):
        full_ref[rows(a), :] = add_octants(
            own_ref[rows(a), :], sums_ref[rows(a), :], list_ref[...], vectors
        )
    pick_octants(full_ref, list_ref, oct_ref)


def gram_kernel(vectors, start_ref, first_ref, own_ref, sums_ref, list_ref, full_ref, gram_ref):
    total = jnp.zeros(gram_ref.shape, jnp.float32)
    for a in range(3):
        second = add_octants(own_ref[rows(a), :], sums_ref[rows(a), :], list_ref[...], vectors)
        full_ref[rows(a), :] = second
        stack = jnp.concatenate([start_ref[rows(a), :], first_ref[rows(a), :], second], axis=0)
        row = lax.broadcasted_iota(jnp.int32, stack.shape, 0)
        stack = jnp.where(row % GROUP < vectors, stack, 0.0)
        pad = jnp.zeros((gram_ref.shape[1] - stack.shape[0], stack.shape[1]), jnp.float32)
        total += lax.dot_general(
            stack,
            jnp.concatenate([stack, pad], axis=0),
            (((1,), (1,)), ((), ())),
            precision=HIGHEST,
            preferred_element_type=jnp.float32,
        )
    gram_ref[...] = total


def last_kernel(
    vectors, scale, start_ref, first_ref, second_ref, gram_ref, next_ref, diag_ref, off_ref
):
    shape = (GROUP, LANES)
    row = lax.broadcasted_iota(jnp.int32, shape, 0)
    lane = lax.broadcasted_iota(jnp.int32, shape, 1)
    inside = (row < vectors) & (lane < vectors)
    eye = jnp.where((row == lane) & inside, 1.0, 0.0)

    def block(i, j):
        part = gram_ref[rows(i), :]
        if j:
            part = pltpu.roll(part, LANES - GROUP * j, 1)
        return jnp.where(inside, part * scale, 0.0)

    def mul(x, y):
        return sum(x[:, k : k + 1] * y[k : k + 1, :] for k in range(vectors))

    def flip(x):
        out = jnp.zeros(shape, jnp.float32)
        for k in range(vectors):
            line = jnp.sum(eye * x[:, k : k + 1], axis=0, keepdims=True)
            out = jnp.where(row == k, line, out)
        return out

    def factor(m):
        upper = jnp.zeros(shape, jnp.float32)
        inverse = eye
        for j in range(vectors):
            scale_j = 1.0 / jnp.sqrt(m[j : j + 1, j : j + 1])
            column = m[:, j : j + 1] * scale_j
            line = m[j : j + 1, :] * scale_j
            upper = jnp.where((row == j) & (lane >= j), line, upper)
            m = m - column * line
            own = inverse[j : j + 1, :] * scale_j
            inverse = jnp.where(
                row == j, own, jnp.where(row > j, inverse - column * own, inverse)
            )
        return upper, inverse

    ss, su, uu = block(0, 0), block(0, 1), block(1, 1)
    sq, uq, qq = block(0, 2), block(1, 2), block(2, 2)
    qu = block(2, 1)
    _, p0 = factor(ss)
    p0t = flip(p0)
    a1 = mul(mul(p0, su), p0t)
    a1t = flip(a1)
    up1, p1 = factor(mul(mul(p0, uu), p0t) - mul(a1t, a1))
    b = mul(p1, p0)
    a = -mul(p1, mul(a1t, p0))
    at, bt = flip(a), flip(b)
    right_s = mul(su, at) + mul(sq, bt)
    right_u = mul(uu, at) + mul(uq, bt)
    right_q = mul(qu, at) + mul(qq, bt)
    a2 = mul(a, right_s) + mul(b, right_u)
    c2 = mul(p0, right_s)
    ww = mul(a, right_u) + mul(b, right_q)
    a2t, c2t = flip(a2), flip(c2)
    up2, p2 = factor(ww - mul(a2t, a2) - mul(c2t, c2))
    weights = (
        -mul(p2, mul(a2t, a) + mul(c2t, p0)),
        mul(p2, a - mul(a2t, b)),
        mul(p2, b),
    )
    small = (slice(0, vectors), slice(0, vectors))
    diag_ref[0] = a1[small]
    diag_ref[1] = a2[small]
    off_ref[0] = up1[small]
    off_ref[1] = up2[small]
    for comp in range(3):
        value = None
        for weight, ref in zip(weights, (start_ref, first_ref, second_ref)):
            for w in range(vectors):
                line = GROUP * comp + w
                term = weight[:, w : w + 1] * ref[line : line + 1, :]
                value = term if value is None else value + term
        next_ref[0, 0, 0, :, comp, :] = value[:vectors]


def call(body, outs, args, scratch=()):
    return pl.pallas_call(
        body,
        out_shape=[jax.ShapeDtypeStruct(shape, jnp.float32) for shape in outs],
        in_specs=[pl.BlockSpec(memory_space=pltpu.VMEM)] * len(args),
        out_specs=[pl.BlockSpec(memory_space=pltpu.VMEM)] * len(outs),
        scratch_shapes=[pltpu.VMEM(shape, jnp.float32) for shape in scratch],
        compiler_params=pltpu.CompilerParams(vmem_limit_bytes=VMEM_BYTES),
    )(*args)


def table_index(neighbors, atoms, ghosts):
    entry = neighbors - atoms
    cell = entry // ghosts
    number = cell
    kept = [n for n in range(64) if not all(m in (1, 2) for m in (n // 16, n // 4 % 4, n % 4))]
    previous = -1
    for position, n in enumerate(kept):
        if n - previous > 1:
            number = number + jnp.where(cell >= position, n - previous - 1, 0)
        previous = n
    member = (number // 16, number // 4 % 4, number % 4)
    kind = 0
    octant = 0
    for bit, m in enumerate(member):
        kind = kind + jnp.where((m == 0) | (m == 3), 1 << bit, 0)
        octant = 2 * octant + (m + 1) % 2
    place = atoms + (kind - 1) * (8 * ghosts) + octant * ghosts + entry % ghosts
    return jnp.where(neighbors < atoms, neighbors, place)


def on_device(
    positions,
    species,
    start_block,
    neighbors,
    ghost_lists,
    embedding,
    radial_in,
    radial_out,
    readout,
):
    atoms = positions.shape[-1]
    ghosts = ghost_lists.shape[-1]
    vectors = start_block.shape[3]
    fanout = neighbors.shape[3]
    channels = embedding.shape[1]
    devices = lax.axis_size("gx") * lax.axis_size("gy") * lax.axis_size("gz")
    scale = 1.0 / (3.0 * atoms * devices)
    width = 8 * ghosts
    high = 3 * GROUP
    edges = fanout * atoms
    lists = ghost_lists.reshape(1, width)
    index = table_index(neighbors.reshape(1, -1), atoms, ghosts)
    table_width = atoms + 7 * width
    tiles = table_width // LANES

    own, octants = call(
        pack_kernel,
        [(high, atoms), (high, width)],
        (positions, species, start_block, lists),
    )
    ghost_parts = halo(octants, ghosts)
    shared = [
        (vectors * 4 * GROUP, edges),
        (4 * GROUP, edges),
        (vectors * 4 * GROUP, edges),
    ]
    tail = [(tiles * high, LANES), (high, atoms)]
    saved_shapes = [
        (high, edges),
        (GROUP, edges),
        (GROUP, edges),
        (channels, edges),
        (channels, edges),
        (channels, edges),
        (channels, edges),
        (channels, edges),
        (4 * channels, atoms),
    ]
    results = call(
        functools.partial(first_kernel, ghosts, vectors),
        [(high, atoms), (high, 7 * width)] + saved_shapes,
        (index, own) + ghost_parts
        + (embedding.T, radial_in.T, radial_out.T, readout.reshape(-1, 1)),
        [(high, table_width), (channels, edges)] + shared + [(8 * GROUP, edges)] + tail,
    )
    own_terms, ghost_terms, saved = results[0], results[1], results[2:]

    def back(terms):
        return halo_back(
            terms[:, :width], terms[:, width : 3 * width], terms[:, 3 * width :], ghosts
        )

    first, octants = call(
        functools.partial(middle_kernel, vectors),
        [(high, atoms), (high, width)],
        (own_terms, back(ghost_terms), lists),
    )
    ghost_parts = halo(octants, ghosts)
    own_terms, ghost_terms = call(
        functools.partial(second_kernel, ghosts, vectors),
        [(high, atoms), (high, 7 * width)],
        (index, first) + ghost_parts + tuple(saved),
        [(high, table_width)] + shared + tail,
    )
    second, gram = call(
        functools.partial(gram_kernel, vectors),
        [(high, atoms), (high, LANES)],
        (own, first, own_terms, back(ghost_terms), lists),
    )
    gram = sum_everywhere(gram)
    return tuple(
        call(
            functools.partial(last_kernel, vectors, scale),
            [(1, 1, 1, vectors, 3, atoms), (2, vectors, vectors), (2, vectors, vectors)],
            (own, first, second, gram),
        )
    )


def solution(mesh):
    return jax.shard_map(
        on_device,
        mesh=mesh,
        in_specs=(
            P("gx", "gy", "gz", None, None),
            P("gx", "gy", "gz", None),
            P("gx", "gy", "gz", None, None, None),
            P("gx", "gy", "gz", None, None),
            P("gx", "gy", "gz", None),
            P(),
            P(),
            P(),
            P(),
        ),
        out_specs=(P("gx", "gy", "gz", None, None, None), P(), P()),
        check_vma=False,
    )
```

```python
import functools

import jax
import jax.numpy as jnp
import numpy as np
from jax import lax
from jax.experimental import pallas as pl
from jax.experimental.pallas import tpu as pltpu
from jax.sharding import PartitionSpec as P

SOFTEN = 0.25
CUTOFF = 4.0
HIGHEST = lax.Precision.HIGHEST
LANES = 128
GROUP = 8
AXES = ("gx", "gy", "gz")
VMEM_BYTES = 48 * 1024 * 1024


def swap_pairs(size, distance):
    return [(i, (i + distance) % size) for i in range(size)]


def octant_bit(shape, bit, ghosts):
    lane = lax.broadcasted_iota(jnp.int32, shape, 1) % (8 * ghosts)
    return (lane // ghosts // (4 >> bit)) % 2 == 1


def pair_exchange(x, axis, distances):
    size = lax.axis_size(axis)
    return [lax.ppermute(x, axis, [(i, i ^ d) for i in range(size)]) for d in distances]


def ring_sides(x, bit):
    axis = AXES[bit]
    size = lax.axis_size(axis)
    if size == 4:
        near, far = pair_exchange(x, axis, (1, 3))
        return near, far, lax.axis_index(axis) % 2 == 1
    above = lax.ppermute(x, axis, swap_pairs(size, -1))
    below = lax.ppermute(x, axis, swap_pairs(size, 1))
    return above, below, False


def fetch_ghosts(x, bit, ghosts):
    axis = AXES[bit]
    size = lax.axis_size(axis)
    if size == 1:
        return x
    if size == 2:
        return lax.ppermute(x, axis, swap_pairs(2, 1))
    near, far, odd = ring_sides(x, bit)
    return jnp.where(octant_bit(x.shape, bit, ghosts) ^ odd, far, near)


def return_ghosts(x, bit, ghosts):
    axis = AXES[bit]
    size = lax.axis_size(axis)
    if size == 1:
        return x
    if size == 2:
        return lax.ppermute(x, axis, swap_pairs(2, 1))
    near, far, odd = ring_sides(x, bit)
    return jnp.where(octant_bit(x.shape, bit, ghosts) ^ odd, near, far)


def spread_outer(level, ghosts):
    second = fetch_ghosts(level, 1, ghosts)
    level = jnp.concatenate([level, second], axis=1)
    return second, fetch_ghosts(level, 2, ghosts)


def return_outer(terms, width, ghosts):
    got = return_ghosts(terms[:, 3 * width :], 2, ghosts)
    inner = got[:, :width]
    first = terms[:, :width] + got[:, width : 2 * width]
    second = terms[:, width : 3 * width] + got[:, 2 * width :]
    got = return_ghosts(second, 1, ghosts)
    return inner + got[:, :width], first + got[:, width:]


def sum_over(x, axes):
    for axis in axes:
        size = lax.axis_size(axis)
        if size & (size - 1):
            x = lax.psum(x, axis)
            continue
        step = 1
        while step < size:
            x = x + lax.ppermute(x, axis, [(i, i ^ step) for i in range(size)])
            step *= 2
    return x


def rows(a):
    return slice(GROUP * a, GROUP * (a + 1))


def gather_lanes(table, index_row, group):
    lane = jnp.broadcast_to(index_row % LANES, (GROUP, LANES))
    tile = jnp.broadcast_to(index_row // LANES, (GROUP, LANES))
    out = None
    for number in range(table.shape[1] // LANES):
        source = table[rows(group), number * LANES : (number + 1) * LANES]
        picked = jnp.take_along_axis(source, lane, axis=1, mode="promise_in_bounds")
        out = picked if out is None else jnp.where(tile == number, picked, out)
    return out


def column(line):
    size = line.shape[1]
    shape = (size, size)
    same = lax.broadcasted_iota(jnp.int32, shape, 0) == lax.broadcasted_iota(jnp.int32, shape, 1)
    return jnp.sum(jnp.where(same, line, 0.0), axis=1, keepdims=True)


def split_rows(y, vectors):
    high = y.astype(jnp.bfloat16).astype(jnp.float32)
    return high + pltpu.roll(y - high, vectors, 0)


def join_rows(y, vectors):
    return y + pltpu.roll(y, GROUP - vectors, 0)


def pack_kernel(pos_ref, spec_ref, block_ref, raw_ref, own_ref, oct_ref, list_ref):
    vectors = block_ref.shape[4]
    atoms = pos_ref.shape[-1]
    for a in range(3):
        parts = [block_ref[0, 0, 0, a], pos_ref[0, 0, 0, a : a + 1, :]]
        used = vectors + 1
        if a == 0:
            parts.append(spec_ref[0, 0].astype(jnp.float32))
            used += 1
        parts.append(jnp.zeros((GROUP - used, atoms), jnp.float32))
        own_ref[rows(a), :] = jnp.concatenate(parts, axis=0)
    pieces = [raw_ref[n // 4, n // 2 % 2, n % 2 : n % 2 + 1, :] for n in range(8)]
    list_ref[...] = jnp.concatenate(pieces, axis=1)
    pick_octants(own_ref, list_ref, oct_ref)


def pick_octants(own_ref, list_ref, oct_ref):
    for j in range(list_ref.shape[1] // LANES):
        cut = slice(j * LANES, (j + 1) * LANES)
        for a in range(3):
            oct_ref[rows(a), cut] = gather_lanes(own_ref, list_ref[:, cut], a)


def add_octants(own, octants, lists, vectors):
    atoms = own.shape[1]
    width = lists.shape[1]
    keep = lax.broadcasted_iota(jnp.int32, octants.shape, 0) < vectors
    packed = split_rows(jnp.where(keep, octants, 0.0), vectors).astype(jnp.bfloat16)
    onehot = lax.broadcasted_iota(jnp.int32, (atoms, width), 0) == lists
    spread = lax.dot_general(
        packed,
        jnp.where(onehot, 1.0, 0.0).astype(jnp.bfloat16),
        (((1,), (1,)), ((), ())),
        preferred_element_type=jnp.float32,
    )
    return own + join_rows(spread, vectors)


def fill_table(table, own_ref, ghost_refs, vectors, ghosts, shifted):
    atoms = own_ref.shape[1]
    table[:, :atoms] = own_ref[...]
    width = 8 * ghosts
    base = atoms
    kind = 1
    for number, ref in enumerate(ghost_refs):
        for j in range(number == 0, ref.shape[1] // width):
            part = ref[:, j * width : (j + 1) * width]
            if shifted:
                row = lax.broadcasted_iota(jnp.int32, part.shape, 0)
                for a in range(3):
                    if (kind >> a) & 1:
                        move = jnp.where(octant_bit(part.shape, a, ghosts), -1.0, 1.0)
                        part = part + jnp.where(row == GROUP * a + vectors, move, 0.0)
            table[:, base : base + width] = part
            base += width
            kind += 1


def gather_slot(table, idx_ref, k, atoms):
    pieces = [[] for _ in range(3)]
    for j in range(atoms // LANES):
        index_row = idx_ref[:, pl.ds(pl.multiple_of(k * atoms + j * LANES, LANES), LANES)]
        for a in range(3):
            pieces[a].append(gather_lanes(table, index_row, a))
    return [jnp.concatenate(p, axis=1) for p in pieces]


def slot_tangents(diff, unit, inv, tn, tdiff, lanes, vectors):
    tau = sum(unit[a] * diff[a] for a in range(3))
    nus = [(diff[a] - unit[a] * tau) * inv for a in range(3)]
    shape = tau.shape
    for v in range(vectors):
        for m, value in enumerate([tau] + nus):
            start = (v * 4 + m) * GROUP
            tn[start : start + GROUP, lanes] = jnp.broadcast_to(value[v : v + 1, :], shape)
    for a in range(3):
        tdiff[rows(a), lanes] = diff[a]
    tdiff[rows(3), lanes] = tau


def channel_products(f, f1, q, rp, rpp, unit, env, tn, acc, half, atoms, fanout, vectors):
    share = 1.0 / fanout
    rpf = [rp[k] * f[k] for k in range(fanout)]
    for v in range(vectors):

        def get(m, k):
            start = (v * 4 + m) * GROUP
            return tn[start : start + GROUP, pl.ds(k * atoms + half, LANES)]

        phi = [f1[k] * get(0, k) for k in range(fanout)]
        de = [share * sum(phi)]
        for a in range(3):
            de.append(
                share * sum(phi[k] * unit(a, k) + f[k] * get(1 + a, k) for k in range(fanout))
            )
        y = []
        hde = []
        for k in range(fanout):
            turn = de[0] + sum(unit(a, k) * de[1 + a] for a in range(3))
            hde.append(turn)
            bend = turn + sum(get(1 + a, k) * env[1 + a] for a in range(3))
            y.append(rpp[k] * (phi[k] * q[k] + f[k] * bend))
        w = [y[k] * f[k] + rp[k] * phi[k] for k in range(fanout)]
        total = [share * sum(w)]
        for a in range(3):
            total.append(
                share * sum(w[k] * unit(a, k) + rpf[k] * get(1 + a, k) for k in range(fanout))
            )
        for k in range(fanout):
            along = total[0] + sum(unit(a, k) * total[1 + a] for a in range(3))
            terms = [f1[k] * (y[k] * q[k] + rp[k] * hde[k] + along)]
            for a in range(3):
                terms.append(f[k] * (y[k] * env[1 + a] + rp[k] * de[1 + a] + total[1 + a]))
            for m in range(4):
                start = (v * 4 + m) * GROUP
                acc[start : start + GROUP, pl.ds(k * atoms + half, LANES)] += terms[m]


def finish_product(
    idx_ref, unit_ref, inv_ref, bend_ref, acc, tdiff, scat, center, own_out, ghost_out, vectors, gram=None
):
    atoms = center.shape[1]
    fanout = idx_ref.shape[1] // atoms
    tiles = scat.shape[0] // (3 * GROUP)
    scat[...] = jnp.zeros_like(scat)
    center[...] = jnp.zeros_like(center)

    def slot(k, carry):
        lanes = pl.ds(pl.multiple_of(k * atoms, LANES), atoms)
        row = lax.broadcasted_iota(jnp.int32, (GROUP, atoms), 0)
        zero = jnp.zeros((GROUP, atoms), jnp.float32)
        outs = []
        for m in range(4):
            value = jnp.zeros((GROUP, atoms), jnp.float32)
            for v in range(vectors):
                start = (v * 4 + m) * GROUP
                part = jnp.sum(acc[start : start + GROUP, lanes], axis=0, keepdims=True)
                value = jnp.where(row == v, part, value)
            outs.append(value)
        unit = [unit_ref[rows(a), lanes] for a in range(3)]
        inv = inv_ref[:, lanes]
        diff = [tdiff[rows(a), lanes] for a in range(3)]
        tau = tdiff[rows(3), lanes]
        bend = bend_ref[:, lanes]
        stretch, turn = bend[0:1], bend[1:2]
        mix = [bend[2 + a : 3 + a] for a in range(3)]
        inner = sum(unit[a] * outs[1 + a] for a in range(3))
        along = (
            outs[0]
            - inner * inv
            + (stretch - turn) * tau
            + sum(mix[a] * diff[a] for a in range(3))
        )
        packed = []
        for a in range(3):
            y = along * unit[a] + outs[1 + a] * inv + turn * diff[a] + mix[a] * tau
            y = jnp.where(row < vectors, y, 0.0)
            center[rows(a), :] -= y
            if gram is not None:
                gram[...] += lax.dot_general(
                    jnp.where(row < vectors, diff[a], 0.0),
                    jnp.concatenate([y] + [zero] * (LANES // GROUP - 1), axis=0),
                    (((1,), (1,)), ((), ())),
                    precision=HIGHEST,
                    preferred_element_type=jnp.float32,
                )
            packed.append(split_rows(y, vectors))
        packed = jnp.concatenate(packed, axis=0)
        index_row = idx_ref[:, lanes]
        tile = index_row // LANES
        low = lax.broadcasted_iota(jnp.int32, (LANES, atoms), 0) == index_row % LANES
        left = jnp.concatenate(
            [jnp.where(tile == number, packed, 0.0) for number in range(tiles)], axis=0
        ).astype(jnp.bfloat16)
        right = jnp.where(low, 1.0, 0.0).astype(jnp.bfloat16)
        scat[...] += lax.dot_general(
            left, right, (((1,), (1,)), ((), ())), preferred_element_type=jnp.float32
        )
        return carry

    lax.fori_loop(0, fanout, slot, 0)
    own_tiles = atoms // LANES
    for number in range(tiles):
        for a in range(3):
            start = (number * 3 + a) * GROUP
            value = join_rows(scat[start : start + GROUP, :], vectors)
            if number < own_tiles:
                cut = slice(number * LANES, (number + 1) * LANES)
                own_out[rows(a), cut] = value + center[rows(a), cut]
            else:
                cut = number - own_tiles
                ghost_out[rows(a), cut * LANES : (cut + 1) * LANES] = value


def first_kernel(
    ghosts,
    vectors,
    idx_ref,
    own_ref,
    g1_ref,
    g2_ref,
    g3_ref,
    emb_ref,
    rin_ref,
    rout_ref,
    read_ref,
    own_out,
    ghost_out,
    unit_ref,
    inv_ref,
    bend_ref,
    f_ref,
    f1_ref,
    q_ref,
    rp_ref,
    rpp_ref,
    env_ref,
    table,
    f2_ref,
    read_col,
    tn,
    tdiff,
    acc,
    acc2,
    scat,
    center,
):
    atoms = own_ref.shape[1]
    fanout = idx_ref.shape[1] // atoms
    species, channels = emb_ref.shape
    basis = rin_ref.shape[0]
    embeds = [column(emb_ref[s : s + 1, :]) for s in range(species)]
    readout = column(read_ref[...])
    read_col[...] = jnp.broadcast_to(readout, read_col.shape)
    fill_table(table, own_ref, (g1_ref, g2_ref, g3_ref), vectors, ghosts, True)

    def embed(kind):
        value = embeds[0]
        for s in range(1, species):
            value = jnp.where(kind == float(s), embeds[s], value)
        return value

    own_embed = embed(own_ref[vectors + 1 : vectors + 2, :])

    def slot(k, carry):
        lanes = pl.ds(pl.multiple_of(k * atoms, LANES), atoms)
        near = gather_slot(table, idx_ref, k, atoms)
        diff = [near[a] - own_ref[rows(a), :] for a in range(3)]
        delta = [
            jnp.broadcast_to(diff[a][vectors : vectors + 1, :], (GROUP, atoms)) for a in range(3)
        ]
        dist = jnp.sqrt(delta[0] * delta[0] + delta[1] * delta[1] + delta[2] * delta[2] + SOFTEN)
        inv = 1.0 / dist
        unit = [delta[a] * inv for a in range(3)]
        for a in range(3):
            unit_ref[rows(a), lanes] = unit[a]
        inv_ref[:, lanes] = inv
        slot_tangents(diff, unit, inv, tn, tdiff, lanes, vectors)
        one = dist[0:1]
        inv_one = inv[0:1]
        order = (lax.broadcasted_iota(jnp.int32, (basis, atoms), 0) + 1).astype(jnp.float32)
        turns = order * (one * (1.0 / CUTOFF))
        whole = jnp.floor(turns + 0.5)
        rest = turns - whole
        odd = whole - 2.0 * jnp.floor(whole * 0.5)
        sign = 1.0 - 2.0 * odd
        x = rest * np.float32(np.pi)
        x2 = x * x
        sine = x * (
            1.0
            + x2
            * (
                -1.0 / 6
                + x2
                * (1.0 / 120 + x2 * (-1.0 / 5040 + x2 * (1.0 / 362880 + x2 * (-1.0 / 39916800))))
            )
        )
        cosine = 1.0 + x2 * (
            -0.5
            + x2
            * (
                1.0 / 24
                + x2
                * (
                    -1.0 / 720
                    + x2 * (1.0 / 40320 + x2 * (-1.0 / 3628800 + x2 * (1.0 / 479001600)))
                )
            )
        )
        sine = sine * sign
        cosine = cosine * sign
        omega = order * np.float32(np.pi / CUTOFF)
        b0 = sine * inv_one
        b1 = (omega * cosine - b0) * inv_one
        b2 = -(omega * omega * sine + 2.0 * b1) * inv_one
        z = lax.dot_general(
            rin_ref[...],
            jnp.concatenate([b0, b1, b2], axis=1),
            (((0,), (0,)), ((), ())),
            precision=HIGHEST,
            preferred_element_type=jnp.float32,
        )
        z0, z1, z2 = z[:, :atoms], z[:, atoms : 2 * atoms], z[:, 2 * atoms :]
        sig = 1.0 / (1.0 + jnp.exp(-z0))
        anti = 1.0 - sig
        slope = sig * (1.0 + z0 * anti)
        curve = sig * anti * (2.0 + z0 * (anti - sig))
        hidden = jnp.concatenate(
            [z0 * sig, slope * z1, curve * z1 * z1 + slope * z2], axis=1
        )
        radial = jnp.dot(
            rout_ref[...], hidden, precision=HIGHEST, preferred_element_type=jnp.float32
        )
        r0, r1, r2 = radial[:, :atoms], radial[:, atoms : 2 * atoms], radial[:, 2 * atoms :]
        square = one * one
        base = 1.0 - square * (1.0 / CUTOFF**2)
        v0 = base * base
        v1 = base * one * (-4.0 / CUTOFF**2)
        v2 = -4.0 / CUTOFF**2 + square * (12.0 / CUTOFF**4)
        pair = own_embed * embed(near[0][vectors + 1 : vectors + 2, :])
        f_ref[:, lanes] = pair * (r0 * v0)
        f1_ref[:, lanes] = pair * (r1 * v0 + r0 * v1)
        f2_ref[:, lanes] = pair * (r2 * v0 + 2.0 * (r1 * v1) + r0 * v2)
        return carry

    lax.fori_loop(0, fanout, slot, 0)
    acc[...] = jnp.zeros_like(acc)
    acc2[...] = jnp.zeros_like(acc2)
    halves = atoms // LANES
    share = 1.0 / fanout

    def tile(number, carry):
        start = pl.multiple_of((number // halves) * GROUP, GROUP)
        half = pl.multiple_of((number % halves) * LANES, LANES)
        here = pl.ds(start, GROUP)

        def cut(k):
            return pl.ds(pl.multiple_of(k * atoms + half, LANES), LANES)

        def unit(a, k):
            return unit_ref[rows(a), cut(k)]

        slots = range(fanout)
        f = [f_ref[here, cut(k)] for k in slots]
        f1 = [f1_ref[here, cut(k)] for k in slots]
        read = read_col[here, :]
        env = [share * sum(f)]
        for a in range(3):
            env.append(share * sum(f[k] * unit(a, k) for k in slots))
        q, rp, rpp = [], [], []
        for k in slots:
            project = env[0] + sum(unit(a, k) * env[1 + a] for a in range(3))
            x = f[k] * project
            sig = 1.0 / (1.0 + jnp.exp(-x))
            anti = 1.0 - sig
            q.append(project)
            rp.append(read * (sig * (1.0 + x * anti)))
            rpp.append(read * (sig * anti * (2.0 + x * (anti - sig))))
            q_ref[here, cut(k)] = q[k]
            rp_ref[here, cut(k)] = rp[k]
            rpp_ref[here, cut(k)] = rpp[k]
        for m in range(4):
            env_ref[pl.ds(m * channels + start, GROUP), pl.ds(half, LANES)] = env[m]
        rpf = [rp[k] * f[k] for k in slots]
        total = [share * sum(rpf)]
        for a in range(3):
            total.append(share * sum(rpf[k] * unit(a, k) for k in slots))
        for k in slots:
            g = [rp[k] * env[m] + total[m] for m in range(4)]
            gamma = g[0] + sum(unit(a, k) * g[1 + a] for a in range(3))
            terms = [f2_ref[here, cut(k)] * gamma, f1[k] * g[0]]
            terms += [f1[k] * g[1 + a] for a in range(3)]
            terms += [f[k] * g[1 + a] for a in range(3)]
            for m, term in enumerate(terms):
                acc2[m * GROUP : (m + 1) * GROUP, cut(k)] += term
        channel_products(
            f, f1, q, rp, rpp, unit, env, tn, acc, half, atoms, fanout, vectors
        )
        return carry

    lax.fori_loop(0, (channels // GROUP) * halves, tile, 0)

    def bend_slot(k, carry):
        lanes = pl.ds(pl.multiple_of(k * atoms, LANES), atoms)
        sums = [
            jnp.sum(acc2[m * GROUP : (m + 1) * GROUP, lanes], axis=0, keepdims=True)
            for m in range(8)
        ]
        inv = inv_ref[0:1, lanes]
        unit = [unit_ref[GROUP * a : GROUP * a + 1, lanes] for a in range(3)]
        up = sum(unit[a] * sums[2 + a] for a in range(3))
        uw = sum(unit[a] * sums[5 + a] for a in range(3))
        turn = (sums[1] + up - uw * inv) * inv
        mix = [
            ((sums[2 + a] - unit[a] * up) - (sums[5 + a] - unit[a] * uw) * inv) * inv
            for a in range(3)
        ]
        pad = jnp.zeros((GROUP - 5, atoms), jnp.float32)
        bend_ref[:, lanes] = jnp.concatenate([sums[0], turn] + mix + [pad], axis=0)
        return carry

    lax.fori_loop(0, fanout, bend_slot, 0)
    finish_product(
        idx_ref, unit_ref, inv_ref, bend_ref, acc, tdiff, scat, center, own_out, ghost_out, vectors
    )


def second_kernel(
    ghosts,
    vectors,
    idx_ref,
    own_ref,
    g1_ref,
    g2_ref,
    g3_ref,
    unit_ref,
    inv_ref,
    bend_ref,
    f_ref,
    f1_ref,
    q_ref,
    rp_ref,
    rpp_ref,
    env_ref,
    own_out,
    ghost_out,
    gram_out,
    table,
    tn,
    tdiff,
    acc,
    scat,
    center,
):
    atoms = own_ref.shape[1]
    fanout = idx_ref.shape[1] // atoms
    channels = f_ref.shape[0]
    fill_table(table, own_ref, (g1_ref, g2_ref, g3_ref), vectors, ghosts, False)

    def slot(k, carry):
        lanes = pl.ds(pl.multiple_of(k * atoms, LANES), atoms)
        near = gather_slot(table, idx_ref, k, atoms)
        diff = [near[a] - own_ref[rows(a), :] for a in range(3)]
        unit = [unit_ref[rows(a), lanes] for a in range(3)]
        slot_tangents(diff, unit, inv_ref[:, lanes], tn, tdiff, lanes, vectors)
        return carry

    lax.fori_loop(0, fanout, slot, 0)
    acc[...] = jnp.zeros_like(acc)
    gram_out[...] = jnp.zeros_like(gram_out)
    halves = atoms // LANES

    def tile(number, carry):
        start = pl.multiple_of((number // halves) * GROUP, GROUP)
        half = pl.multiple_of((number % halves) * LANES, LANES)
        here = pl.ds(start, GROUP)

        def cut(k):
            return pl.ds(pl.multiple_of(k * atoms + half, LANES), LANES)

        def unit(a, k):
            return unit_ref[rows(a), cut(k)]

        def load(ref):
            return [ref[here, cut(k)] for k in range(fanout)]

        env = [
            env_ref[pl.ds(m * channels + start, GROUP), pl.ds(half, LANES)] for m in range(4)
        ]
        channel_products(
            load(f_ref),
            load(f1_ref),
            load(q_ref),
            load(rp_ref),
            load(rpp_ref),
            unit,
            env,
            tn,
            acc,
            half,
            atoms,
            fanout,
            vectors,
        )
        return carry

    lax.fori_loop(0, (channels // GROUP) * halves, tile, 0)
    finish_product(
        idx_ref,
        unit_ref,
        inv_ref,
        bend_ref,
        acc,
        tdiff,
        scat,
        center,
        own_out,
        ghost_out,
        vectors,
        gram_out,
    )


def middle_kernel(vectors, own_ref, sums_ref, list_ref, full_ref, oct_ref):
    for a in range(3):
        full_ref[rows(a), :] = add_octants(
            own_ref[rows(a), :], sums_ref[rows(a), :], list_ref[...], vectors
        )
    pick_octants(full_ref, list_ref, oct_ref)


def inner(x, y, pad_to=LANES):
    pad = jnp.zeros((pad_to - y.shape[0], y.shape[1]), jnp.float32)
    return lax.dot_general(
        x,
        jnp.concatenate([y, pad], axis=0),
        (((1,), (1,)), ((), ())),
        precision=HIGHEST,
        preferred_element_type=jnp.float32,
    )


def only_vectors(x, vectors):
    row = lax.broadcasted_iota(jnp.int32, x.shape, 0)
    return jnp.where(row % GROUP < vectors, x, 0.0)


def gram_kernel(vectors, start_ref, first_ref, own_ref, sums_ref, list_ref, full_ref, gram_ref):
    total = jnp.zeros(gram_ref.shape, jnp.float32)
    for a in range(3):
        second = add_octants(own_ref[rows(a), :], sums_ref[rows(a), :], list_ref[...], vectors)
        full_ref[rows(a), :] = second
        stack = jnp.concatenate([start_ref[rows(a), :], first_ref[rows(a), :], second], axis=0)
        stack = only_vectors(stack, vectors)
        total += inner(stack, stack)
    gram_ref[...] = total


def packet_start(vectors, own_ref, sums_ref, ghost_ref, list_ref, part_ref, packet_ref):
    width = list_ref.shape[1]
    for a in range(3):
        part_ref[rows(a), :] = add_octants(
            own_ref[rows(a), :], sums_ref[rows(a), :], list_ref[...], vectors
        )
    mark = vectors + 1
    for j in range(width // LANES):
        cut = slice(j * LANES, (j + 1) * LANES)
        for a in range(3):
            value = gather_lanes(part_ref, list_ref[:, cut], a)
            if a == 0:
                row = lax.broadcasted_iota(jnp.int32, value.shape, 0)
                value = jnp.where(row == mark, list_ref[:, cut].astype(jnp.float32), value)
            packet_ref[rows(a), cut] = value
    packet_ref[:, width : 2 * width] = ghost_ref[...]


def arriving(side, packets, n, a, width):
    cut = slice(width, 2 * width)
    after, before = packets[(n + 1) % 4], packets[(n + 3) % 4]
    return jnp.where(side > 0.5, after[rows(a), cut], before[rows(a), cut])


def packet_lists(packet, vectors, width):
    mark = vectors + 1
    return packet[mark : mark + 1, :width].astype(jnp.int32)


def start_kernel(vectors, own_ref, sums_ref, ghost_ref, list_ref, part_ref, packet_ref):
    packet_start(vectors, own_ref, sums_ref, ghost_ref, list_ref, part_ref, packet_ref)


def merge_kernel(
    vectors, side_ref, part_ref, p0_ref, p1_ref, p2_ref, p3_ref, full_ref, level_ref, spread
):
    width = p0_ref.shape[1] // 2
    side = side_ref[...]
    packets = (p0_ref, p1_ref, p2_ref, p3_ref)
    lists = [packet_lists(p, vectors, width) for p in packets]
    for a in range(3):
        full_ref[rows(a), :] = add_octants(
            part_ref[rows(a), :], arriving(side, packets, 0, a, width), lists[0], vectors
        )
    near = []
    for n in (1, 3):
        for a in range(3):
            zero = jnp.zeros((GROUP, part_ref.shape[1]), jnp.float32)
            spread[rows(a), :] = add_octants(
                zero, arriving(side, packets, n, a, width), lists[n], vectors
            )
        values = []
        for a in range(3):
            pieces = [
                gather_lanes(spread, lists[n][:, j * LANES : (j + 1) * LANES], a)
                for j in range(width // LANES)
            ]
            values.append(packets[n][rows(a), :width] + jnp.concatenate(pieces, axis=1))
        near.append(values)
    for a in range(3):
        for j in range(width // LANES):
            cut = slice(j * LANES, (j + 1) * LANES)
            level_ref[rows(a), cut] = gather_lanes(full_ref, lists[0][:, cut], a)
        level_ref[rows(a), width : 2 * width] = jnp.where(side > 0.5, near[1][a], near[0][a])


def gram_start_kernel(
    vectors,
    start_ref,
    first_ref,
    own_ref,
    sums_ref,
    ghost_ref,
    list_ref,
    edge_ref,
    part_ref,
    packet_ref,
):
    packet_start(vectors, own_ref, sums_ref, ghost_ref, list_ref, part_ref, packet_ref)
    width = list_ref.shape[1]
    total = jnp.zeros((3 * GROUP, LANES), jnp.float32)
    for a in range(3):
        stack = jnp.concatenate(
            [start_ref[rows(a), :], first_ref[rows(a), :], part_ref[rows(a), :]], axis=0
        )
        stack = only_vectors(stack, vectors)
        total += inner(stack, stack)
    edge = pltpu.roll(edge_ref[...], 2 * GROUP, 1)
    lane = lax.broadcasted_iota(jnp.int32, edge.shape, 1)
    cut = slice(2 * width, 2 * width + LANES)
    packet_ref[rows(0), cut] = total[rows(0)]
    packet_ref[rows(1), cut] = jnp.where(lane // GROUP == 2, edge, total[rows(1)])
    packet_ref[rows(2), cut] = total[rows(2)]


def gram_merge_kernel(
    vectors, side_ref, part_ref, p0_ref, p1_ref, p2_ref, p3_ref, full_ref, gram_ref
):
    width = (p0_ref.shape[1] - LANES) // 2
    side = side_ref[...]
    packets = (p0_ref, p1_ref, p2_ref, p3_ref)
    shares = []
    for n in range(4):
        lists = packet_lists(packets[n], vectors, width)
        extra = jnp.zeros((GROUP, LANES), jnp.float32)
        for a in range(3):
            terms = only_vectors(arriving(side, packets, n, a, width), vectors)
            values = only_vectors(packets[n][rows(a), :width], vectors)
            zero = jnp.zeros((GROUP, part_ref.shape[1]), jnp.float32)
            spread = only_vectors(add_octants(zero, terms, lists, vectors), vectors)
            extra += inner(terms, values) + inner(values, terms) + inner(spread, spread)
            if n == 0:
                full_ref[rows(a), :] = part_ref[rows(a), :] + spread
        share = packets[n][:, 2 * width : 2 * width + LANES]
        shares.append((share, pltpu.roll(extra, 2 * GROUP, 1)))

    def add(x, y):
        return x[0] + y[0], x[1] + y[1]

    share, extra = add(add(shares[0], shares[1]), add(shares[2], shares[3]))
    gram_ref[0 : 2 * GROUP, :] = share[0 : 2 * GROUP]
    gram_ref[rows(2), :] = share[rows(2)] + extra


def last_kernel(
    vectors, scale, start_ref, first_ref, second_ref, gram_ref, next_ref, diag_ref, off_ref
):
    shape = (GROUP, LANES)
    row = lax.broadcasted_iota(jnp.int32, shape, 0)
    lane = lax.broadcasted_iota(jnp.int32, shape, 1)
    inside = (row < vectors) & (lane < vectors)
    eye = jnp.where((row == lane) & inside, 1.0, 0.0)

    def block(i, j):
        part = gram_ref[rows(i), :]
        if j:
            part = pltpu.roll(part, LANES - GROUP * j, 1)
        return jnp.where(inside, part * scale, 0.0)

    def mul(x, y):
        return sum(x[:, k : k + 1] * y[k : k + 1, :] for k in range(vectors))

    def flip(x):
        out = jnp.zeros(shape, jnp.float32)
        for k in range(vectors):
            line = jnp.sum(eye * x[:, k : k + 1], axis=0, keepdims=True)
            out = jnp.where(row == k, line, out)
        return out

    def factor(m):
        upper = jnp.zeros(shape, jnp.float32)
        inverse = eye
        for j in range(vectors):
            scale_j = 1.0 / jnp.sqrt(m[j : j + 1, j : j + 1])
            column = m[:, j : j + 1] * scale_j
            line = m[j : j + 1, :] * scale_j
            upper = jnp.where((row == j) & (lane >= j), line, upper)
            m = m - column * line
            own = inverse[j : j + 1, :] * scale_j
            inverse = jnp.where(
                row == j, own, jnp.where(row > j, inverse - column * own, inverse)
            )
        return upper, inverse

    ss, su, uu = block(0, 0), block(0, 1), block(1, 1)
    uq, qq = block(1, 2), block(2, 2)
    sq, qu = uu, uq
    _, p0 = factor(ss)
    p0t = flip(p0)
    a1 = mul(mul(p0, su), p0t)
    a1t = flip(a1)
    up1, p1 = factor(mul(mul(p0, uu), p0t) - mul(a1t, a1))
    b = mul(p1, p0)
    a = -mul(p1, mul(a1t, p0))
    at, bt = flip(a), flip(b)
    right_s = mul(su, at) + mul(sq, bt)
    right_u = mul(uu, at) + mul(uq, bt)
    right_q = mul(qu, at) + mul(qq, bt)
    a2 = mul(a, right_s) + mul(b, right_u)
    c2 = mul(p0, right_s)
    ww = mul(a, right_u) + mul(b, right_q)
    a2t, c2t = flip(a2), flip(c2)
    up2, p2 = factor(ww - mul(a2t, a2) - mul(c2t, c2))
    weights = (
        -mul(p2, mul(a2t, a) + mul(c2t, p0)),
        mul(p2, a - mul(a2t, b)),
        mul(p2, b),
    )
    small = (slice(0, vectors), slice(0, vectors))
    diag_ref[0] = a1[small]
    diag_ref[1] = a2[small]
    off_ref[0] = up1[small]
    off_ref[1] = up2[small]
    for comp in range(3):
        value = None
        for weight, ref in zip(weights, (start_ref, first_ref, second_ref)):
            for w in range(vectors):
                line = GROUP * comp + w
                term = weight[:, w : w + 1] * ref[line : line + 1, :]
                value = term if value is None else value + term
        next_ref[0, 0, 0, comp] = value[:vectors]


def call(body, outs, args, scratch=()):
    outs = [shape if isinstance(shape[0], tuple) else (shape, jnp.float32) for shape in outs]
    return pl.pallas_call(
        body,
        out_shape=[jax.ShapeDtypeStruct(shape, kind) for shape, kind in outs],
        in_specs=[pl.BlockSpec(memory_space=pltpu.VMEM)] * len(args),
        out_specs=[pl.BlockSpec(memory_space=pltpu.VMEM)] * len(outs),
        scratch_shapes=[pltpu.VMEM(shape, jnp.float32) for shape in scratch],
        compiler_params=pltpu.CompilerParams(vmem_limit_bytes=VMEM_BYTES),
    )(*args)


def table_index(neighbors, atoms, ghosts):
    entry = neighbors - atoms
    cell = entry // ghosts
    number = cell
    kept = [n for n in range(64) if not all(m in (1, 2) for m in (n // 16, n // 4 % 4, n % 4))]
    previous = -1
    for position, n in enumerate(kept):
        if n - previous > 1:
            number = number + jnp.where(cell >= position, n - previous - 1, 0)
        previous = n
    member = (number // 16, number // 4 % 4, number % 4)
    kind = 0
    octant = 0
    for bit, m in enumerate(member):
        kind = kind + jnp.where((m == 0) | (m == 3), 1 << bit, 0)
        octant = 2 * octant + (m + 1) % 2
    place = atoms + (kind - 1) * (8 * ghosts) + octant * ghosts + entry % ghosts
    return jnp.where(neighbors < atoms, neighbors, place)


def on_device(
    positions,
    species,
    start_block,
    neighbors,
    ghost_lists,
    embedding,
    radial_in,
    radial_out,
    readout,
):
    atoms = positions.shape[-1]
    ghosts = ghost_lists.shape[-1]
    vectors = start_block.shape[3]
    fanout = neighbors.shape[3]
    channels = embedding.shape[1]
    devices = lax.axis_size("gx") * lax.axis_size("gy") * lax.axis_size("gz")
    scale = 1.0 / (3.0 * atoms * devices)
    width = 8 * ghosts
    high = 3 * GROUP
    edges = fanout * atoms
    index = table_index(neighbors.reshape(1, -1), atoms, ghosts)
    table_width = atoms + 7 * width
    tiles = table_width // LANES
    ring = lax.axis_size("gx") == 4
    side = (octant_bit((GROUP, width), 0, ghosts) ^ (lax.axis_index("gx") % 2 == 1)).astype(
        jnp.float32
    )

    own, octants, lists = call(
        pack_kernel,
        [(high, atoms), (high, width), ((1, width), jnp.int32)],
        (positions, species, start_block.transpose(0, 1, 2, 4, 3, 5), ghost_lists),
    )

    def spread(level):
        if level.shape[1] == width:
            level = jnp.concatenate([level, fetch_ghosts(level, 0, ghosts)], axis=1)
        return (level,) + spread_outer(level, ghosts)

    shared = [
        (vectors * 4 * GROUP, edges),
        (4 * GROUP, edges),
        (vectors * 4 * GROUP, edges),
    ]
    tail = [(tiles * high, LANES), (high, atoms)]
    saved_shapes = [
        (high, edges),
        (GROUP, edges),
        (GROUP, edges),
        (channels, edges),
        (channels, edges),
        (channels, edges),
        (channels, edges),
        (channels, edges),
        (4 * channels, atoms),
    ]
    results = call(
        functools.partial(first_kernel, ghosts, vectors),
        [(high, atoms), (high, 7 * width)] + saved_shapes,
        (index, own)
        + spread(octants)
        + (embedding, radial_in, radial_out.T, readout.reshape(1, -1)),
        [(high, table_width), (channels, edges), (channels, LANES)]
        + shared
        + [(8 * GROUP, edges)]
        + tail,
    )
    own_terms, ghost_terms, saved = results[0], results[1], results[2:]

    sums, beside = return_outer(ghost_terms, width, ghosts)
    if ring:
        part, packet = call(
            functools.partial(start_kernel, vectors),
            [(high, atoms), (high, 2 * width)],
            (own_terms, sums, beside, lists),
        )
        others = pair_exchange(packet, "gx", (1, 2, 3))
        first, level = call(
            functools.partial(merge_kernel, vectors),
            [(high, atoms), (high, 2 * width)],
            (side, part, packet, *others),
            [(high, atoms)],
        )
    else:
        first, level = call(
            functools.partial(middle_kernel, vectors),
            [(high, atoms), (high, width)],
            (own_terms, sums + return_ghosts(beside, 0, ghosts), lists),
        )
    own_terms, ghost_terms, edge_gram = call(
        functools.partial(second_kernel, ghosts, vectors),
        [(high, atoms), (high, 7 * width), (GROUP, LANES)],
        (index, first) + spread(level) + tuple(saved),
        [(high, table_width)] + shared + tail,
    )
    sums, beside = return_outer(ghost_terms, width, ghosts)
    if ring:
        part, packet = call(
            functools.partial(gram_start_kernel, vectors),
            [(high, atoms), (high, 2 * width + LANES)],
            (own, first, own_terms, sums, beside, lists, edge_gram),
        )
        others = pair_exchange(packet, "gx", (1, 2, 3))
        second, gram = call(
            functools.partial(gram_merge_kernel, vectors),
            [(high, atoms), (high, LANES)],
            (side, part, packet, *others),
        )
        gram = sum_over(gram, AXES[1:])
    else:
        second, gram = call(
            functools.partial(gram_kernel, vectors),
            [(high, atoms), (high, LANES)],
            (own, first, own_terms, sums + return_ghosts(beside, 0, ghosts), lists),
        )
        gram = sum_over(gram, AXES)
    following, diagonal, off = call(
        functools.partial(last_kernel, vectors, scale),
        [(1, 1, 1, 3, vectors, atoms), (2, vectors, vectors), (2, vectors, vectors)],
        (own, first, second, gram),
    )
    return following.transpose(0, 1, 2, 4, 3, 5), diagonal, off


def solution(mesh):
    return jax.shard_map(
        on_device,
        mesh=mesh,
        in_specs=(
            P("gx", "gy", "gz", None, None),
            P("gx", "gy", "gz", None),
            P("gx", "gy", "gz", None, None, None),
            P("gx", "gy", "gz", None, None),
            P("gx", "gy", "gz", None),
            P(),
            P(),
            P(),
            P(),
        ),
        out_specs=(P("gx", "gy", "gz", None, None, None), P(), P()),
        check_vma=False,
    )
```

```python
import functools
import math

import jax
import jax.numpy as jnp
import numpy as np
from jax import lax
from jax.experimental import pallas as pl
from jax.experimental.pallas import tpu as pltpu
from jax.sharding import PartitionSpec as P

SOFTEN = 0.25
CUTOFF = 4.0
HIGHEST = lax.Precision.HIGHEST
LANES = 128
GROUP = 8
AXES = ("gx", "gy", "gz")
VMEM_BYTES = 48 * 1024 * 1024


def swap_pairs(size, distance):
    return [(i, (i + distance) % size) for i in range(size)]


def octant_bit(shape, bit, ghosts):
    lane = lax.broadcasted_iota(jnp.int32, shape, 1) % (8 * ghosts)
    return (lane // ghosts // (4 >> bit)) % 2 == 1


def pair_exchange(x, axis, distances):
    size = lax.axis_size(axis)
    return [lax.ppermute(x, axis, [(i, i ^ d) for i in range(size)]) for d in distances]


def ring_sides(x, bit):
    axis = AXES[bit]
    size = lax.axis_size(axis)
    if size == 4:
        near, far = pair_exchange(x, axis, (1, 3))
        return near, far, lax.axis_index(axis) % 2 == 1
    above = lax.ppermute(x, axis, swap_pairs(size, -1))
    below = lax.ppermute(x, axis, swap_pairs(size, 1))
    return above, below, False


def fetch_ghosts(x, bit, ghosts):
    axis = AXES[bit]
    size = lax.axis_size(axis)
    if size == 1:
        return x
    if size == 2:
        return lax.ppermute(x, axis, swap_pairs(2, 1))
    near, far, odd = ring_sides(x, bit)
    return jnp.where(octant_bit(x.shape, bit, ghosts) ^ odd, far, near)


def return_ghosts(x, bit, ghosts):
    axis = AXES[bit]
    size = lax.axis_size(axis)
    if size == 1:
        return x
    if size == 2:
        return lax.ppermute(x, axis, swap_pairs(2, 1))
    near, far, odd = ring_sides(x, bit)
    return jnp.where(octant_bit(x.shape, bit, ghosts) ^ odd, near, far)


def spread_outer(level, ghosts):
    second = fetch_ghosts(level, 1, ghosts)
    level = jnp.concatenate([level, second], axis=1)
    return second, fetch_ghosts(level, 2, ghosts)


def return_outer(terms, width, ghosts):
    got = return_ghosts(terms[:, 3 * width :], 2, ghosts)
    inner = got[:, :width]
    first = terms[:, :width] + got[:, width : 2 * width]
    second = terms[:, width : 3 * width] + got[:, 2 * width :]
    got = return_ghosts(second, 1, ghosts)
    return inner + got[:, :width], first + got[:, width:]


def sum_over(x, axes):
    for axis in axes:
        size = lax.axis_size(axis)
        if size & (size - 1):
            x = lax.psum(x, axis)
            continue
        step = 1
        while step < size:
            x = x + lax.ppermute(x, axis, [(i, i ^ step) for i in range(size)])
            step *= 2
    return x


def rows(a):
    return slice(GROUP * a, GROUP * (a + 1))


def gather_lanes(table, index_row, group):
    lane = jnp.broadcast_to(index_row % LANES, (GROUP, LANES))
    tile = jnp.broadcast_to(index_row // LANES, (GROUP, LANES))
    out = None
    for number in range(table.shape[1] // LANES):
        source = table[rows(group), number * LANES : (number + 1) * LANES]
        picked = jnp.take_along_axis(source, lane, axis=1, mode="promise_in_bounds")
        out = picked if out is None else jnp.where(tile == number, picked, out)
    return out


def column(line):
    size = line.shape[1]
    shape = (size, size)
    same = lax.broadcasted_iota(jnp.int32, shape, 0) == lax.broadcasted_iota(jnp.int32, shape, 1)
    return jnp.sum(jnp.where(same, line, 0.0), axis=1, keepdims=True)


def split_rows(y, vectors):
    high = y.astype(jnp.bfloat16).astype(jnp.float32)
    return high + pltpu.roll(y - high, vectors, 0)


def join_rows(y, vectors):
    return y + pltpu.roll(y, GROUP - vectors, 0)


def pack_kernel(pos_ref, spec_ref, block_ref, raw_ref, own_ref, oct_ref, list_ref):
    vectors = block_ref.shape[4]
    atoms = pos_ref.shape[-1]
    for a in range(3):
        parts = [block_ref[0, 0, 0, a], pos_ref[0, 0, 0, a : a + 1, :]]
        used = vectors + 1
        if a == 0:
            parts.append(spec_ref[0, 0].astype(jnp.float32))
            used += 1
        parts.append(jnp.zeros((GROUP - used, atoms), jnp.float32))
        own_ref[rows(a), :] = jnp.concatenate(parts, axis=0)
    pieces = [raw_ref[n // 4, n // 2 % 2, n % 2 : n % 2 + 1, :] for n in range(8)]
    list_ref[...] = jnp.concatenate(pieces, axis=1)
    pick_octants(own_ref, list_ref, oct_ref)


def pick_octants(own_ref, list_ref, oct_ref):
    for j in range(list_ref.shape[1] // LANES):
        cut = slice(j * LANES, (j + 1) * LANES)
        for a in range(3):
            oct_ref[rows(a), cut] = gather_lanes(own_ref, list_ref[:, cut], a)


def add_octants(own, octants, lists, vectors):
    atoms = own.shape[1]
    width = lists.shape[1]
    keep = lax.broadcasted_iota(jnp.int32, octants.shape, 0) < vectors
    packed = split_rows(jnp.where(keep, octants, 0.0), vectors).astype(jnp.bfloat16)
    onehot = lax.broadcasted_iota(jnp.int32, (atoms, width), 0) == lists
    spread = lax.dot_general(
        packed,
        jnp.where(onehot, 1.0, 0.0).astype(jnp.bfloat16),
        (((1,), (1,)), ((), ())),
        preferred_element_type=jnp.float32,
    )
    return own + join_rows(spread, vectors)


def fill_table(table, own_ref, ghost_refs, vectors, ghosts, shifted):
    atoms = own_ref.shape[1]
    table[:, :atoms] = own_ref[...]
    width = 8 * ghosts
    base = atoms
    kind = 1
    for number, ref in enumerate(ghost_refs):
        for j in range(number == 0, ref.shape[1] // width):
            part = ref[:, j * width : (j + 1) * width]
            if shifted:
                row = lax.broadcasted_iota(jnp.int32, part.shape, 0)
                for a in range(3):
                    if (kind >> a) & 1:
                        move = jnp.where(octant_bit(part.shape, a, ghosts), -1.0, 1.0)
                        part = part + jnp.where(row == GROUP * a + vectors, move, 0.0)
            table[:, base : base + width] = part
            base += width
            kind += 1


def gather_slot(table, idx_ref, k, atoms):
    pieces = [[] for _ in range(3)]
    for j in range(atoms // LANES):
        index_row = idx_ref[:, pl.ds(pl.multiple_of(k * atoms + j * LANES, LANES), LANES)]
        for a in range(3):
            pieces[a].append(gather_lanes(table, index_row, a))
    return [jnp.concatenate(p, axis=1) for p in pieces]


def pair_list(fanout):
    return [(k, l) for k in range(fanout) for l in range(k, fanout)]


def lookup(table, fanout):
    where = {pair: n for n, pair in enumerate(pair_list(fanout))}
    return lambda k, l: table[where[min(k, l), max(k, l)]]


def sum_rows(parts):
    row = lax.broadcasted_iota(jnp.int32, parts[0].shape, 0)
    if len(parts) != 4 or GROUP != 8:
        out = jnp.zeros_like(parts[0])
        for n, part in enumerate(parts):
            out = jnp.where(row == n, jnp.sum(part, axis=0, keepdims=True), out)
        return out
    fold = [part + pltpu.roll(part, 4, 0) for part in parts]
    low = row < 4
    lead = jnp.where(low, fold[0], fold[1])
    rest = jnp.where(low, fold[2], fold[3])
    both = jnp.where(row % 4 < 2, lead + pltpu.roll(lead, 6, 0), rest + pltpu.roll(rest, 2, 0))
    even = both + pltpu.roll(both, 7, 0)
    odd = both + pltpu.roll(both, 1, 0)
    return jnp.where(row % 2 == 1, pltpu.roll(odd, 4, 0), even)


def dot3(x, y):
    return x[0] * y[0] + x[1] * y[1] + x[2] * y[2]


def slot_cut(k, atoms):
    return slice(k * atoms, (k + 1) * atoms)


def tile_rows(n):
    return slice(GROUP * n, GROUP * (n + 1))


def tangents(diffs, units, invs, tn, changes, vectors):
    fanout = len(diffs)
    pairs = pair_list(fanout)
    per_vector = fanout + len(pairs)
    taus = [dot3(units[k], diffs[k]) for k in range(fanout)]
    turns = [
        [(diffs[k][a] - units[k][a] * taus[k]) * invs[k] for a in range(3)] for k in range(fanout)
    ]
    values = list(taus)
    for k, l in pairs:
        half = dot3(units[k], turns[l])
        values.append(2.0 * half if k == l else half + dot3(units[l], turns[k]))
    for n, value in enumerate(values):
        changes[tile_rows(n), :] = value
        for v in range(vectors):
            tn[tile_rows(v * per_vector + n), :] = jnp.broadcast_to(
                value[v : v + 1, :], value.shape
            )


def channel_products(f, f1, q, rp, rpp, cosine, tn, acc, lanes, fanout, vectors):
    pairs = pair_list(fanout)
    per_vector = fanout + len(pairs)
    slots = range(fanout)
    rpp_q = [rpp[k] * q[k] for k in slots]
    rpp_f = [rpp[k] * f[k] for k in slots]
    for v in range(vectors):
        base = v * per_vector

        def tangent(n):
            return tn[tile_rows(base + n), lanes]

        phi = [f1[k] * tangent(k) for k in slots]
        index = {pair: fanout + n for n, pair in enumerate(pairs)}
        dq = []
        for k in slots:
            total = None
            for l in slots:
                term = phi[l] * cosine(k, l) + f[l] * tangent(index[min(k, l), max(k, l)])
                total = term if total is None else total + term
            dq.append(total)
        y = [phi[k] * rpp_q[k] + dq[k] * rpp_f[k] for k in slots]
        w = [y[k] * f[k] + rp[k] * phi[k] for k in slots]
        for k in slots:
            total = y[k] * q[k] + rp[k] * dq[k]
            for l in slots:
                total = total + w[l] * cosine(k, l)
            acc[tile_rows(base + k), lanes] += f1[k] * total
        for n, (k, l) in enumerate(pairs):
            term = w[k] * f[l] if k == l else w[k] * f[l] + w[l] * f[k]
            acc[tile_rows(base + fanout + n), lanes] += term


def finish_product(
    idx_ref, low_ref, unit_ref, inv_ref, sums_ref, acc, changes, diffs, own_out, ghost_out, vectors
):
    atoms = own_out.shape[1]
    fanout = idx_ref.shape[1] // atoms
    tiles = (atoms + ghost_out.shape[1]) // LANES
    pairs = pair_list(fanout)
    per_vector = fanout + len(pairs)
    slots = range(fanout)
    row = lax.broadcasted_iota(jnp.int32, (GROUP, atoms), 0)
    outs = [
        sum_rows([acc[tile_rows(v * per_vector + n), :] for v in range(vectors)])
        for n in range(per_vector)
    ]
    taus = [changes[tile_rows(k), :] for k in slots]
    turned = lookup([changes[tile_rows(fanout + n), :] for n in range(len(pairs))], fanout)
    bent = lookup(outs[fanout:], fanout)
    units = [[unit_ref[rows(a), slot_cut(k, atoms)] for a in range(3)] for k in slots]
    invs = [inv_ref[:, slot_cut(k, atoms)] for k in slots]
    turns = [
        [(diffs[k][a] - units[k][a] * taus[k]) * invs[k] for a in range(3)] for k in slots
    ]

    def base_sum(n):
        line = (n // 4) * GROUP + n % 4
        return sums_ref[line : line + 1, :]

    stretch = [base_sum(k) for k in slots]
    curve = [base_sum(fanout + k) for k in slots]
    weight = lookup([base_sum(2 * fanout + n) for n in range(len(pairs))], fanout)
    mixed = [[base_sum(2 * fanout + len(pairs) + k * fanout + l) for l in slots] for k in slots]
    center = [jnp.zeros((GROUP, atoms), jnp.float32) for _ in range(3)]
    shifted = [jnp.zeros((GROUP, atoms), jnp.float32) for _ in range(vectors)]
    left = []
    for k in slots:
        along = outs[k] + curve[k] * taus[k]
        force = [0.0, 0.0, 0.0]
        change = [0.0, 0.0, 0.0]
        for l in slots:
            along = along + turned(k, l) * mixed[k][l]
            bend = bent(k, l) + taus[l] * mixed[l][k] + taus[k] * mixed[k][l]
            pull = weight(k, l)
            if k == l:
                bend = bend + bent(k, l)
                pull = pull + pull
            for a in range(3):
                force[a] = force[a] + pull * units[l][a]
                change[a] = change[a] + bend * units[l][a] + pull * turns[l][a]
        flat = dot3(units[k], force)
        inv = invs[k]
        along = (
            along
            - (dot3(units[k], change) + dot3(turns[k], force)) * inv
            + taus[k] * flat * (inv * inv)
        )
        keep = stretch[k] - flat * inv
        packed = []
        for a in range(3):
            y = (
                along * units[k][a]
                + keep * turns[k][a]
                + (change[a] - taus[k] * inv * force[a]) * inv
            )
            y = jnp.where(row < vectors, y, 0.0)
            center[a] = center[a] - y
            for n in range(vectors):
                other = y if n == 0 else pltpu.roll(y, n, 0)
                if n:
                    other = other + pltpu.roll(y, GROUP - vectors + n, 0)
                shifted[n] = shifted[n] + other * diffs[k][a]
            packed.append(split_rows(y, vectors))
        packed = jnp.concatenate(packed, axis=0)
        tile = idx_ref[:, slot_cut(k, atoms)] // LANES
        left.append(
            jnp.concatenate(
                [jnp.where(tile == number, packed, 0.0) for number in range(tiles)], axis=0
            ).astype(jnp.bfloat16)
        )
    spread = lax.dot_general(
        jnp.concatenate(left, axis=1),
        low_ref[...],
        (((1,), (1,)), ((), ())),
        preferred_element_type=jnp.float32,
    )
    own_tiles = atoms // LANES
    for number in range(tiles):
        for a in range(3):
            value = join_rows(spread[tile_rows(number * 3 + a)], vectors)
            if number < own_tiles:
                cut = slice(number * LANES, (number + 1) * LANES)
                own_out[rows(a), cut] = value + center[a][:, cut]
            else:
                cut = number - own_tiles
                ghost_out[rows(a), cut * LANES : (cut + 1) * LANES] = value
    return shifted


def split_parts(x):
    high = x.astype(jnp.bfloat16).astype(jnp.float32)
    rest = x - high
    middle = rest.astype(jnp.bfloat16).astype(jnp.float32)
    low = (rest - middle).astype(jnp.bfloat16).astype(jnp.float32)
    return high, middle, low


def silu_slopes(x):
    sig = 0.5 + 0.5 * jnp.tanh(0.5 * x)
    anti = 1.0 - sig
    return sig, sig * (1.0 + x * anti), sig * anti * (2.0 + x * (anti - sig))


def half_turns(dist, inv, basis):
    shape = (basis, dist.shape[1])
    order = (lax.broadcasted_iota(jnp.int32, shape, 0) + 1).astype(jnp.float32)
    turns = order * (dist * (1.0 / CUTOFF))
    whole = jnp.floor(turns + 0.5)
    sign = 1.0 - 2.0 * (whole - 2.0 * jnp.floor(whole * 0.5))
    x = (turns - whole) * np.float32(np.pi)
    x2 = x * x

    def series(terms):
        value = terms[-1]
        for term in terms[-2::-1]:
            value = term + x2 * value
        return value

    sine = sign * x * series([(-1.0) ** n / math.factorial(2 * n + 1) for n in range(6)])
    cosine = sign * series([(-1.0) ** n / math.factorial(2 * n) for n in range(7)])
    omega = order * np.float32(np.pi / CUTOFF)
    b0 = sine * inv
    b1 = (omega * cosine - b0) * inv
    b2 = -(omega * omega * sine + 2.0 * b1) * inv
    return jnp.concatenate([b0, b1, b2], axis=1)


def first_kernel(
    ghosts,
    vectors,
    idx_ref,
    own_ref,
    g1_ref,
    g2_ref,
    g3_ref,
    emb_ref,
    rin_ref,
    rout_ref,
    read_ref,
    own_out,
    ghost_out,
    low_out,
    unit_ref,
    inv_ref,
    sums_ref,
    cos_ref,
    f_ref,
    f1_ref,
    q_ref,
    rp_ref,
    rpp_ref,
    table,
    f2_ref,
    read_col,
    tn,
    changes,
    acc,
    acc2,
):
    atoms = own_ref.shape[1]
    fanout = idx_ref.shape[1] // atoms
    species, channels = emb_ref.shape
    basis, hidden_units = rin_ref.shape
    pairs = pair_list(fanout)
    slots = range(fanout)
    embeds = [column(emb_ref[s : s + 1, :]) for s in range(species)]
    read_col[...] = jnp.broadcast_to(column(read_ref[...]), read_col.shape)
    fill_table(table, own_ref, (g1_ref, g2_ref, g3_ref), vectors, ghosts, True)

    def embed(kind):
        value = embeds[0]
        for s in range(1, species):
            value = jnp.where(kind == float(s), embeds[s], value)
        return value

    own_embed = embed(own_ref[vectors + 1 : vectors + 2, :])
    low = lax.broadcasted_iota(jnp.int32, (LANES, idx_ref.shape[1]), 0) == idx_ref[...] % LANES
    low_out[...] = jnp.where(low, 1.0, 0.0).astype(jnp.bfloat16)

    high, middle, rest = split_parts(rin_ref[...])
    stack = [high, middle, rest, high, middle, high]
    pad = LANES * (-(-(6 * basis) // LANES)) - 6 * basis
    stack = jnp.concatenate(stack + [jnp.zeros((pad, hidden_units), jnp.float32)], axis=0)
    inward = jnp.transpose(stack)[:, : 6 * basis].astype(jnp.bfloat16)
    high, rest, _ = split_parts(rout_ref[...])
    outward = jnp.concatenate(
        [jnp.concatenate([high, high], axis=1), jnp.concatenate([rest, rest], axis=1)], axis=0
    ).astype(jnp.bfloat16)

    diffs, units, invs = [], [], []
    for k in slots:
        cut = slot_cut(k, atoms)
        near = gather_slot(table, idx_ref, k, atoms)
        diff = [near[a] - own_ref[rows(a), :] for a in range(3)]
        delta = [
            jnp.broadcast_to(diff[a][vectors : vectors + 1, :], (GROUP, atoms)) for a in range(3)
        ]
        dist = jnp.sqrt(dot3(delta, delta) + SOFTEN)
        inv = 1.0 / dist
        unit = [delta[a] * inv for a in range(3)]
        for a in range(3):
            unit_ref[rows(a), cut] = unit[a]
        inv_ref[:, cut] = inv
        diffs.append(diff)
        units.append(unit)
        invs.append(inv)
        one = dist[0:1]
        radii = half_turns(one, inv[0:1], basis)
        high, middle, rest = split_parts(radii)
        z = jnp.dot(
            inward,
            jnp.concatenate([high, high, high, middle, middle, rest], axis=0).astype(jnp.bfloat16),
            preferred_element_type=jnp.float32,
        )
        z0, z1, z2 = z[:, :atoms], z[:, atoms : 2 * atoms], z[:, 2 * atoms :]
        sig, slope, curve = silu_slopes(z0)
        hidden = jnp.concatenate([z0 * sig, slope * z1, curve * z1 * z1 + slope * z2], axis=1)
        high = hidden.astype(jnp.bfloat16)
        rest = (hidden - high.astype(jnp.float32)).astype(jnp.bfloat16)
        radial = jnp.dot(
            outward, jnp.concatenate([high, rest], axis=0), preferred_element_type=jnp.float32
        )
        radial = radial[:channels] + radial[channels:]
        r0, r1, r2 = radial[:, :atoms], radial[:, atoms : 2 * atoms], radial[:, 2 * atoms :]
        square = one * one
        base = 1.0 - square * (1.0 / CUTOFF**2)
        v0 = base * base
        v1 = base * one * (-4.0 / CUTOFF**2)
        v2 = -4.0 / CUTOFF**2 + square * (12.0 / CUTOFF**4)
        pair = own_embed * embed(near[0][vectors + 1 : vectors + 2, :])
        f_ref[:, cut] = pair * (r0 * v0)
        f1_ref[:, cut] = pair * (r1 * v0 + r0 * v1)
        f2_ref[:, cut] = pair * (r2 * v0 + 2.0 * (r1 * v1) + r0 * v2)
    for n, (k, l) in enumerate(pairs):
        cos_ref[tile_rows(n), :] = 1.0 + dot3(units[k], units[l])
    tangents(diffs, units, invs, tn, changes, vectors)
    acc[...] = jnp.zeros_like(acc)
    acc2[...] = jnp.zeros_like(acc2)
    share = 1.0 / fanout

    def tile(number, carry):
        here = pl.ds(pl.multiple_of(number * GROUP, GROUP), GROUP)
        for half in range(atoms // LANES):
            lanes = slice(half * LANES, (half + 1) * LANES)
            cuts = [slice(k * atoms + half * LANES, k * atoms + (half + 1) * LANES) for k in slots]
            cosine = lookup([cos_ref[tile_rows(n), lanes] for n in range(len(pairs))], fanout)
            f = [f_ref[here, cut] for cut in cuts]
            f1 = [f1_ref[here, cut] for cut in cuts]
            read = read_col[here, :] * share
            q, rp, rpp = [], [], []
            for k in slots:
                project = sum(f[l] * cosine(k, l) for l in slots)
                _, slope, curve = silu_slopes(f[k] * project * share)
                q.append(project)
                rp.append(read * slope)
                rpp.append(read * share * curve)
                q_ref[here, cuts[k]] = q[k]
                rp_ref[here, cuts[k]] = rp[k]
                rpp_ref[here, cuts[k]] = rpp[k]
            m = [rp[k] * f[k] for k in slots]
            slope = [rp[k] * q[k] + sum(m[l] * cosine(k, l) for l in slots) for k in slots]
            terms = [slope[k] * f1[k] for k in slots]
            terms += [slope[k] * f2_ref[here, cuts[k]] for k in slots]
            terms += [m[k] * f[l] if k == l else m[k] * f[l] + m[l] * f[k] for k, l in pairs]
            terms += [f1[k] * m[l] for k in slots for l in slots]
            for n, term in enumerate(terms):
                acc2[tile_rows(n), lanes] += term
            channel_products(f, f1, q, rp, rpp, cosine, tn, acc, lanes, fanout, vectors)
        return carry

    lax.fori_loop(0, channels // GROUP, tile, 0)
    count = acc2.shape[0] // GROUP
    for n in range(0, count, 4):
        parts = [acc2[tile_rows(min(n + j, count - 1)), :] for j in range(4)]
        sums_ref[tile_rows(n // 4), :] = sum_rows(parts)
    finish_product(
        idx_ref,
        low_out,
        unit_ref,
        inv_ref,
        sums_ref,
        acc,
        changes,
        diffs,
        own_out,
        ghost_out,
        vectors,
    )


def second_kernel(
    ghosts,
    vectors,
    idx_ref,
    own_ref,
    g1_ref,
    g2_ref,
    g3_ref,
    low_ref,
    unit_ref,
    inv_ref,
    sums_ref,
    cos_ref,
    f_ref,
    f1_ref,
    q_ref,
    rp_ref,
    rpp_ref,
    own_out,
    ghost_out,
    gram_out,
    table,
    tn,
    changes,
    acc,
):
    atoms = own_ref.shape[1]
    fanout = idx_ref.shape[1] // atoms
    channels = f_ref.shape[0]
    pairs = pair_list(fanout)
    slots = range(fanout)
    fill_table(table, own_ref, (g1_ref, g2_ref, g3_ref), vectors, ghosts, False)
    diffs = []
    for k in slots:
        near = gather_slot(table, idx_ref, k, atoms)
        diffs.append([near[a] - own_ref[rows(a), :] for a in range(3)])
    units = [[unit_ref[rows(a), slot_cut(k, atoms)] for a in range(3)] for k in slots]
    invs = [inv_ref[:, slot_cut(k, atoms)] for k in slots]
    tangents(diffs, units, invs, tn, changes, vectors)
    acc[...] = jnp.zeros_like(acc)

    def tile(number, carry):
        here = pl.ds(pl.multiple_of(number * GROUP, GROUP), GROUP)
        for half in range(atoms // LANES):
            lanes = slice(half * LANES, (half + 1) * LANES)
            cuts = [slice(k * atoms + half * LANES, k * atoms + (half + 1) * LANES) for k in slots]
            cosine = lookup([cos_ref[tile_rows(n), lanes] for n in range(len(pairs))], fanout)
            parts = [
                [ref[here, cut] for cut in cuts] for ref in (f_ref, f1_ref, q_ref, rp_ref, rpp_ref)
            ]
            channel_products(*parts, cosine, tn, acc, lanes, fanout, vectors)
        return carry

    lax.fori_loop(0, channels // GROUP, tile, 0)
    shifted = finish_product(
        idx_ref,
        low_ref,
        unit_ref,
        inv_ref,
        sums_ref,
        acc,
        changes,
        diffs,
        own_out,
        ghost_out,
        vectors,
    )
    row = lax.broadcasted_iota(jnp.int32, gram_out.shape, 0)
    lane = lax.broadcasted_iota(jnp.int32, gram_out.shape, 1)
    total = jnp.zeros(gram_out.shape, jnp.float32)
    for n in range(vectors):
        value = jnp.sum(shifted[n], axis=1, keepdims=True)
        total = jnp.where(lane == (row + vectors - n) % vectors, value, total)
    gram_out[...] = jnp.where((row < vectors) & (lane < vectors), total, 0.0)


def middle_kernel(vectors, own_ref, sums_ref, list_ref, full_ref, oct_ref):
    for a in range(3):
        full_ref[rows(a), :] = add_octants(
            own_ref[rows(a), :], sums_ref[rows(a), :], list_ref[...], vectors
        )
    pick_octants(full_ref, list_ref, oct_ref)


def inner(x, y, pad_to=LANES):
    pad = jnp.zeros((pad_to - y.shape[0], y.shape[1]), jnp.float32)
    return lax.dot_general(
        x,
        jnp.concatenate([y, pad], axis=0),
        (((1,), (1,)), ((), ())),
        precision=HIGHEST,
        preferred_element_type=jnp.float32,
    )


def only_vectors(x, vectors):
    row = lax.broadcasted_iota(jnp.int32, x.shape, 0)
    return jnp.where(row % GROUP < vectors, x, 0.0)


def gram_kernel(vectors, start_ref, first_ref, own_ref, sums_ref, list_ref, full_ref, gram_ref):
    total = jnp.zeros(gram_ref.shape, jnp.float32)
    for a in range(3):
        second = add_octants(own_ref[rows(a), :], sums_ref[rows(a), :], list_ref[...], vectors)
        full_ref[rows(a), :] = second
        stack = jnp.concatenate([start_ref[rows(a), :], first_ref[rows(a), :], second], axis=0)
        stack = only_vectors(stack, vectors)
        total += inner(stack, stack)
    gram_ref[...] = total


def packet_start(vectors, own_ref, sums_ref, ghost_ref, list_ref, part_ref, packet_ref):
    width = list_ref.shape[1]
    for a in range(3):
        part_ref[rows(a), :] = add_octants(
            own_ref[rows(a), :], sums_ref[rows(a), :], list_ref[...], vectors
        )
    mark = vectors + 1
    for j in range(width // LANES):
        cut = slice(j * LANES, (j + 1) * LANES)
        for a in range(3):
            value = gather_lanes(part_ref, list_ref[:, cut], a)
            if a == 0:
                row = lax.broadcasted_iota(jnp.int32, value.shape, 0)
                value = jnp.where(row == mark, list_ref[:, cut].astype(jnp.float32), value)
            packet_ref[rows(a), cut] = value
    packet_ref[:, width : 2 * width] = ghost_ref[...]


def arriving(side, packets, n, a, width):
    cut = slice(width, 2 * width)
    after, before = packets[(n + 1) % 4], packets[(n + 3) % 4]
    return jnp.where(side > 0.5, after[rows(a), cut], before[rows(a), cut])


def packet_lists(packet, vectors, width):
    mark = vectors + 1
    return packet[mark : mark + 1, :width].astype(jnp.int32)


def start_kernel(vectors, own_ref, sums_ref, ghost_ref, list_ref, part_ref, packet_ref):
    packet_start(vectors, own_ref, sums_ref, ghost_ref, list_ref, part_ref, packet_ref)


def merge_kernel(
    vectors, side_ref, part_ref, p0_ref, p1_ref, p2_ref, p3_ref, full_ref, level_ref, spread
):
    width = p0_ref.shape[1] // 2
    side = side_ref[...]
    packets = (p0_ref, p1_ref, p2_ref, p3_ref)
    lists = [packet_lists(p, vectors, width) for p in packets]
    for a in range(3):
        full_ref[rows(a), :] = add_octants(
            part_ref[rows(a), :], arriving(side, packets, 0, a, width), lists[0], vectors
        )
    near = []
    for n in (1, 3):
        for a in range(3):
            zero = jnp.zeros((GROUP, part_ref.shape[1]), jnp.float32)
            spread[rows(a), :] = add_octants(
                zero, arriving(side, packets, n, a, width), lists[n], vectors
            )
        values = []
        for a in range(3):
            pieces = [
                gather_lanes(spread, lists[n][:, j * LANES : (j + 1) * LANES], a)
                for j in range(width // LANES)
            ]
            values.append(packets[n][rows(a), :width] + jnp.concatenate(pieces, axis=1))
        near.append(values)
    for a in range(3):
        for j in range(width // LANES):
            cut = slice(j * LANES, (j + 1) * LANES)
            level_ref[rows(a), cut] = gather_lanes(full_ref, lists[0][:, cut], a)
        level_ref[rows(a), width : 2 * width] = jnp.where(side > 0.5, near[1][a], near[0][a])


def gram_start_kernel(
    vectors,
    start_ref,
    first_ref,
    own_ref,
    sums_ref,
    ghost_ref,
    list_ref,
    edge_ref,
    part_ref,
    packet_ref,
):
    packet_start(vectors, own_ref, sums_ref, ghost_ref, list_ref, part_ref, packet_ref)
    width = list_ref.shape[1]
    total = jnp.zeros((3 * GROUP, LANES), jnp.float32)
    for a in range(3):
        stack = jnp.concatenate(
            [start_ref[rows(a), :], first_ref[rows(a), :], part_ref[rows(a), :]], axis=0
        )
        stack = only_vectors(stack, vectors)
        total += inner(stack, stack)
    edge = pltpu.roll(edge_ref[...], 2 * GROUP, 1)
    lane = lax.broadcasted_iota(jnp.int32, edge.shape, 1)
    cut = slice(2 * width, 2 * width + LANES)
    packet_ref[rows(0), cut] = total[rows(0)]
    packet_ref[rows(1), cut] = jnp.where(lane // GROUP == 2, edge, total[rows(1)])
    packet_ref[rows(2), cut] = total[rows(2)]


def gram_merge_kernel(
    vectors, side_ref, part_ref, p0_ref, p1_ref, p2_ref, p3_ref, full_ref, gram_ref
):
    width = (p0_ref.shape[1] - LANES) // 2
    side = side_ref[...]
    packets = (p0_ref, p1_ref, p2_ref, p3_ref)
    shares = []
    for n in range(4):
        lists = packet_lists(packets[n], vectors, width)
        extra = jnp.zeros((GROUP, LANES), jnp.float32)
        for a in range(3):
            terms = only_vectors(arriving(side, packets, n, a, width), vectors)
            values = only_vectors(packets[n][rows(a), :width], vectors)
            zero = jnp.zeros((GROUP, part_ref.shape[1]), jnp.float32)
            spread = only_vectors(add_octants(zero, terms, lists, vectors), vectors)
            extra += inner(terms, values) + inner(values, terms) + inner(spread, spread)
            if n == 0:
                full_ref[rows(a), :] = part_ref[rows(a), :] + spread
        share = packets[n][:, 2 * width : 2 * width + LANES]
        shares.append((share, pltpu.roll(extra, 2 * GROUP, 1)))

    def add(x, y):
        return x[0] + y[0], x[1] + y[1]

    share, extra = add(add(shares[0], shares[1]), add(shares[2], shares[3]))
    gram_ref[0 : 2 * GROUP, :] = share[0 : 2 * GROUP]
    gram_ref[rows(2), :] = share[rows(2)] + extra


def last_kernel(
    vectors, scale, start_ref, first_ref, second_ref, gram_ref, next_ref, diag_ref, off_ref
):
    shape = (GROUP, LANES)
    row = lax.broadcasted_iota(jnp.int32, shape, 0)
    lane = lax.broadcasted_iota(jnp.int32, shape, 1)
    inside = (row < vectors) & (lane < vectors)
    eye = jnp.where((row == lane) & inside, 1.0, 0.0)

    def block(i, j):
        part = gram_ref[rows(i), :]
        if j:
            part = pltpu.roll(part, LANES - GROUP * j, 1)
        return jnp.where(inside, part * scale, 0.0)

    def mul(x, y):
        return sum(x[:, k : k + 1] * y[k : k + 1, :] for k in range(vectors))

    def flip(x):
        out = jnp.zeros(shape, jnp.float32)
        for k in range(vectors):
            line = jnp.sum(eye * x[:, k : k + 1], axis=0, keepdims=True)
            out = jnp.where(row == k, line, out)
        return out

    def factor(m):
        upper = jnp.zeros(shape, jnp.float32)
        inverse = eye
        for j in range(vectors):
            scale_j = 1.0 / jnp.sqrt(m[j : j + 1, j : j + 1])
            column = m[:, j : j + 1] * scale_j
            line = m[j : j + 1, :] * scale_j
            upper = jnp.where((row == j) & (lane >= j), line, upper)
            m = m - column * line
            own = inverse[j : j + 1, :] * scale_j
            inverse = jnp.where(
                row == j, own, jnp.where(row > j, inverse - column * own, inverse)
            )
        return upper, inverse

    ss, su, uu = block(0, 0), block(0, 1), block(1, 1)
    uq, qq = block(1, 2), block(2, 2)
    sq, qu = uu, uq
    _, p0 = factor(ss)
    p0t = flip(p0)
    a1 = mul(mul(p0, su), p0t)
    a1t = flip(a1)
    up1, p1 = factor(mul(mul(p0, uu), p0t) - mul(a1t, a1))
    b = mul(p1, p0)
    a = -mul(p1, mul(a1t, p0))
    at, bt = flip(a), flip(b)
    right_s = mul(su, at) + mul(sq, bt)
    right_u = mul(uu, at) + mul(uq, bt)
    right_q = mul(qu, at) + mul(qq, bt)
    a2 = mul(a, right_s) + mul(b, right_u)
    c2 = mul(p0, right_s)
    ww = mul(a, right_u) + mul(b, right_q)
    a2t, c2t = flip(a2), flip(c2)
    up2, p2 = factor(ww - mul(a2t, a2) - mul(c2t, c2))
    weights = (
        -mul(p2, mul(a2t, a) + mul(c2t, p0)),
        mul(p2, a - mul(a2t, b)),
        mul(p2, b),
    )
    small = (slice(0, vectors), slice(0, vectors))
    diag_ref[0] = a1[small]
    diag_ref[1] = a2[small]
    off_ref[0] = up1[small]
    off_ref[1] = up2[small]
    for comp in range(3):
        value = None
        for weight, ref in zip(weights, (start_ref, first_ref, second_ref)):
            for w in range(vectors):
                line = GROUP * comp + w
                term = weight[:, w : w + 1] * ref[line : line + 1, :]
                value = term if value is None else value + term
        next_ref[0, 0, 0, comp] = value[:vectors]


def call(body, outs, args, scratch=()):
    outs = [shape if isinstance(shape[0], tuple) else (shape, jnp.float32) for shape in outs]
    return pl.pallas_call(
        body,
        out_shape=[jax.ShapeDtypeStruct(shape, kind) for shape, kind in outs],
        in_specs=[pl.BlockSpec(memory_space=pltpu.VMEM)] * len(args),
        out_specs=[pl.BlockSpec(memory_space=pltpu.VMEM)] * len(outs),
        scratch_shapes=[pltpu.VMEM(shape, jnp.float32) for shape in scratch],
        compiler_params=pltpu.CompilerParams(vmem_limit_bytes=VMEM_BYTES),
    )(*args)


def table_index(neighbors, atoms, ghosts):
    entry = neighbors - atoms
    cell = entry // ghosts
    number = cell
    kept = [n for n in range(64) if not all(m in (1, 2) for m in (n // 16, n // 4 % 4, n % 4))]
    previous = -1
    for position, n in enumerate(kept):
        if n - previous > 1:
            number = number + jnp.where(cell >= position, n - previous - 1, 0)
        previous = n
    member = (number // 16, number // 4 % 4, number % 4)
    kind = 0
    octant = 0
    for bit, m in enumerate(member):
        kind = kind + jnp.where((m == 0) | (m == 3), 1 << bit, 0)
        octant = 2 * octant + (m + 1) % 2
    place = atoms + (kind - 1) * (8 * ghosts) + octant * ghosts + entry % ghosts
    return jnp.where(neighbors < atoms, neighbors, place)


def on_device(
    positions,
    species,
    start_block,
    neighbors,
    ghost_lists,
    embedding,
    radial_in,
    radial_out,
    readout,
):
    atoms = positions.shape[-1]
    ghosts = ghost_lists.shape[-1]
    vectors = start_block.shape[3]
    fanout = neighbors.shape[3]
    channels = embedding.shape[1]
    devices = lax.axis_size("gx") * lax.axis_size("gy") * lax.axis_size("gz")
    scale = 1.0 / (3.0 * atoms * devices)
    width = 8 * ghosts
    high = 3 * GROUP
    edges = fanout * atoms
    index = table_index(neighbors.reshape(1, -1), atoms, ghosts)
    table_width = atoms + 7 * width
    ring = lax.axis_size("gx") == 4
    side = (octant_bit((GROUP, width), 0, ghosts) ^ (lax.axis_index("gx") % 2 == 1)).astype(
        jnp.float32
    )

    own, octants, lists = call(
        pack_kernel,
        [(high, atoms), (high, width), ((1, width), jnp.int32)],
        (positions, species, start_block.transpose(0, 1, 2, 4, 3, 5), ghost_lists),
    )

    def spread(level):
        if level.shape[1] == width:
            level = jnp.concatenate([level, fetch_ghosts(level, 0, ghosts)], axis=1)
        return (level,) + spread_outer(level, ghosts)

    pairs = len(pair_list(fanout))
    shared = [
        (vectors * (fanout + pairs) * GROUP, atoms),
        ((fanout + pairs) * GROUP, atoms),
        (vectors * (fanout + pairs) * GROUP, atoms),
    ]
    base_sums = 2 * fanout + pairs + fanout * fanout
    saved_shapes = [
        ((LANES, edges), jnp.bfloat16),
        (high, edges),
        (GROUP, edges),
        (GROUP * (-(-base_sums // 4)), atoms),
        (pairs * GROUP, atoms),
    ] + [(channels, edges)] * 5
    results = call(
        functools.partial(first_kernel, ghosts, vectors),
        [(high, atoms), (high, 7 * width)] + saved_shapes,
        (index, own)
        + spread(octants)
        + (embedding, radial_in, radial_out.T, readout.reshape(1, -1)),
        [(high, table_width), (channels, edges), (channels, LANES)]
        + shared
        + [(base_sums * GROUP, atoms)],
    )
    own_terms, ghost_terms, saved = results[0], results[1], results[2:]

    sums, beside = return_outer(ghost_terms, width, ghosts)
    if ring:
        part, packet = call(
            functools.partial(start_kernel, vectors),
            [(high, atoms), (high, 2 * width)],
            (own_terms, sums, beside, lists),
        )
        others = pair_exchange(packet, "gx", (1, 2, 3))
        first, level = call(
            functools.partial(merge_kernel, vectors),
            [(high, atoms), (high, 2 * width)],
            (side, part, packet, *others),
            [(high, atoms)],
        )
    else:
        first, level = call(
            functools.partial(middle_kernel, vectors),
            [(high, atoms), (high, width)],
            (own_terms, sums + return_ghosts(beside, 0, ghosts), lists),
        )
    own_terms, ghost_terms, edge_gram = call(
        functools.partial(second_kernel, ghosts, vectors),
        [(high, atoms), (high, 7 * width), (GROUP, LANES)],
        (index, first) + spread(level) + tuple(saved),
        [(high, table_width)] + shared,
    )
    sums, beside = return_outer(ghost_terms, width, ghosts)
    if ring:
        part, packet = call(
            functools.partial(gram_start_kernel, vectors),
            [(high, atoms), (high, 2 * width + LANES)],
            (own, first, own_terms, sums, beside, lists, edge_gram),
        )
        others = pair_exchange(packet, "gx", (1, 2, 3))
        second, gram = call(
            functools.partial(gram_merge_kernel, vectors),
            [(high, atoms), (high, LANES)],
            (side, part, packet, *others),
        )
        gram = sum_over(gram, AXES[1:])
    else:
        second, gram = call(
            functools.partial(gram_kernel, vectors),
            [(high, atoms), (high, LANES)],
            (own, first, own_terms, sums + return_ghosts(beside, 0, ghosts), lists),
        )
        gram = sum_over(gram, AXES)
    following, diagonal, off = call(
        functools.partial(last_kernel, vectors, scale),
        [(1, 1, 1, 3, vectors, atoms), (2, vectors, vectors), (2, vectors, vectors)],
        (own, first, second, gram),
    )
    return following.transpose(0, 1, 2, 4, 3, 5), diagonal, off


def solution(mesh):
    return jax.shard_map(
        on_device,
        mesh=mesh,
        in_specs=(
            P("gx", "gy", "gz", None, None),
            P("gx", "gy", "gz", None),
            P("gx", "gy", "gz", None, None, None),
            P("gx", "gy", "gz", None, None),
            P("gx", "gy", "gz", None),
            P(),
            P(),
            P(),
            P(),
        ),
        out_specs=(P("gx", "gy", "gz", None, None, None), P(), P()),
        check_vma=False,
    )
```

```python
import functools
import math

import jax
import jax.numpy as jnp
import numpy as np
from jax import lax
from jax.experimental import pallas as pl
from jax.experimental.pallas import tpu as pltpu
from jax.sharding import PartitionSpec as P

SOFTEN = 0.25
CUTOFF = 4.0
HIGHEST = lax.Precision.HIGHEST
LANES = 128
GROUP = 8
AXES = ("gx", "gy", "gz")
VMEM_BYTES = 48 * 1024 * 1024


def swap_pairs(size, distance):
    return [(i, (i + distance) % size) for i in range(size)]


def octant_bit(shape, bit, ghosts):
    lane = lax.broadcasted_iota(jnp.int32, shape, 1) % (8 * ghosts)
    return (lane // ghosts // (4 >> bit)) % 2 == 1


def pair_exchange(x, axis, distances):
    size = lax.axis_size(axis)
    return [lax.ppermute(x, axis, [(i, i ^ d) for i in range(size)]) for d in distances]


def ring_sides(x, bit):
    axis = AXES[bit]
    size = lax.axis_size(axis)
    if size == 4:
        near, far = pair_exchange(x, axis, (1, 3))
        return near, far, lax.axis_index(axis) % 2 == 1
    above = lax.ppermute(x, axis, swap_pairs(size, -1))
    below = lax.ppermute(x, axis, swap_pairs(size, 1))
    return above, below, False


def fetch_ghosts(x, bit, ghosts):
    axis = AXES[bit]
    size = lax.axis_size(axis)
    if size == 1:
        return x
    if size == 2:
        return lax.ppermute(x, axis, swap_pairs(2, 1))
    near, far, odd = ring_sides(x, bit)
    return jnp.where(octant_bit(x.shape, bit, ghosts) ^ odd, far, near)


def return_ghosts(x, bit, ghosts):
    axis = AXES[bit]
    size = lax.axis_size(axis)
    if size == 1:
        return x
    if size == 2:
        return lax.ppermute(x, axis, swap_pairs(2, 1))
    near, far, odd = ring_sides(x, bit)
    return jnp.where(octant_bit(x.shape, bit, ghosts) ^ odd, near, far)


def spread_outer(level, ghosts):
    second = fetch_ghosts(level, 1, ghosts)
    level = jnp.concatenate([level, second], axis=1)
    return second, fetch_ghosts(level, 2, ghosts)


def return_outer(terms, width, ghosts):
    got = return_ghosts(terms[:, 3 * width :], 2, ghosts)
    inner = got[:, :width]
    first = terms[:, :width] + got[:, width : 2 * width]
    second = terms[:, width : 3 * width] + got[:, 2 * width :]
    got = return_ghosts(second, 1, ghosts)
    return inner + got[:, :width], first + got[:, width:]


def sum_over(x, axes):
    for axis in axes:
        size = lax.axis_size(axis)
        if size & (size - 1):
            x = lax.psum(x, axis)
            continue
        step = 1
        while step < size:
            x = x + lax.ppermute(x, axis, [(i, i ^ step) for i in range(size)])
            step *= 2
    return x


def rows(a):
    return slice(GROUP * a, GROUP * (a + 1))


def gather_lanes(table, index_row, group):
    lane = jnp.broadcast_to(index_row % LANES, (GROUP, LANES))
    tile = jnp.broadcast_to(index_row // LANES, (GROUP, LANES))
    out = None
    for number in range(table.shape[1] // LANES):
        source = table[rows(group), number * LANES : (number + 1) * LANES]
        picked = jnp.take_along_axis(source, lane, axis=1, mode="promise_in_bounds")
        out = picked if out is None else jnp.where(tile == number, picked, out)
    return out


def column(line):
    size = line.shape[1]
    shape = (size, size)
    same = lax.broadcasted_iota(jnp.int32, shape, 0) == lax.broadcasted_iota(jnp.int32, shape, 1)
    return jnp.sum(jnp.where(same, line, 0.0), axis=1, keepdims=True)


def split_rows(y, vectors):
    high = y.astype(jnp.bfloat16).astype(jnp.float32)
    return high + pltpu.roll(y - high, vectors, 0)


def join_rows(y, vectors):
    return y + pltpu.roll(y, GROUP - vectors, 0)


def pack_kernel(pos_hbm, spec_hbm, block_hbm, raw_hbm, own_ref, oct_ref, list_ref, *scratch):
    pos_ref, spec_ref, block_ref, raw_ref, sems = scratch
    copies = [
        pltpu.make_async_copy(source, target, sems.at[n])
        for n, (source, target) in enumerate(
            (
                (pos_hbm, pos_ref),
                (spec_hbm, spec_ref),
                (block_hbm, block_ref),
                (raw_hbm, raw_ref),
            )
        )
    ]
    for copy in copies:
        copy.start()
    for copy in copies:
        copy.wait()
    vectors = block_ref.shape[4]
    atoms = pos_ref.shape[-1]
    for a in range(3):
        parts = [block_ref[0, 0, 0, a], pos_ref[a]]
        used = vectors + 1
        if a == 0:
            parts.append(spec_ref[0, 0].astype(jnp.float32))
            used += 1
        parts.append(jnp.zeros((GROUP - used, atoms), jnp.float32))
        own_ref[rows(a), :] = jnp.concatenate(parts, axis=0)
    pieces = [raw_ref[n // 4, n // 2 % 2, n % 2 : n % 2 + 1, :] for n in range(8)]
    list_ref[...] = jnp.concatenate(pieces, axis=1)
    pick_octants(own_ref, list_ref, oct_ref)


def prepare_kernel(
    atoms, ghosts, near_ref, emb_ref, rin_ref, rout_ref, read_ref, idx_ref, low_ref, in_ref, out_ref, col_ref
):
    index = table_index(near_ref[...], atoms, ghosts)
    idx_ref[...] = index
    low = lax.broadcasted_iota(jnp.int32, low_ref.shape, 0) == index % LANES
    low_ref[...] = jnp.where(low, 1.0, 0.0).astype(jnp.bfloat16)
    high, middle, rest = split_parts(rin_ref[...])
    stack = [high, middle, rest, high, middle, high]
    pad = in_ref.shape[1] - 6 * rin_ref.shape[0]
    stack = jnp.concatenate(stack + [jnp.zeros((pad, rin_ref.shape[1]), jnp.float32)], axis=0)
    in_ref[...] = jnp.transpose(stack).astype(jnp.bfloat16)
    high, rest, _ = split_parts(rout_ref[...])
    out_ref[...] = jnp.concatenate(
        [jnp.concatenate([high, high], axis=1), jnp.concatenate([rest, rest], axis=1)], axis=0
    ).astype(jnp.bfloat16)
    species = emb_ref.shape[0]
    lane = lax.broadcasted_iota(jnp.int32, col_ref.shape, 1)
    columns = jnp.broadcast_to(column(read_ref[...]), col_ref.shape)
    for n in range(species):
        columns = jnp.where(lane == n, column(emb_ref[n : n + 1, :]), columns)
    col_ref[...] = columns


def pick_octants(own_ref, list_ref, oct_ref):
    for j in range(list_ref.shape[1] // LANES):
        cut = slice(j * LANES, (j + 1) * LANES)
        for a in range(3):
            oct_ref[rows(a), cut] = gather_lanes(own_ref, list_ref[:, cut], a)


def add_octants(own, octants, lists, vectors):
    atoms = own.shape[1]
    width = lists.shape[1]
    keep = lax.broadcasted_iota(jnp.int32, octants.shape, 0) < vectors
    packed = split_rows(jnp.where(keep, octants, 0.0), vectors).astype(jnp.bfloat16)
    onehot = lax.broadcasted_iota(jnp.int32, (atoms, width), 0) == lists
    spread = lax.dot_general(
        packed,
        jnp.where(onehot, 1.0, 0.0).astype(jnp.bfloat16),
        (((1,), (1,)), ((), ())),
        preferred_element_type=jnp.float32,
    )
    return own + join_rows(spread, vectors)


def fill_table(table, own_ref, ghost_refs, vectors, ghosts, shifted):
    atoms = own_ref.shape[1]
    table[:, :atoms] = own_ref[...]
    width = 8 * ghosts
    base = atoms
    kind = 1
    for number, ref in enumerate(ghost_refs):
        for j in range(number == 0, ref.shape[1] // width):
            part = ref[:, j * width : (j + 1) * width]
            if shifted:
                row = lax.broadcasted_iota(jnp.int32, part.shape, 0)
                for a in range(3):
                    if (kind >> a) & 1:
                        move = jnp.where(octant_bit(part.shape, a, ghosts), -1.0, 1.0)
                        part = part + jnp.where(row == GROUP * a + vectors, move, 0.0)
            table[:, base : base + width] = part
            base += width
            kind += 1


def gather_slot(table, idx_ref, k, atoms):
    pieces = [[] for _ in range(3)]
    for j in range(atoms // LANES):
        index_row = idx_ref[:, pl.ds(pl.multiple_of(k * atoms + j * LANES, LANES), LANES)]
        for a in range(3):
            pieces[a].append(gather_lanes(table, index_row, a))
    return [jnp.concatenate(p, axis=1) for p in pieces]


def pair_list(fanout):
    return [(k, l) for k in range(fanout) for l in range(k, fanout)]


def lookup(table, fanout):
    where = {pair: n for n, pair in enumerate(pair_list(fanout))}
    return lambda k, l: table[where[min(k, l), max(k, l)]]


def sum_rows(parts):
    row = lax.broadcasted_iota(jnp.int32, parts[0].shape, 0)
    if len(parts) != 4 or GROUP != 8:
        out = jnp.zeros_like(parts[0])
        for n, part in enumerate(parts):
            out = jnp.where(row == n, jnp.sum(part, axis=0, keepdims=True), out)
        return out
    fold = [part + pltpu.roll(part, 4, 0) for part in parts]
    low = row < 4
    lead = jnp.where(low, fold[0], fold[1])
    rest = jnp.where(low, fold[2], fold[3])
    both = jnp.where(row % 4 < 2, lead + pltpu.roll(lead, 6, 0), rest + pltpu.roll(rest, 2, 0))
    even = both + pltpu.roll(both, 7, 0)
    odd = both + pltpu.roll(both, 1, 0)
    return jnp.where(row % 2 == 1, pltpu.roll(odd, 4, 0), even)


def dot3(x, y):
    return x[0] * y[0] + x[1] * y[1] + x[2] * y[2]


def slot_cut(k, atoms):
    return slice(k * atoms, (k + 1) * atoms)


def tile_rows(n):
    return slice(GROUP * n, GROUP * (n + 1))


def tangents(diffs, units, invs, tn, changes, vectors):
    fanout = len(diffs)
    pairs = pair_list(fanout)
    per_vector = fanout + len(pairs)
    taus = [dot3(units[k], diffs[k]) for k in range(fanout)]
    turns = [
        [(diffs[k][a] - units[k][a] * taus[k]) * invs[k] for a in range(3)] for k in range(fanout)
    ]
    values = list(taus)
    for k, l in pairs:
        half = dot3(units[k], turns[l])
        values.append(2.0 * half if k == l else half + dot3(units[l], turns[k]))
    for n, value in enumerate(values):
        changes[tile_rows(n), :] = value
        for v in range(vectors):
            tn[tile_rows(v * per_vector + n), :] = jnp.broadcast_to(
                value[v : v + 1, :], value.shape
            )


def channel_products(f, f1, q, rp, rpp, cosine, tn, acc, lanes, fanout, vectors):
    pairs = pair_list(fanout)
    per_vector = fanout + len(pairs)
    slots = range(fanout)
    rpp_q = [rpp[k] * q[k] for k in slots]
    rpp_f = [rpp[k] * f[k] for k in slots]
    for v in range(vectors):
        base = v * per_vector

        def tangent(n):
            return tn[tile_rows(base + n), lanes]

        phi = [f1[k] * tangent(k) for k in slots]
        index = {pair: fanout + n for n, pair in enumerate(pairs)}
        dq = []
        for k in slots:
            total = None
            for l in slots:
                term = phi[l] * cosine(k, l) + f[l] * tangent(index[min(k, l), max(k, l)])
                total = term if total is None else total + term
            dq.append(total)
        y = [phi[k] * rpp_q[k] + dq[k] * rpp_f[k] for k in slots]
        w = [y[k] * f[k] + rp[k] * phi[k] for k in slots]
        for k in slots:
            total = y[k] * q[k] + rp[k] * dq[k]
            for l in slots:
                total = total + w[l] * cosine(k, l)
            acc[tile_rows(base + k), lanes] += f1[k] * total
        for n, (k, l) in enumerate(pairs):
            term = w[k] * f[l] if k == l else w[k] * f[l] + w[l] * f[k]
            acc[tile_rows(base + fanout + n), lanes] += term


def finish_product(
    idx_ref, low_ref, unit_ref, inv_ref, sums_ref, acc, changes, diffs, own_out, ghost_out, vectors
):
    atoms = own_out.shape[1]
    fanout = idx_ref.shape[1] // atoms
    tiles = (atoms + ghost_out.shape[1]) // LANES
    pairs = pair_list(fanout)
    per_vector = fanout + len(pairs)
    slots = range(fanout)
    row = lax.broadcasted_iota(jnp.int32, (GROUP, atoms), 0)
    outs = [
        sum_rows([acc[tile_rows(v * per_vector + n), :] for v in range(vectors)])
        for n in range(per_vector)
    ]
    taus = [changes[tile_rows(k), :] for k in slots]
    turned = lookup([changes[tile_rows(fanout + n), :] for n in range(len(pairs))], fanout)
    bent = lookup(outs[fanout:], fanout)
    units = [[unit_ref[rows(a), slot_cut(k, atoms)] for a in range(3)] for k in slots]
    invs = [inv_ref[:, slot_cut(k, atoms)] for k in slots]
    turns = [
        [(diffs[k][a] - units[k][a] * taus[k]) * invs[k] for a in range(3)] for k in slots
    ]

    def base_sum(n):
        line = (n // 4) * GROUP + n % 4
        return sums_ref[line : line + 1, :]

    stretch = [base_sum(k) for k in slots]
    curve = [base_sum(fanout + k) for k in slots]
    weight = lookup([base_sum(2 * fanout + n) for n in range(len(pairs))], fanout)
    mixed = [[base_sum(2 * fanout + len(pairs) + k * fanout + l) for l in slots] for k in slots]
    center = [jnp.zeros((GROUP, atoms), jnp.float32) for _ in range(3)]
    shifted = [jnp.zeros((GROUP, atoms), jnp.float32) for _ in range(vectors)]
    left = []
    for k in slots:
        along = outs[k] + curve[k] * taus[k]
        force = [0.0, 0.0, 0.0]
        change = [0.0, 0.0, 0.0]
        for l in slots:
            along = along + turned(k, l) * mixed[k][l]
            bend = bent(k, l) + taus[l] * mixed[l][k] + taus[k] * mixed[k][l]
            pull = weight(k, l)
            if k == l:
                bend = bend + bent(k, l)
                pull = pull + pull
            for a in range(3):
                force[a] = force[a] + pull * units[l][a]
                change[a] = change[a] + bend * units[l][a] + pull * turns[l][a]
        flat = dot3(units[k], force)
        inv = invs[k]
        along = (
            along
            - (dot3(units[k], change) + dot3(turns[k], force)) * inv
            + taus[k] * flat * (inv * inv)
        )
        keep = stretch[k] - flat * inv
        packed = []
        for a in range(3):
            y = (
                along * units[k][a]
                + keep * turns[k][a]
                + (change[a] - taus[k] * inv * force[a]) * inv
            )
            y = jnp.where(row < vectors, y, 0.0)
            center[a] = center[a] - y
            for n in range(vectors):
                other = y if n == 0 else pltpu.roll(y, n, 0)
                if n:
                    other = other + pltpu.roll(y, GROUP - vectors + n, 0)
                shifted[n] = shifted[n] + other * diffs[k][a]
            packed.append(split_rows(y, vectors))
        packed = jnp.concatenate(packed, axis=0)
        tile = idx_ref[:, slot_cut(k, atoms)] // LANES
        left.append(
            jnp.concatenate(
                [jnp.where(tile == number, packed, 0.0) for number in range(tiles)], axis=0
            ).astype(jnp.bfloat16)
        )
    spread = lax.dot_general(
        jnp.concatenate(left, axis=1),
        low_ref[...],
        (((1,), (1,)), ((), ())),
        preferred_element_type=jnp.float32,
    )
    own_tiles = atoms // LANES
    for number in range(tiles):
        for a in range(3):
            value = join_rows(spread[tile_rows(number * 3 + a)], vectors)
            if number < own_tiles:
                cut = slice(number * LANES, (number + 1) * LANES)
                own_out[rows(a), cut] = value + center[a][:, cut]
            else:
                cut = number - own_tiles
                ghost_out[rows(a), cut * LANES : (cut + 1) * LANES] = value
    return shifted


def split_parts(x):
    high = x.astype(jnp.bfloat16).astype(jnp.float32)
    rest = x - high
    middle = rest.astype(jnp.bfloat16).astype(jnp.float32)
    low = (rest - middle).astype(jnp.bfloat16).astype(jnp.float32)
    return high, middle, low


def silu_slopes(x):
    sig = 0.5 + 0.5 * jnp.tanh(0.5 * x)
    anti = 1.0 - sig
    return sig, sig * (1.0 + x * anti), sig * anti * (2.0 + x * (anti - sig))


def half_turns(dist, inv, basis):
    shape = (basis, dist.shape[1])
    order = (lax.broadcasted_iota(jnp.int32, shape, 0) + 1).astype(jnp.float32)
    turns = order * (dist * (1.0 / CUTOFF))
    whole = jnp.floor(turns + 0.5)
    sign = 1.0 - 2.0 * (whole - 2.0 * jnp.floor(whole * 0.5))
    x = (turns - whole) * np.float32(np.pi)
    x2 = x * x

    def series(terms):
        value = terms[-1]
        for term in terms[-2::-1]:
            value = term + x2 * value
        return value

    sine = sign * x * series([(-1.0) ** n / math.factorial(2 * n + 1) for n in range(6)])
    cosine = sign * series([(-1.0) ** n / math.factorial(2 * n) for n in range(7)])
    omega = order * np.float32(np.pi / CUTOFF)
    b0 = sine * inv
    b1 = (omega * cosine - b0) * inv
    b2 = -(omega * omega * sine + 2.0 * b1) * inv
    return jnp.concatenate([b0, b1, b2], axis=1)


def first_kernel(
    ghosts,
    vectors,
    basis,
    species,
    idx_ref,
    own_ref,
    g1_ref,
    g2_ref,
    g3_ref,
    low_ref,
    in_ref,
    out_ref,
    col_ref,
    own_out,
    ghost_out,
    unit_ref,
    inv_ref,
    sums_ref,
    cos_ref,
    f_ref,
    f1_ref,
    q_ref,
    rp_ref,
    rpp_ref,
    table,
    f2_ref,
    read_col,
    tn,
    changes,
    acc,
    acc2,
):
    atoms = own_ref.shape[1]
    fanout = idx_ref.shape[1] // atoms
    channels = col_ref.shape[0]
    pairs = pair_list(fanout)
    slots = range(fanout)
    embeds = [col_ref[:, n : n + 1] for n in range(species)]
    read_col[...] = jnp.broadcast_to(col_ref[:, species : species + 1], read_col.shape)
    fill_table(table, own_ref, (g1_ref, g2_ref, g3_ref), vectors, ghosts, True)

    def embed(kind):
        value = embeds[0]
        for n in range(1, species):
            value = jnp.where(kind == float(n), embeds[n], value)
        return value

    own_embed = embed(own_ref[vectors + 1 : vectors + 2, :])
    inward = in_ref[:, : 6 * basis]
    outward = out_ref[...]
    diffs, units, invs = [], [], []
    for k in slots:
        cut = slot_cut(k, atoms)
        near = gather_slot(table, idx_ref, k, atoms)
        diff = [near[a] - own_ref[rows(a), :] for a in range(3)]
        delta = [
            jnp.broadcast_to(diff[a][vectors : vectors + 1, :], (GROUP, atoms)) for a in range(3)
        ]
        dist = jnp.sqrt(dot3(delta, delta) + SOFTEN)
        inv = 1.0 / dist
        unit = [delta[a] * inv for a in range(3)]
        for a in range(3):
            unit_ref[rows(a), cut] = unit[a]
        inv_ref[:, cut] = inv
        diffs.append(diff)
        units.append(unit)
        invs.append(inv)
        one = dist[0:1]
        radii = half_turns(one, inv[0:1], basis)
        high, middle, rest = split_parts(radii)
        z = jnp.dot(
            inward,
            jnp.concatenate([high, high, high, middle, middle, rest], axis=0).astype(jnp.bfloat16),
            preferred_element_type=jnp.float32,
        )
        z0, z1, z2 = z[:, :atoms], z[:, atoms : 2 * atoms], z[:, 2 * atoms :]
        sig, slope, curve = silu_slopes(z0)
        hidden = jnp.concatenate([z0 * sig, slope * z1, curve * z1 * z1 + slope * z2], axis=1)
        high = hidden.astype(jnp.bfloat16)
        rest = (hidden - high.astype(jnp.float32)).astype(jnp.bfloat16)
        radial = jnp.dot(
            outward, jnp.concatenate([high, rest], axis=0), preferred_element_type=jnp.float32
        )
        radial = radial[:channels] + radial[channels:]
        r0, r1, r2 = radial[:, :atoms], radial[:, atoms : 2 * atoms], radial[:, 2 * atoms :]
        square = one * one
        base = 1.0 - square * (1.0 / CUTOFF**2)
        v0 = base * base
        v1 = base * one * (-4.0 / CUTOFF**2)
        v2 = -4.0 / CUTOFF**2 + square * (12.0 / CUTOFF**4)
        pair = own_embed * embed(near[0][vectors + 1 : vectors + 2, :])
        f_ref[:, cut] = pair * (r0 * v0)
        f1_ref[:, cut] = pair * (r1 * v0 + r0 * v1)
        f2_ref[:, cut] = pair * (r2 * v0 + 2.0 * (r1 * v1) + r0 * v2)
    for n, (k, l) in enumerate(pairs):
        cos_ref[tile_rows(n), :] = 1.0 + dot3(units[k], units[l])
    tangents(diffs, units, invs, tn, changes, vectors)
    acc[...] = jnp.zeros_like(acc)
    acc2[...] = jnp.zeros_like(acc2)
    share = 1.0 / fanout

    def tile(number, carry):
        here = pl.ds(pl.multiple_of(number * GROUP, GROUP), GROUP)
        for half in range(atoms // LANES):
            lanes = slice(half * LANES, (half + 1) * LANES)
            cuts = [slice(k * atoms + half * LANES, k * atoms + (half + 1) * LANES) for k in slots]
            cosine = lookup([cos_ref[tile_rows(n), lanes] for n in range(len(pairs))], fanout)
            f = [f_ref[here, cut] for cut in cuts]
            f1 = [f1_ref[here, cut] for cut in cuts]
            read = read_col[here, :] * share
            q, rp, rpp = [], [], []
            for k in slots:
                project = sum(f[l] * cosine(k, l) for l in slots)
                _, slope, curve = silu_slopes(f[k] * project * share)
                q.append(project)
                rp.append(read * slope)
                rpp.append(read * share * curve)
                q_ref[here, cuts[k]] = q[k]
                rp_ref[here, cuts[k]] = rp[k]
                rpp_ref[here, cuts[k]] = rpp[k]
            m = [rp[k] * f[k] for k in slots]
            slope = [rp[k] * q[k] + sum(m[l] * cosine(k, l) for l in slots) for k in slots]
            terms = [slope[k] * f1[k] for k in slots]
            terms += [slope[k] * f2_ref[here, cuts[k]] for k in slots]
            terms += [m[k] * f[l] if k == l else m[k] * f[l] + m[l] * f[k] for k, l in pairs]
            terms += [f1[k] * m[l] for k in slots for l in slots]
            for n, term in enumerate(terms):
                acc2[tile_rows(n), lanes] += term
            channel_products(f, f1, q, rp, rpp, cosine, tn, acc, lanes, fanout, vectors)
        return carry

    lax.fori_loop(0, channels // GROUP, tile, 0)
    count = acc2.shape[0] // GROUP
    for n in range(0, count, 4):
        parts = [acc2[tile_rows(min(n + j, count - 1)), :] for j in range(4)]
        sums_ref[tile_rows(n // 4), :] = sum_rows(parts)
    finish_product(
        idx_ref,
        low_ref,
        unit_ref,
        inv_ref,
        sums_ref,
        acc,
        changes,
        diffs,
        own_out,
        ghost_out,
        vectors,
    )


def second_kernel(
    ghosts,
    vectors,
    idx_ref,
    own_ref,
    g1_ref,
    g2_ref,
    g3_ref,
    low_ref,
    unit_ref,
    inv_ref,
    sums_ref,
    cos_ref,
    f_ref,
    f1_ref,
    q_ref,
    rp_ref,
    rpp_ref,
    own_out,
    ghost_out,
    gram_out,
    table,
    tn,
    changes,
    acc,
):
    atoms = own_ref.shape[1]
    fanout = idx_ref.shape[1] // atoms
    channels = f_ref.shape[0]
    pairs = pair_list(fanout)
    slots = range(fanout)
    fill_table(table, own_ref, (g1_ref, g2_ref, g3_ref), vectors, ghosts, False)
    diffs = []
    for k in slots:
        near = gather_slot(table, idx_ref, k, atoms)
        diffs.append([near[a] - own_ref[rows(a), :] for a in range(3)])
    units = [[unit_ref[rows(a), slot_cut(k, atoms)] for a in range(3)] for k in slots]
    invs = [inv_ref[:, slot_cut(k, atoms)] for k in slots]
    tangents(diffs, units, invs, tn, changes, vectors)
    acc[...] = jnp.zeros_like(acc)

    def tile(number, carry):
        here = pl.ds(pl.multiple_of(number * GROUP, GROUP), GROUP)
        for half in range(atoms // LANES):
            lanes = slice(half * LANES, (half + 1) * LANES)
            cuts = [slice(k * atoms + half * LANES, k * atoms + (half + 1) * LANES) for k in slots]
            cosine = lookup([cos_ref[tile_rows(n), lanes] for n in range(len(pairs))], fanout)
            parts = [
                [ref[here, cut] for cut in cuts] for ref in (f_ref, f1_ref, q_ref, rp_ref, rpp_ref)
            ]
            channel_products(*parts, cosine, tn, acc, lanes, fanout, vectors)
        return carry

    lax.fori_loop(0, channels // GROUP, tile, 0)
    shifted = finish_product(
        idx_ref,
        low_ref,
        unit_ref,
        inv_ref,
        sums_ref,
        acc,
        changes,
        diffs,
        own_out,
        ghost_out,
        vectors,
    )
    gram_out[...] = from_shifted(shifted, vectors)


def middle_kernel(vectors, own_ref, sums_ref, list_ref, full_ref, oct_ref):
    for a in range(3):
        full_ref[rows(a), :] = add_octants(
            own_ref[rows(a), :], sums_ref[rows(a), :], list_ref[...], vectors
        )
    pick_octants(full_ref, list_ref, oct_ref)


def inner(x, y, pad_to=LANES):
    pad = jnp.zeros((pad_to - y.shape[0], y.shape[1]), jnp.float32)
    return lax.dot_general(
        x,
        jnp.concatenate([y, pad], axis=0),
        (((1,), (1,)), ((), ())),
        precision=HIGHEST,
        preferred_element_type=jnp.float32,
    )


def only_vectors(x, vectors):
    row = lax.broadcasted_iota(jnp.int32, x.shape, 0)
    return jnp.where(row % GROUP < vectors, x, 0.0)


def pack_gram(total, edge):
    lane = lax.broadcasted_iota(jnp.int32, (GROUP, LANES), 1)
    out = total[rows(0)]
    out = jnp.where(lane >= 2 * GROUP, pltpu.roll(total[rows(1)], GROUP, 1), out)
    if edge is not None:
        out = jnp.where(lane >= 3 * GROUP, pltpu.roll(edge, 3 * GROUP, 1), out)
    return jnp.where(lane >= 4 * GROUP, pltpu.roll(total[rows(2)], 2 * GROUP, 1), out)


def gram_kernel(vectors, start_ref, first_ref, own_ref, sums_ref, list_ref, full_ref, gram_ref):
    total = jnp.zeros((3 * GROUP, LANES), jnp.float32)
    for a in range(3):
        second = add_octants(own_ref[rows(a), :], sums_ref[rows(a), :], list_ref[...], vectors)
        full_ref[rows(a), :] = second
        stack = jnp.concatenate([start_ref[rows(a), :], first_ref[rows(a), :], second], axis=0)
        stack = only_vectors(stack, vectors)
        total += inner(stack, stack)
    gram_ref[...] = pack_gram(total, None)


def packet_start(vectors, own_ref, sums_ref, ghost_ref, list_ref, part_ref, packet_ref):
    width = list_ref.shape[1]
    for a in range(3):
        part_ref[rows(a), :] = add_octants(
            own_ref[rows(a), :], sums_ref[rows(a), :], list_ref[...], vectors
        )
    mark = vectors + 1
    for j in range(width // LANES):
        cut = slice(j * LANES, (j + 1) * LANES)
        for a in range(3):
            value = gather_lanes(part_ref, list_ref[:, cut], a)
            if a == 0:
                row = lax.broadcasted_iota(jnp.int32, value.shape, 0)
                value = jnp.where(row == mark, list_ref[:, cut].astype(jnp.float32), value)
            packet_ref[rows(a), cut] = value
    packet_ref[:, width : 2 * width] = ghost_ref[...]


def arriving(side, packets, n, a, width):
    cut = slice(width, 2 * width)
    after, before = packets[(n + 1) % 4], packets[(n + 3) % 4]
    return jnp.where(side > 0.5, after[rows(a), cut], before[rows(a), cut])


def packet_lists(packet, vectors, width):
    mark = vectors + 1
    return packet[mark : mark + 1, :width].astype(jnp.int32)


def start_kernel(vectors, own_ref, sums_ref, ghost_ref, list_ref, part_ref, packet_ref):
    packet_start(vectors, own_ref, sums_ref, ghost_ref, list_ref, part_ref, packet_ref)


def merge_kernel(
    vectors, side_ref, part_ref, p0_ref, p1_ref, p2_ref, p3_ref, full_ref, level_ref, spread
):
    width = p0_ref.shape[1] // 2
    side = side_ref[...]
    packets = (p0_ref, p1_ref, p2_ref, p3_ref)
    lists = [packet_lists(p, vectors, width) for p in packets]
    for a in range(3):
        full_ref[rows(a), :] = add_octants(
            part_ref[rows(a), :], arriving(side, packets, 0, a, width), lists[0], vectors
        )
    near = []
    for n in (1, 3):
        for a in range(3):
            zero = jnp.zeros((GROUP, part_ref.shape[1]), jnp.float32)
            spread[rows(a), :] = add_octants(
                zero, arriving(side, packets, n, a, width), lists[n], vectors
            )
        values = []
        for a in range(3):
            pieces = [
                gather_lanes(spread, lists[n][:, j * LANES : (j + 1) * LANES], a)
                for j in range(width // LANES)
            ]
            values.append(packets[n][rows(a), :width] + jnp.concatenate(pieces, axis=1))
        near.append(values)
    for a in range(3):
        for j in range(width // LANES):
            cut = slice(j * LANES, (j + 1) * LANES)
            level_ref[rows(a), cut] = gather_lanes(full_ref, lists[0][:, cut], a)
        level_ref[rows(a), width : 2 * width] = jnp.where(side > 0.5, near[1][a], near[0][a])


def gram_start_kernel(
    vectors,
    start_ref,
    first_ref,
    own_ref,
    sums_ref,
    ghost_ref,
    list_ref,
    edge_ref,
    part_ref,
    packet_ref,
):
    packet_start(vectors, own_ref, sums_ref, ghost_ref, list_ref, part_ref, packet_ref)
    width = list_ref.shape[1]
    total = jnp.zeros((3 * GROUP, LANES), jnp.float32)
    for a in range(3):
        stack = jnp.concatenate(
            [start_ref[rows(a), :], first_ref[rows(a), :], part_ref[rows(a), :]], axis=0
        )
        stack = only_vectors(stack, vectors)
        total += inner(stack, stack)
    cut = slice(2 * width, 2 * width + LANES)
    packet_ref[rows(0), cut] = pack_gram(total, edge_ref[...])
    packet_ref[GROUP : 3 * GROUP, cut] = jnp.zeros((2 * GROUP, LANES), jnp.float32)


def shifted_products(x, y, vectors):
    return [x * (pltpu.roll(y, n, 0) if n else y) for n in range(vectors)]


def from_shifted(shifted, vectors):
    shape = (GROUP, LANES)
    row = lax.broadcasted_iota(jnp.int32, shape, 0)
    lane = lax.broadcasted_iota(jnp.int32, shape, 1)
    total = jnp.zeros(shape, jnp.float32)
    for n in range(vectors):
        value = jnp.sum(shifted[n], axis=1, keepdims=True)
        total = jnp.where(lane == (row + vectors - n) % vectors, value, total)
    return jnp.where((row < vectors) & (lane < vectors), total, 0.0)


def gram_merge_kernel(
    vectors, side_ref, part_ref, p0_ref, p1_ref, p2_ref, p3_ref, full_ref, gram_ref, spread
):
    width = (p0_ref.shape[1] - LANES) // 2
    atoms = part_ref.shape[1]
    side = side_ref[...]
    packets = (p0_ref, p1_ref, p2_ref, p3_ref)
    shares = []
    for n in range(4):
        lists = packet_lists(packets[n], vectors, width)
        terms = [only_vectors(arriving(side, packets, n, a, width), vectors) for a in range(3)]
        packed = jnp.concatenate([split_rows(t, vectors) for t in terms], axis=0)
        onehot = lax.broadcasted_iota(jnp.int32, (atoms, width), 0) == lists
        placed = lax.dot_general(
            packed.astype(jnp.bfloat16),
            jnp.where(onehot, 1.0, 0.0).astype(jnp.bfloat16),
            (((1,), (1,)), ((), ())),
            preferred_element_type=jnp.float32,
        )
        total = None
        for a in range(3):
            value = join_rows(placed[rows(a)], vectors)
            spread[rows(a), :] = value
            if n == 0:
                full_ref[rows(a), :] = part_ref[rows(a), :] + value
            at = only_vectors(packets[n][rows(a), :width], vectors)
            at = at + pltpu.roll(at, vectors, 0)
            back = jnp.concatenate(
                [
                    gather_lanes(spread, lists[:, j * LANES : (j + 1) * LANES], a)
                    for j in range(width // LANES)
                ],
                axis=1,
            )
            found = shifted_products(terms[a], at + at + back, vectors)
            total = found if total is None else [x + y for x, y in zip(total, found)]
        shares.append([packets[n][rows(0), 2 * width : 2 * width + LANES]] + total)

    def add(x, y):
        return [p + q for p, q in zip(x, y)]

    total = add(add(shares[0], shares[1]), add(shares[2], shares[3]))
    gram = total[0] + pltpu.roll(from_shifted(total[1:], vectors), 4 * GROUP, 1)
    for n in range(gram_ref.shape[0]):
        gram_ref[n] = gram


def last_kernel(
    vectors, scale, start_ref, first_ref, second_ref, gram_ref, next_ref, diag_ref, off_ref
):
    shape = (GROUP, LANES)
    row = lax.broadcasted_iota(jnp.int32, shape, 0)
    lane = lax.broadcasted_iota(jnp.int32, shape, 1)
    inside = (row < vectors) & (lane < vectors)
    eye = jnp.where((row == lane) & inside, 1.0, 0.0)
    levels = [gram_ref[n] for n in range(gram_ref.shape[0])]
    while len(levels) > 1:
        levels = [sum(levels[n : n + 2]) for n in range(0, len(levels), 2)]
    gram = levels[0] * scale

    def block(x, n):
        return jnp.where(inside, pltpu.roll(x, LANES - GROUP * n, 1) if n else x, 0.0)

    def beside(*parts):
        out = parts[0]
        for n, part in enumerate(parts[1:]):
            out = out + pltpu.roll(part, GROUP * (n + 1), 1)
        return out

    def mul(x, y):
        return sum(x[:, k : k + 1] * y[k : k + 1, :] for k in range(vectors))

    def flip(x):
        out = jnp.zeros(shape, jnp.float32)
        for k in range(vectors):
            line = jnp.sum(eye * x[:, k : k + 1], axis=0, keepdims=True)
            out = jnp.where(row == k, line, out)
        return out

    def solve(m):
        for j in range(vectors):
            inverse = lax.rsqrt(m[j : j + 1, j : j + 1])
            line = m[j : j + 1, :] * inverse
            m = jnp.where(
                row == j, line, jnp.where(row > j, m - (m[:, j : j + 1] * inverse) * line, m)
            )
        return jnp.where((lane >= row) & inside, m, 0.0), m

    ss, su, uu, uq, qq = (block(gram, n) for n in range(5))
    qq = 0.5 * (qq + flip(qq))
    _, m = solve(beside(ss, su, uu, eye))
    p0 = block(m, 3)
    p0t = flip(p0)
    a1 = mul(block(m, 1), p0t)
    up1, m = solve(beside(mul(block(m, 2), p0t) - mul(a1, a1), p0, mul(a1, p0)))
    b, a = block(m, 1), -block(m, 2)
    at, bt = flip(a), flip(b)
    known = mul(up1, beside(flip(up1), p0))
    right_s = mul(su, at) + mul(uu, bt)
    right_u = mul(uu, at) + mul(uq, bt)
    right_q = mul(uq, at) + mul(qq, bt)
    a2 = mul(a, right_s) + mul(b, right_u)
    ww = mul(a, right_u) + mul(b, right_q)
    moved = mul(a2, beside(a2, a, b)) + known
    up2, m = solve(
        beside(ww - block(moved, 0), -block(moved, 1), a - block(moved, 2), b)
    )
    small = (slice(0, vectors), slice(0, vectors))
    diag_ref[0] = a1[small]
    diag_ref[1] = a2[small]
    off_ref[0] = up1[small]
    off_ref[1] = up2[small]
    for comp in range(3):
        value = None
        for n, ref in enumerate((start_ref, first_ref, second_ref)):
            for w in range(vectors):
                line = GROUP * comp + w
                place = GROUP * (n + 1) + w
                term = m[:, place : place + 1] * ref[line : line + 1, :]
                value = term if value is None else value + term
        next_ref[0, 0, 0, comp] = value[:vectors]


def call(body, outs, args, scratch=(), flops=0, spaces=pltpu.VMEM):
    outs = [shape if isinstance(shape[0], tuple) else (shape, jnp.float32) for shape in outs]
    return pl.pallas_call(
        body,
        out_shape=[jax.ShapeDtypeStruct(shape, kind) for shape, kind in outs],
        in_specs=[pl.BlockSpec(memory_space=spaces)] * len(args),
        out_specs=[pl.BlockSpec(memory_space=pltpu.VMEM)] * len(outs),
        scratch_shapes=[
            pltpu.VMEM(shape, jnp.float32) if isinstance(shape, tuple) else shape
            for shape in scratch
        ],
        cost_estimate=pl.CostEstimate(flops=flops, bytes_accessed=0, transcendentals=0)
        if flops
        else None,
        compiler_params=pltpu.CompilerParams(vmem_limit_bytes=VMEM_BYTES),
    )(*args)


def table_index(neighbors, atoms, ghosts):
    entry = neighbors - atoms
    cell = entry // ghosts
    number = cell
    kept = [n for n in range(64) if not all(m in (1, 2) for m in (n // 16, n // 4 % 4, n % 4))]
    previous = -1
    for position, n in enumerate(kept):
        if n - previous > 1:
            number = number + jnp.where(cell >= position, n - previous - 1, 0)
        previous = n
    member = (number // 16, number // 4 % 4, number % 4)
    kind = 0
    octant = 0
    for bit, m in enumerate(member):
        kind = kind + jnp.where((m == 0) | (m == 3), 1 << bit, 0)
        octant = 2 * octant + (m + 1) % 2
    place = atoms + (kind - 1) * (8 * ghosts) + octant * ghosts + entry % ghosts
    return jnp.where(neighbors < atoms, neighbors, place)


def on_device(
    positions,
    species,
    start_block,
    neighbors,
    ghost_lists,
    embedding,
    radial_in,
    radial_out,
    readout,
):
    atoms = positions.shape[-1]
    ghosts = ghost_lists.shape[-1]
    vectors = start_block.shape[3]
    fanout = neighbors.shape[3]
    channels = embedding.shape[1]
    devices = lax.axis_size("gx") * lax.axis_size("gy") * lax.axis_size("gz")
    scale = 1.0 / (3.0 * atoms * devices)
    width = 8 * ghosts
    high = 3 * GROUP
    edges = fanout * atoms
    table_width = atoms + 7 * width
    ring = lax.axis_size("gx") == 4
    others_count = lax.axis_size("gy") * lax.axis_size("gz")
    side = (octant_bit((GROUP, width), 0, ghosts) ^ (lax.axis_index("gx") % 2 == 1)).astype(
        jnp.float32
    )

    inputs = (
        positions.transpose(0, 1, 3, 2, 4).reshape(3, 1, atoms),
        species,
        start_block.transpose(0, 1, 2, 4, 3, 5),
        ghost_lists,
    )
    own, octants, lists = call(
        pack_kernel,
        [(high, atoms), (high, width), ((1, width), jnp.int32)],
        inputs,
        [pltpu.VMEM(x.shape, x.dtype) for x in inputs]
        + [pltpu.SemaphoreType.DMA((len(inputs),))],
        spaces=pl.ANY,
    )
    basis, hidden = radial_in.shape
    index, low, inward, outward, columns = call(
        functools.partial(prepare_kernel, atoms, ghosts),
        [
            ((1, edges), jnp.int32),
            ((LANES, edges), jnp.bfloat16),
            ((hidden, LANES * (-(-6 * basis // LANES))), jnp.bfloat16),
            ((2 * channels, 2 * hidden), jnp.bfloat16),
            (channels, LANES),
        ],
        (neighbors.reshape(1, -1), embedding, radial_in, radial_out.T, readout.reshape(1, -1)),
        flops=2_000_000,
    )

    def spread(level):
        if level.shape[1] == width:
            level = jnp.concatenate([level, fetch_ghosts(level, 0, ghosts)], axis=1)
        return (level,) + spread_outer(level, ghosts)

    pairs = len(pair_list(fanout))
    shared = [
        (vectors * (fanout + pairs) * GROUP, atoms),
        ((fanout + pairs) * GROUP, atoms),
        (vectors * (fanout + pairs) * GROUP, atoms),
    ]
    base_sums = 2 * fanout + pairs + fanout * fanout
    saved_shapes = [
        (high, edges),
        (GROUP, edges),
        (GROUP * (-(-base_sums // 4)), atoms),
        (pairs * GROUP, atoms),
    ] + [(channels, edges)] * 5
    results = call(
        functools.partial(first_kernel, ghosts, vectors, basis, embedding.shape[0]),
        [(high, atoms), (high, 7 * width)] + saved_shapes,
        (index, own)
        + spread(octants)
        + (low, inward, outward, columns),
        [(high, table_width), (channels, edges), (channels, LANES)]
        + shared
        + [(base_sums * GROUP, atoms)],
    )
    own_terms, ghost_terms, saved = results[0], results[1], results[2:]

    sums, beside = return_outer(ghost_terms, width, ghosts)
    if ring:
        part, packet = call(
            functools.partial(start_kernel, vectors),
            [(high, atoms), (high, 2 * width)],
            (own_terms, sums, beside, lists),
        )
        others = pair_exchange(packet, "gx", (1, 2, 3))
        first, level = call(
            functools.partial(merge_kernel, vectors),
            [(high, atoms), (high, 2 * width)],
            (side, part, packet, *others),
            [(high, atoms)],
        )
    else:
        first, level = call(
            functools.partial(middle_kernel, vectors),
            [(high, atoms), (high, width)],
            (own_terms, sums + return_ghosts(beside, 0, ghosts), lists),
        )
    own_terms, ghost_terms, edge_gram = call(
        functools.partial(second_kernel, ghosts, vectors),
        [(high, atoms), (high, 7 * width), (GROUP, LANES)],
        (index, first) + spread(level) + (low,) + tuple(saved),
        [(high, table_width)] + shared,
    )
    sums, beside = return_outer(ghost_terms, width, ghosts)
    if ring:
        part, packet = call(
            functools.partial(gram_start_kernel, vectors),
            [(high, atoms), (high, 2 * width + LANES)],
            (own, first, own_terms, sums, beside, lists, edge_gram),
        )
        others = pair_exchange(packet, "gx", (1, 2, 3))
        second, gram = call(
            functools.partial(gram_merge_kernel, vectors),
            [(high, atoms), (others_count, GROUP, LANES)],
            (side, part, packet, *others),
            [(high, atoms)],
        )
        gram = lax.all_to_all(gram, AXES[1:], 0, 0, tiled=True)
    else:
        second, gram = call(
            functools.partial(gram_kernel, vectors),
            [(high, atoms), (GROUP, LANES)],
            (own, first, own_terms, sums + return_ghosts(beside, 0, ghosts), lists),
        )
        gram = sum_over(gram, AXES)[None]
    following, diagonal, off = call(
        functools.partial(last_kernel, vectors, scale),
        [(1, 1, 1, 3, vectors, atoms), (2, vectors, vectors), (2, vectors, vectors)],
        (own, first, second, gram),
    )
    return following.transpose(0, 1, 2, 4, 3, 5), diagonal, off


def solution(mesh):
    return jax.shard_map(
        on_device,
        mesh=mesh,
        in_specs=(
            P("gx", "gy", "gz", None, None),
            P("gx", "gy", "gz", None),
            P("gx", "gy", "gz", None, None, None),
            P("gx", "gy", "gz", None, None),
            P("gx", "gy", "gz", None),
            P(),
            P(),
            P(),
            P(),
        ),
        out_specs=(P("gx", "gy", "gz", None, None, None), P(), P()),
        check_vma=False,
    )
```

```python
import functools
import math

import jax
import jax.numpy as jnp
import numpy as np
from jax import lax
from jax.experimental import pallas as pl
from jax.experimental.pallas import tpu as pltpu
from jax.sharding import PartitionSpec as P

SOFTEN = 0.25
CUTOFF = 4.0
HIGHEST = lax.Precision.HIGHEST
LANES = 128
GROUP = 8
AXES = ("gx", "gy", "gz")
VMEM_BYTES = 48 * 1024 * 1024


def swap_pairs(size, distance):
    return [(i, (i + distance) % size) for i in range(size)]


def octant_bit(shape, bit, ghosts):
    lane = lax.broadcasted_iota(jnp.int32, shape, 1) % (8 * ghosts)
    return (lane // ghosts // (4 >> bit)) % 2 == 1


def pair_exchange(x, axis, distances):
    size = lax.axis_size(axis)
    return [lax.ppermute(x, axis, [(i, i ^ d) for i in range(size)]) for d in distances]


def ring_sides(x, bit):
    axis = AXES[bit]
    size = lax.axis_size(axis)
    if size == 4:
        near, far = pair_exchange(x, axis, (1, 3))
        return near, far, lax.axis_index(axis) % 2 == 1
    above = lax.ppermute(x, axis, swap_pairs(size, -1))
    below = lax.ppermute(x, axis, swap_pairs(size, 1))
    return above, below, False


def fetch_ghosts(x, bit, ghosts):
    axis = AXES[bit]
    size = lax.axis_size(axis)
    if size == 1:
        return x
    if size == 2:
        return lax.ppermute(x, axis, swap_pairs(2, 1))
    near, far, odd = ring_sides(x, bit)
    return jnp.where(octant_bit(x.shape, bit, ghosts) ^ odd, far, near)


def return_ghosts(x, bit, ghosts):
    axis = AXES[bit]
    size = lax.axis_size(axis)
    if size == 1:
        return x
    if size == 2:
        return lax.ppermute(x, axis, swap_pairs(2, 1))
    near, far, odd = ring_sides(x, bit)
    return jnp.where(octant_bit(x.shape, bit, ghosts) == odd, far, near)


def spread_outer(level, ghosts):
    second = fetch_ghosts(level, 1, ghosts)
    level = jnp.concatenate([level, second], axis=1)
    return second, fetch_ghosts(level, 2, ghosts)


def return_outer(terms, width, ghosts):
    got = return_ghosts(terms[:, 3 * width :], 2, ghosts)
    inner = got[:, :width]
    first = terms[:, :width] + got[:, width : 2 * width]
    second = terms[:, width : 3 * width] + got[:, 2 * width :]
    got = return_ghosts(second, 1, ghosts)
    return inner + got[:, :width], first + got[:, width:]


def sum_over(x, axes):
    for axis in axes:
        size = lax.axis_size(axis)
        if size & (size - 1):
            x = lax.psum(x, axis)
            continue
        step = 1
        while step < size:
            x = x + lax.ppermute(x, axis, [(i, i ^ step) for i in range(size)])
            step *= 2
    return x


def sum_across(x):
    axes = AXES[1:]
    sizes = [lax.axis_size(axis) for axis in axes]
    if sizes != [4, 2]:
        return [sum_over(x, axes)]
    x = x + pair_exchange(x, axes[0], (1,))[0]
    count = sizes[0] * sizes[1]
    terms = [
        lax.ppermute(x, axes, [(i, i ^ d) for i in range(count)])
        for d in (2 * sizes[1], 1, 2 * sizes[1] + 1)
    ]
    return [x] + terms


def rows(a):
    return slice(GROUP * a, GROUP * (a + 1))


def gather_lanes(table, index_row, group):
    lane = jnp.broadcast_to(index_row % LANES, (GROUP, LANES))
    tile = jnp.broadcast_to(index_row // LANES, (GROUP, LANES))
    out = None
    for number in range(table.shape[1] // LANES):
        source = table[rows(group), number * LANES : (number + 1) * LANES]
        picked = jnp.take_along_axis(source, lane, axis=1, mode="promise_in_bounds")
        out = picked if out is None else jnp.where(tile == number, picked, out)
    return out


def column(line):
    size = line.shape[1]
    shape = (size, size)
    same = lax.broadcasted_iota(jnp.int32, shape, 0) == lax.broadcasted_iota(jnp.int32, shape, 1)
    return jnp.sum(jnp.where(same, line, 0.0), axis=1, keepdims=True)


def split_rows(y, vectors):
    high = y.astype(jnp.bfloat16).astype(jnp.float32)
    return high + pltpu.roll(y - high, vectors, 0)


def join_rows(y, vectors):
    return y + pltpu.roll(y, GROUP - vectors, 0)


def pack_kernel(pos_hbm, spec_hbm, block_hbm, raw_hbm, own_ref, oct_ref, list_ref, *scratch):
    pos_ref, spec_ref, block_ref, raw_ref, sems = scratch
    copies = [
        pltpu.make_async_copy(source, target, sems.at[n])
        for n, (source, target) in enumerate(
            (
                (pos_hbm, pos_ref),
                (spec_hbm, spec_ref),
                (block_hbm, block_ref),
                (raw_hbm, raw_ref),
            )
        )
    ]
    for copy in copies:
        copy.start()
    for copy in copies:
        copy.wait()
    vectors = block_ref.shape[4]
    atoms = pos_ref.shape[-1]
    for a in range(3):
        parts = [block_ref[0, 0, 0, a], pos_ref[a]]
        used = vectors + 1
        if a == 0:
            parts.append(spec_ref[0, 0].astype(jnp.float32))
            used += 1
        parts.append(jnp.zeros((GROUP - used, atoms), jnp.float32))
        own_ref[rows(a), :] = jnp.concatenate(parts, axis=0)
    pieces = [raw_ref[n // 4, n // 2 % 2, n % 2 : n % 2 + 1, :] for n in range(8)]
    list_ref[...] = jnp.concatenate(pieces, axis=1)
    pick_octants(own_ref, list_ref, oct_ref)


def prepare_kernel(
    atoms, ghosts, near_ref, emb_ref, rin_ref, rout_ref, read_ref, idx_ref, low_ref, in_ref, out_ref, col_ref
):
    index = table_index(near_ref[...], atoms, ghosts)
    idx_ref[...] = index
    low = lax.broadcasted_iota(jnp.int32, low_ref.shape, 0) == index % LANES
    low_ref[...] = jnp.where(low, 1.0, 0.0).astype(jnp.bfloat16)
    high, middle, rest = split_parts(rin_ref[...])
    stack = [high, middle, rest, high, middle, high]
    pad = in_ref.shape[1] - 6 * rin_ref.shape[0]
    stack = jnp.concatenate(stack + [jnp.zeros((pad, rin_ref.shape[1]), jnp.float32)], axis=0)
    in_ref[...] = jnp.transpose(stack).astype(jnp.bfloat16)
    high, rest, _ = split_parts(rout_ref[...])
    out_ref[...] = jnp.concatenate(
        [jnp.concatenate([high, high], axis=1), jnp.concatenate([rest, rest], axis=1)], axis=0
    ).astype(jnp.bfloat16)
    species = emb_ref.shape[0]
    lane = lax.broadcasted_iota(jnp.int32, col_ref.shape, 1)
    columns = jnp.broadcast_to(column(read_ref[...]), col_ref.shape)
    for n in range(species):
        columns = jnp.where(lane == n, column(emb_ref[n : n + 1, :]), columns)
    col_ref[...] = columns


def pick_octants(own_ref, list_ref, oct_ref):
    for j in range(list_ref.shape[1] // LANES):
        cut = slice(j * LANES, (j + 1) * LANES)
        for a in range(3):
            oct_ref[rows(a), cut] = gather_lanes(own_ref, list_ref[:, cut], a)


def add_octants(own, octants, lists, vectors):
    atoms = own.shape[1]
    width = lists.shape[1]
    keep = lax.broadcasted_iota(jnp.int32, octants.shape, 0) < vectors
    packed = split_rows(jnp.where(keep, octants, 0.0), vectors).astype(jnp.bfloat16)
    onehot = lax.broadcasted_iota(jnp.int32, (atoms, width), 0) == lists
    spread = lax.dot_general(
        packed,
        jnp.where(onehot, 1.0, 0.0).astype(jnp.bfloat16),
        (((1,), (1,)), ((), ())),
        preferred_element_type=jnp.float32,
    )
    return own + join_rows(spread, vectors)


def fill_table(table, own_ref, ghost_refs, vectors, ghosts, shifted):
    atoms = own_ref.shape[1]
    table[:, :atoms] = own_ref[...]
    width = 8 * ghosts
    base = atoms
    kind = 1
    for number, ref in enumerate(ghost_refs):
        for j in range(number == 0, ref.shape[1] // width):
            part = ref[:, j * width : (j + 1) * width]
            if shifted:
                row = lax.broadcasted_iota(jnp.int32, part.shape, 0)
                for a in range(3):
                    if (kind >> a) & 1:
                        move = jnp.where(octant_bit(part.shape, a, ghosts), -1.0, 1.0)
                        part = part + jnp.where(row == GROUP * a + vectors, move, 0.0)
            table[:, base : base + width] = part
            base += width
            kind += 1


def gather_slot(table, idx_ref, k, atoms):
    pieces = [[] for _ in range(3)]
    for j in range(atoms // LANES):
        index_row = idx_ref[:, pl.ds(pl.multiple_of(k * atoms + j * LANES, LANES), LANES)]
        for a in range(3):
            pieces[a].append(gather_lanes(table, index_row, a))
    return [jnp.concatenate(p, axis=1) for p in pieces]


def pair_list(fanout):
    return [(k, l) for k in range(fanout) for l in range(k, fanout)]


def lookup(table, fanout):
    where = {pair: n for n, pair in enumerate(pair_list(fanout))}
    return lambda k, l: table[where[min(k, l), max(k, l)]]


def sum_rows(parts):
    row = lax.broadcasted_iota(jnp.int32, parts[0].shape, 0)
    if len(parts) != 4 or GROUP != 8:
        out = jnp.zeros_like(parts[0])
        for n, part in enumerate(parts):
            out = jnp.where(row == n, jnp.sum(part, axis=0, keepdims=True), out)
        return out
    fold = [part + pltpu.roll(part, 4, 0) for part in parts]
    low = row < 4
    lead = jnp.where(low, fold[0], fold[1])
    rest = jnp.where(low, fold[2], fold[3])
    both = jnp.where(row % 4 < 2, lead + pltpu.roll(lead, 6, 0), rest + pltpu.roll(rest, 2, 0))
    even = both + pltpu.roll(both, 7, 0)
    odd = both + pltpu.roll(both, 1, 0)
    return jnp.where(row % 2 == 1, pltpu.roll(odd, 4, 0), even)


def dot3(x, y):
    return x[0] * y[0] + x[1] * y[1] + x[2] * y[2]


def slot_cut(k, atoms):
    return slice(k * atoms, (k + 1) * atoms)


def tile_rows(n):
    return slice(GROUP * n, GROUP * (n + 1))


def tangents(diffs, units, invs, tn, changes, vectors):
    fanout = len(diffs)
    pairs = pair_list(fanout)
    per_vector = fanout + len(pairs)
    taus = [dot3(units[k], diffs[k]) for k in range(fanout)]
    turns = [
        [(diffs[k][a] - units[k][a] * taus[k]) * invs[k] for a in range(3)] for k in range(fanout)
    ]
    values = list(taus)
    for k, l in pairs:
        half = dot3(units[k], turns[l])
        values.append(2.0 * half if k == l else half + dot3(units[l], turns[k]))
    for n, value in enumerate(values):
        changes[tile_rows(n), :] = value
        for v in range(vectors):
            tn[tile_rows(v * per_vector + n), :] = jnp.broadcast_to(
                value[v : v + 1, :], value.shape
            )


def channel_products(f, f1, q, rp, rpp, cosine, tn, acc, lanes, fanout, vectors):
    pairs = pair_list(fanout)
    per_vector = fanout + len(pairs)
    slots = range(fanout)
    rpp_q = [rpp[k] * q[k] for k in slots]
    rpp_f = [rpp[k] * f[k] for k in slots]
    for v in range(vectors):
        base = v * per_vector

        def tangent(n):
            return tn[tile_rows(base + n), lanes]

        phi = [f1[k] * tangent(k) for k in slots]
        index = {pair: fanout + n for n, pair in enumerate(pairs)}
        dq = []
        for k in slots:
            total = None
            for l in slots:
                term = phi[l] * cosine(k, l) + f[l] * tangent(index[min(k, l), max(k, l)])
                total = term if total is None else total + term
            dq.append(total)
        y = [phi[k] * rpp_q[k] + dq[k] * rpp_f[k] for k in slots]
        w = [y[k] * f[k] + rp[k] * phi[k] for k in slots]
        for k in slots:
            total = y[k] * q[k] + rp[k] * dq[k]
            for l in slots:
                total = total + w[l] * cosine(k, l)
            acc[tile_rows(base + k), lanes] += f1[k] * total
        for n, (k, l) in enumerate(pairs):
            term = w[k] * f[l] if k == l else w[k] * f[l] + w[l] * f[k]
            acc[tile_rows(base + fanout + n), lanes] += term


def finish_product(
    idx_ref, low_ref, unit_ref, inv_ref, sums_ref, acc, changes, diffs, own_out, ghost_out, vectors
):
    atoms = own_out.shape[1]
    fanout = idx_ref.shape[1] // atoms
    tiles = (atoms + ghost_out.shape[1]) // LANES
    pairs = pair_list(fanout)
    per_vector = fanout + len(pairs)
    slots = range(fanout)
    row = lax.broadcasted_iota(jnp.int32, (GROUP, atoms), 0)
    outs = [
        sum_rows([acc[tile_rows(v * per_vector + n), :] for v in range(vectors)])
        for n in range(per_vector)
    ]
    taus = [changes[tile_rows(k), :] for k in slots]
    turned = lookup([changes[tile_rows(fanout + n), :] for n in range(len(pairs))], fanout)
    bent = lookup(outs[fanout:], fanout)
    units = [[unit_ref[rows(a), slot_cut(k, atoms)] for a in range(3)] for k in slots]
    invs = [inv_ref[:, slot_cut(k, atoms)] for k in slots]
    turns = [
        [(diffs[k][a] - units[k][a] * taus[k]) * invs[k] for a in range(3)] for k in slots
    ]

    def base_sum(n):
        line = (n // 4) * GROUP + n % 4
        return sums_ref[line : line + 1, :]

    stretch = [base_sum(k) for k in slots]
    curve = [base_sum(fanout + k) for k in slots]
    weight = lookup([base_sum(2 * fanout + n) for n in range(len(pairs))], fanout)
    mixed = [[base_sum(2 * fanout + len(pairs) + k * fanout + l) for l in slots] for k in slots]
    center = [jnp.zeros((GROUP, atoms), jnp.float32) for _ in range(3)]
    shifted = [jnp.zeros((GROUP, atoms), jnp.float32) for _ in range(vectors)]
    left = []
    for k in slots:
        along = outs[k] + curve[k] * taus[k]
        force = [0.0, 0.0, 0.0]
        change = [0.0, 0.0, 0.0]
        for l in slots:
            along = along + turned(k, l) * mixed[k][l]
            bend = bent(k, l) + taus[l] * mixed[l][k] + taus[k] * mixed[k][l]
            pull = weight(k, l)
            if k == l:
                bend = bend + bent(k, l)
                pull = pull + pull
            for a in range(3):
                force[a] = force[a] + pull * units[l][a]
                change[a] = change[a] + bend * units[l][a] + pull * turns[l][a]
        flat = dot3(units[k], force)
        inv = invs[k]
        along = (
            along
            - (dot3(units[k], change) + dot3(turns[k], force)) * inv
            + taus[k] * flat * (inv * inv)
        )
        keep = stretch[k] - flat * inv
        packed = []
        for a in range(3):
            y = (
                along * units[k][a]
                + keep * turns[k][a]
                + (change[a] - taus[k] * inv * force[a]) * inv
            )
            y = jnp.where(row < vectors, y, 0.0)
            center[a] = center[a] - y
            for n in range(vectors):
                other = y if n == 0 else pltpu.roll(y, n, 0)
                if n:
                    other = other + pltpu.roll(y, GROUP - vectors + n, 0)
                shifted[n] = shifted[n] + other * diffs[k][a]
            packed.append(split_rows(y, vectors))
        packed = jnp.concatenate(packed, axis=0)
        tile = idx_ref[:, slot_cut(k, atoms)] // LANES
        left.append(
            jnp.concatenate(
                [jnp.where(tile == number, packed, 0.0) for number in range(tiles)], axis=0
            ).astype(jnp.bfloat16)
        )
    spread = lax.dot_general(
        jnp.concatenate(left, axis=1),
        low_ref[...],
        (((1,), (1,)), ((), ())),
        preferred_element_type=jnp.float32,
    )
    own_tiles = atoms // LANES
    for number in range(tiles):
        for a in range(3):
            value = join_rows(spread[tile_rows(number * 3 + a)], vectors)
            if number < own_tiles:
                cut = slice(number * LANES, (number + 1) * LANES)
                own_out[rows(a), cut] = value + center[a][:, cut]
            else:
                cut = number - own_tiles
                ghost_out[rows(a), cut * LANES : (cut + 1) * LANES] = value
    return shifted


def split_parts(x):
    high = x.astype(jnp.bfloat16).astype(jnp.float32)
    rest = x - high
    middle = rest.astype(jnp.bfloat16).astype(jnp.float32)
    low = (rest - middle).astype(jnp.bfloat16).astype(jnp.float32)
    return high, middle, low


def silu_slopes(x):
    sig = 0.5 + 0.5 * jnp.tanh(0.5 * x)
    anti = 1.0 - sig
    return sig, sig * (1.0 + x * anti), sig * anti * (2.0 + x * (anti - sig))


def half_turns(dist, inv, basis):
    shape = (basis, dist.shape[1])
    order = (lax.broadcasted_iota(jnp.int32, shape, 0) + 1).astype(jnp.float32)
    turns = order * (dist * (1.0 / CUTOFF))
    whole = jnp.floor(turns + 0.5)
    sign = 1.0 - 2.0 * (whole - 2.0 * jnp.floor(whole * 0.5))
    x = (turns - whole) * np.float32(np.pi)
    x2 = x * x

    def series(terms):
        value = terms[-1]
        for term in terms[-2::-1]:
            value = term + x2 * value
        return value

    sine = sign * x * series([(-1.0) ** n / math.factorial(2 * n + 1) for n in range(6)])
    cosine = sign * series([(-1.0) ** n / math.factorial(2 * n) for n in range(7)])
    omega = order * np.float32(np.pi / CUTOFF)
    b0 = sine * inv
    b1 = (omega * cosine - b0) * inv
    b2 = -(omega * omega * sine + 2.0 * b1) * inv
    return jnp.concatenate([b0, b1, b2], axis=1)


def first_kernel(
    ghosts,
    vectors,
    basis,
    species,
    idx_ref,
    own_ref,
    g1_ref,
    g2_ref,
    g3_ref,
    low_ref,
    in_ref,
    out_ref,
    col_ref,
    own_out,
    ghost_out,
    unit_ref,
    inv_ref,
    sums_ref,
    cos_ref,
    f_ref,
    f1_ref,
    q_ref,
    rp_ref,
    rpp_ref,
    table,
    f2_ref,
    read_col,
    tn,
    changes,
    acc,
    acc2,
):
    atoms = own_ref.shape[1]
    fanout = idx_ref.shape[1] // atoms
    channels = col_ref.shape[0]
    pairs = pair_list(fanout)
    slots = range(fanout)
    embeds = [col_ref[:, n : n + 1] for n in range(species)]
    read_col[...] = jnp.broadcast_to(col_ref[:, species : species + 1], read_col.shape)
    fill_table(table, own_ref, (g1_ref, g2_ref, g3_ref), vectors, ghosts, True)

    def embed(kind):
        value = embeds[0]
        for n in range(1, species):
            value = jnp.where(kind == float(n), embeds[n], value)
        return value

    own_embed = embed(own_ref[vectors + 1 : vectors + 2, :])
    inward = in_ref[:, : 6 * basis]
    outward = out_ref[...]
    diffs, units, invs = [], [], []
    for k in slots:
        cut = slot_cut(k, atoms)
        near = gather_slot(table, idx_ref, k, atoms)
        diff = [near[a] - own_ref[rows(a), :] for a in range(3)]
        delta = [
            jnp.broadcast_to(diff[a][vectors : vectors + 1, :], (GROUP, atoms)) for a in range(3)
        ]
        dist = jnp.sqrt(dot3(delta, delta) + SOFTEN)
        inv = 1.0 / dist
        unit = [delta[a] * inv for a in range(3)]
        for a in range(3):
            unit_ref[rows(a), cut] = unit[a]
        inv_ref[:, cut] = inv
        diffs.append(diff)
        units.append(unit)
        invs.append(inv)
        one = dist[0:1]
        radii = half_turns(one, inv[0:1], basis)
        high, middle, rest = split_parts(radii)
        z = jnp.dot(
            inward,
            jnp.concatenate([high, high, high, middle, middle, rest], axis=0).astype(jnp.bfloat16),
            preferred_element_type=jnp.float32,
        )
        z0, z1, z2 = z[:, :atoms], z[:, atoms : 2 * atoms], z[:, 2 * atoms :]
        sig, slope, curve = silu_slopes(z0)
        hidden = jnp.concatenate([z0 * sig, slope * z1, curve * z1 * z1 + slope * z2], axis=1)
        high = hidden.astype(jnp.bfloat16)
        rest = (hidden - high.astype(jnp.float32)).astype(jnp.bfloat16)
        radial = jnp.dot(
            outward, jnp.concatenate([high, rest], axis=0), preferred_element_type=jnp.float32
        )
        radial = radial[:channels] + radial[channels:]
        r0, r1, r2 = radial[:, :atoms], radial[:, atoms : 2 * atoms], radial[:, 2 * atoms :]
        square = one * one
        base = 1.0 - square * (1.0 / CUTOFF**2)
        v0 = base * base
        v1 = base * one * (-4.0 / CUTOFF**2)
        v2 = -4.0 / CUTOFF**2 + square * (12.0 / CUTOFF**4)
        pair = own_embed * embed(near[0][vectors + 1 : vectors + 2, :])
        f_ref[:, cut] = pair * (r0 * v0)
        f1_ref[:, cut] = pair * (r1 * v0 + r0 * v1)
        f2_ref[:, cut] = pair * (r2 * v0 + 2.0 * (r1 * v1) + r0 * v2)
    for n, (k, l) in enumerate(pairs):
        cos_ref[tile_rows(n), :] = 1.0 + dot3(units[k], units[l])
    tangents(diffs, units, invs, tn, changes, vectors)
    acc[...] = jnp.zeros_like(acc)
    acc2[...] = jnp.zeros_like(acc2)
    share = 1.0 / fanout

    def tile(number, carry):
        here = pl.ds(pl.multiple_of(number * GROUP, GROUP), GROUP)
        for half in range(atoms // LANES):
            lanes = slice(half * LANES, (half + 1) * LANES)
            cuts = [slice(k * atoms + half * LANES, k * atoms + (half + 1) * LANES) for k in slots]
            cosine = lookup([cos_ref[tile_rows(n), lanes] for n in range(len(pairs))], fanout)
            f = [f_ref[here, cut] for cut in cuts]
            f1 = [f1_ref[here, cut] for cut in cuts]
            read = read_col[here, :] * share
            q, rp, rpp = [], [], []
            for k in slots:
                project = sum(f[l] * cosine(k, l) for l in slots)
                _, slope, curve = silu_slopes(f[k] * project * share)
                q.append(project)
                rp.append(read * slope)
                rpp.append(read * share * curve)
                q_ref[here, cuts[k]] = q[k]
                rp_ref[here, cuts[k]] = rp[k]
                rpp_ref[here, cuts[k]] = rpp[k]
            m = [rp[k] * f[k] for k in slots]
            slope = [rp[k] * q[k] + sum(m[l] * cosine(k, l) for l in slots) for k in slots]
            terms = [slope[k] * f1[k] for k in slots]
            terms += [slope[k] * f2_ref[here, cuts[k]] for k in slots]
            terms += [m[k] * f[l] if k == l else m[k] * f[l] + m[l] * f[k] for k, l in pairs]
            terms += [f1[k] * m[l] for k in slots for l in slots]
            for n, term in enumerate(terms):
                acc2[tile_rows(n), lanes] += term
            channel_products(f, f1, q, rp, rpp, cosine, tn, acc, lanes, fanout, vectors)
        return carry

    lax.fori_loop(0, channels // GROUP, tile, 0)
    count = acc2.shape[0] // GROUP
    for n in range(0, count, 4):
        parts = [acc2[tile_rows(min(n + j, count - 1)), :] for j in range(4)]
        sums_ref[tile_rows(n // 4), :] = sum_rows(parts)
    finish_product(
        idx_ref,
        low_ref,
        unit_ref,
        inv_ref,
        sums_ref,
        acc,
        changes,
        diffs,
        own_out,
        ghost_out,
        vectors,
    )


def second_kernel(
    ghosts,
    vectors,
    idx_ref,
    own_ref,
    g1_ref,
    g2_ref,
    g3_ref,
    low_ref,
    unit_ref,
    inv_ref,
    sums_ref,
    cos_ref,
    f_ref,
    f1_ref,
    q_ref,
    rp_ref,
    rpp_ref,
    own_out,
    ghost_out,
    gram_out,
    table,
    tn,
    changes,
    acc,
):
    atoms = own_ref.shape[1]
    fanout = idx_ref.shape[1] // atoms
    channels = f_ref.shape[0]
    pairs = pair_list(fanout)
    slots = range(fanout)
    fill_table(table, own_ref, (g1_ref, g2_ref, g3_ref), vectors, ghosts, False)
    diffs = []
    for k in slots:
        near = gather_slot(table, idx_ref, k, atoms)
        diffs.append([near[a] - own_ref[rows(a), :] for a in range(3)])
    units = [[unit_ref[rows(a), slot_cut(k, atoms)] for a in range(3)] for k in slots]
    invs = [inv_ref[:, slot_cut(k, atoms)] for k in slots]
    tangents(diffs, units, invs, tn, changes, vectors)
    acc[...] = jnp.zeros_like(acc)

    def tile(number, carry):
        here = pl.ds(pl.multiple_of(number * GROUP, GROUP), GROUP)
        for half in range(atoms // LANES):
            lanes = slice(half * LANES, (half + 1) * LANES)
            cuts = [slice(k * atoms + half * LANES, k * atoms + (half + 1) * LANES) for k in slots]
            cosine = lookup([cos_ref[tile_rows(n), lanes] for n in range(len(pairs))], fanout)
            parts = [
                [ref[here, cut] for cut in cuts] for ref in (f_ref, f1_ref, q_ref, rp_ref, rpp_ref)
            ]
            channel_products(*parts, cosine, tn, acc, lanes, fanout, vectors)
        return carry

    lax.fori_loop(0, channels // GROUP, tile, 0)
    shifted = finish_product(
        idx_ref,
        low_ref,
        unit_ref,
        inv_ref,
        sums_ref,
        acc,
        changes,
        diffs,
        own_out,
        ghost_out,
        vectors,
    )
    gram_out[...] = from_shifted(shifted, vectors)


def middle_kernel(vectors, own_ref, sums_ref, list_ref, full_ref, oct_ref):
    for a in range(3):
        full_ref[rows(a), :] = add_octants(
            own_ref[rows(a), :], sums_ref[rows(a), :], list_ref[...], vectors
        )
    pick_octants(full_ref, list_ref, oct_ref)


def inner(x, y, pad_to=LANES):
    pad = jnp.zeros((pad_to - y.shape[0], y.shape[1]), jnp.float32)
    return lax.dot_general(
        x,
        jnp.concatenate([y, pad], axis=0),
        (((1,), (1,)), ((), ())),
        precision=HIGHEST,
        preferred_element_type=jnp.float32,
    )


def only_vectors(x, vectors):
    row = lax.broadcasted_iota(jnp.int32, x.shape, 0)
    return jnp.where(row % GROUP < vectors, x, 0.0)


def pack_gram(total, edge):
    lane = lax.broadcasted_iota(jnp.int32, (GROUP, LANES), 1)
    out = total[rows(0)]
    out = jnp.where(lane >= 2 * GROUP, pltpu.roll(total[rows(1)], GROUP, 1), out)
    if edge is not None:
        out = jnp.where(lane >= 3 * GROUP, pltpu.roll(edge, 3 * GROUP, 1), out)
    return jnp.where(lane >= 4 * GROUP, pltpu.roll(total[rows(2)], 2 * GROUP, 1), out)


def gram_kernel(vectors, start_ref, first_ref, own_ref, sums_ref, list_ref, full_ref, gram_ref):
    total = jnp.zeros((3 * GROUP, LANES), jnp.float32)
    for a in range(3):
        second = add_octants(own_ref[rows(a), :], sums_ref[rows(a), :], list_ref[...], vectors)
        full_ref[rows(a), :] = second
        stack = jnp.concatenate([start_ref[rows(a), :], first_ref[rows(a), :], second], axis=0)
        stack = only_vectors(stack, vectors)
        total += inner(stack, stack)
    gram_ref[...] = pack_gram(total, None)


def packet_start(vectors, own_ref, sums_ref, ghost_ref, list_ref, part_ref, packet_ref):
    width = list_ref.shape[1]
    for a in range(3):
        part_ref[rows(a), :] = add_octants(
            own_ref[rows(a), :], sums_ref[rows(a), :], list_ref[...], vectors
        )
    mark = vectors + 1
    for j in range(width // LANES):
        cut = slice(j * LANES, (j + 1) * LANES)
        for a in range(3):
            value = gather_lanes(part_ref, list_ref[:, cut], a)
            if a == 0:
                row = lax.broadcasted_iota(jnp.int32, value.shape, 0)
                value = jnp.where(row == mark, list_ref[:, cut].astype(jnp.float32), value)
            packet_ref[rows(a), cut] = value
    packet_ref[:, width : 2 * width] = ghost_ref[...]


def arriving(side, packets, n, a, width):
    cut = slice(width, 2 * width)
    after, before = packets[(n + 1) % 4], packets[(n + 3) % 4]
    return jnp.where(side > 0.5, after[rows(a), cut], before[rows(a), cut])


def packet_lists(packet, vectors, width):
    mark = vectors + 1
    return packet[mark : mark + 1, :width].astype(jnp.int32)


def start_kernel(vectors, own_ref, sums_ref, ghost_ref, list_ref, part_ref, packet_ref):
    packet_start(vectors, own_ref, sums_ref, ghost_ref, list_ref, part_ref, packet_ref)


def merge_kernel(
    vectors, side_ref, part_ref, p0_ref, p1_ref, p2_ref, p3_ref, full_ref, level_ref, spread
):
    width = p0_ref.shape[1] // 2
    side = side_ref[...]
    packets = (p0_ref, p1_ref, p2_ref, p3_ref)
    lists = [packet_lists(p, vectors, width) for p in packets]
    for a in range(3):
        full_ref[rows(a), :] = add_octants(
            part_ref[rows(a), :], arriving(side, packets, 0, a, width), lists[0], vectors
        )
    near = []
    for n in (1, 3):
        for a in range(3):
            zero = jnp.zeros((GROUP, part_ref.shape[1]), jnp.float32)
            spread[rows(a), :] = add_octants(
                zero, arriving(side, packets, n, a, width), lists[n], vectors
            )
        values = []
        for a in range(3):
            pieces = [
                gather_lanes(spread, lists[n][:, j * LANES : (j + 1) * LANES], a)
                for j in range(width // LANES)
            ]
            values.append(packets[n][rows(a), :width] + jnp.concatenate(pieces, axis=1))
        near.append(values)
    for a in range(3):
        for j in range(width // LANES):
            cut = slice(j * LANES, (j + 1) * LANES)
            level_ref[rows(a), cut] = gather_lanes(full_ref, lists[0][:, cut], a)
        level_ref[rows(a), width : 2 * width] = jnp.where(side > 0.5, near[1][a], near[0][a])


def gram_start_kernel(
    vectors,
    start_ref,
    first_ref,
    own_ref,
    sums_ref,
    ghost_ref,
    list_ref,
    edge_ref,
    part_ref,
    packet_ref,
):
    packet_start(vectors, own_ref, sums_ref, ghost_ref, list_ref, part_ref, packet_ref)
    width = list_ref.shape[1]
    total = jnp.zeros((3 * GROUP, LANES), jnp.float32)
    for a in range(3):
        stack = jnp.concatenate(
            [start_ref[rows(a), :], first_ref[rows(a), :], part_ref[rows(a), :]], axis=0
        )
        stack = only_vectors(stack, vectors)
        total += inner(stack, stack)
    cut = slice(2 * width, 2 * width + LANES)
    packet_ref[rows(0), cut] = pack_gram(total, edge_ref[...])
    packet_ref[GROUP : 3 * GROUP, cut] = jnp.zeros((2 * GROUP, LANES), jnp.float32)


def shifted_products(x, y, vectors):
    return [x * (pltpu.roll(y, n, 0) if n else y) for n in range(vectors)]


def from_shifted(shifted, vectors):
    shape = (GROUP, LANES)
    row = lax.broadcasted_iota(jnp.int32, shape, 0)
    lane = lax.broadcasted_iota(jnp.int32, shape, 1)
    total = jnp.zeros(shape, jnp.float32)
    for n in range(vectors):
        value = jnp.sum(shifted[n], axis=1, keepdims=True)
        total = jnp.where(lane == (row + vectors - n) % vectors, value, total)
    return jnp.where((row < vectors) & (lane < vectors), total, 0.0)


def gram_merge_kernel(
    vectors, side_ref, p3_ref, p2_ref, part_ref, p0_ref, p1_ref, full_ref, gram_ref, spread
):
    width = (p0_ref.shape[1] - LANES) // 2
    atoms = part_ref.shape[1]
    side = side_ref[...]
    packets = (p0_ref, p1_ref, p2_ref, p3_ref)
    shares = []
    for n in range(4):
        lists = packet_lists(packets[n], vectors, width)
        terms = [only_vectors(arriving(side, packets, n, a, width), vectors) for a in range(3)]
        packed = jnp.concatenate([split_rows(t, vectors) for t in terms], axis=0)
        onehot = lax.broadcasted_iota(jnp.int32, (atoms, width), 0) == lists
        placed = lax.dot_general(
            packed.astype(jnp.bfloat16),
            jnp.where(onehot, 1.0, 0.0).astype(jnp.bfloat16),
            (((1,), (1,)), ((), ())),
            preferred_element_type=jnp.float32,
        )
        total = None
        for a in range(3):
            value = join_rows(placed[rows(a)], vectors)
            spread[rows(a), :] = value
            if n == 0:
                full_ref[rows(a), :] = part_ref[rows(a), :] + value
            at = only_vectors(packets[n][rows(a), :width], vectors)
            at = at + pltpu.roll(at, vectors, 0)
            back = jnp.concatenate(
                [
                    gather_lanes(spread, lists[:, j * LANES : (j + 1) * LANES], a)
                    for j in range(width // LANES)
                ],
                axis=1,
            )
            found = shifted_products(terms[a], at + at + back, vectors)
            total = found if total is None else [x + y for x, y in zip(total, found)]
        shares.append([packets[n][rows(0), 2 * width : 2 * width + LANES]] + total)

    def add(x, y):
        return [p + q for p, q in zip(x, y)]

    total = add(add(shares[0], shares[1]), add(shares[2], shares[3]))
    gram_ref[...] = total[0] + pltpu.roll(from_shifted(total[1:], vectors), 4 * GROUP, 1)


def last_kernel(vectors, scale, start_ref, first_ref, second_ref, *refs):
    gram_refs, refs = refs[:-7], refs[-7:]
    next_hbm, diag_hbm, off_hbm, next_ref, diag_ref, off_ref, sems = refs
    shape = (GROUP, LANES)
    row = lax.broadcasted_iota(jnp.int32, shape, 0)
    lane = lax.broadcasted_iota(jnp.int32, shape, 1)
    inside = (row < vectors) & (lane < vectors)
    eye = jnp.where((row == lane) & inside, 1.0, 0.0)
    levels = [ref[...] for ref in gram_refs]
    while len(levels) > 1:
        levels = [sum(levels[n : n + 2]) for n in range(0, len(levels), 2)]
    gram = levels[0] * scale

    def block(x, n):
        return jnp.where(inside, pltpu.roll(x, LANES - GROUP * n, 1) if n else x, 0.0)

    def beside(*parts):
        out = parts[0]
        for n, part in enumerate(parts[1:]):
            out = out + pltpu.roll(part, GROUP * (n + 1), 1)
        return out

    def mul(x, y):
        return sum(x[:, k : k + 1] * y[k : k + 1, :] for k in range(vectors))

    def flip(x):
        out = jnp.zeros(shape, jnp.float32)
        for k in range(vectors):
            line = jnp.sum(eye * x[:, k : k + 1], axis=0, keepdims=True)
            out = jnp.where(row == k, line, out)
        return out

    def solve(m):
        for j in range(vectors):
            inverse = lax.rsqrt(m[j : j + 1, j : j + 1])
            line = m[j : j + 1, :] * inverse
            m = jnp.where(
                row == j, line, jnp.where(row > j, m - (m[:, j : j + 1] * inverse) * line, m)
            )
        return jnp.where((lane >= row) & inside, m, 0.0), m

    ss, su, uu, uq, qq = (block(gram, n) for n in range(5))
    qq = 0.5 * (qq + flip(qq))
    _, m = solve(beside(ss, su, uu, eye))
    p0 = block(m, 3)
    p0t = flip(p0)
    a1 = mul(block(m, 1), p0t)
    up1, m = solve(beside(mul(block(m, 2), p0t) - mul(a1, a1), p0, mul(a1, p0)))
    b, a = block(m, 1), -block(m, 2)
    at, bt = flip(a), flip(b)
    known = mul(up1, beside(flip(up1), p0))
    right_s = mul(su, at) + mul(uu, bt)
    right_u = mul(uu, at) + mul(uq, bt)
    right_q = mul(uq, at) + mul(qq, bt)
    a2 = mul(a, right_s) + mul(b, right_u)
    ww = mul(a, right_u) + mul(b, right_q)
    moved = mul(a2, beside(a2, a, b)) + known
    up2, m = solve(
        beside(ww - block(moved, 0), -block(moved, 1), a - block(moved, 2), b)
    )
    small = (slice(0, vectors), slice(0, vectors))
    diag_ref[0] = a1[small]
    diag_ref[1] = a2[small]
    off_ref[0] = up1[small]
    off_ref[1] = up2[small]
    copies = [
        pltpu.make_async_copy(diag_ref, diag_hbm, sems.at[0]),
        pltpu.make_async_copy(off_ref, off_hbm, sems.at[1]),
    ]
    for copy in copies:
        copy.start()
    for comp in range(3):
        value = None
        for n, ref in enumerate((start_ref, first_ref, second_ref)):
            for w in range(vectors):
                line = GROUP * comp + w
                place = GROUP * (n + 1) + w
                term = m[:, place : place + 1] * ref[line : line + 1, :]
                value = term if value is None else value + term
        next_ref[0, 0, 0, comp] = value[:vectors]
    copies.append(pltpu.make_async_copy(next_ref, next_hbm, sems.at[2]))
    copies[-1].start()
    for copy in copies:
        copy.wait()


def call(body, outs, args, scratch=(), flops=0, spaces=pltpu.VMEM, out_spaces=pltpu.VMEM):
    outs = [shape if isinstance(shape[0], tuple) else (shape, jnp.float32) for shape in outs]
    return pl.pallas_call(
        body,
        out_shape=[jax.ShapeDtypeStruct(shape, kind) for shape, kind in outs],
        in_specs=[pl.BlockSpec(memory_space=spaces)] * len(args),
        out_specs=[pl.BlockSpec(memory_space=out_spaces)] * len(outs),
        scratch_shapes=[
            pltpu.VMEM(shape, jnp.float32) if isinstance(shape, tuple) else shape
            for shape in scratch
        ],
        cost_estimate=pl.CostEstimate(flops=flops, bytes_accessed=0, transcendentals=0)
        if flops
        else None,
        compiler_params=pltpu.CompilerParams(vmem_limit_bytes=VMEM_BYTES),
    )(*args)


def table_index(neighbors, atoms, ghosts):
    entry = neighbors - atoms
    cell = entry // ghosts
    number = cell
    kept = [n for n in range(64) if not all(m in (1, 2) for m in (n // 16, n // 4 % 4, n % 4))]
    previous = -1
    for position, n in enumerate(kept):
        if n - previous > 1:
            number = number + jnp.where(cell >= position, n - previous - 1, 0)
        previous = n
    member = (number // 16, number // 4 % 4, number % 4)
    kind = 0
    octant = 0
    for bit, m in enumerate(member):
        kind = kind + jnp.where((m == 0) | (m == 3), 1 << bit, 0)
        octant = 2 * octant + (m + 1) % 2
    place = atoms + (kind - 1) * (8 * ghosts) + octant * ghosts + entry % ghosts
    return jnp.where(neighbors < atoms, neighbors, place)


def on_device(
    positions,
    species,
    start_block,
    neighbors,
    ghost_lists,
    embedding,
    radial_in,
    radial_out,
    readout,
):
    atoms = positions.shape[-1]
    ghosts = ghost_lists.shape[-1]
    vectors = start_block.shape[3]
    fanout = neighbors.shape[3]
    channels = embedding.shape[1]
    devices = lax.axis_size("gx") * lax.axis_size("gy") * lax.axis_size("gz")
    scale = 1.0 / (3.0 * atoms * devices)
    width = 8 * ghosts
    high = 3 * GROUP
    edges = fanout * atoms
    table_width = atoms + 7 * width
    ring = lax.axis_size("gx") == 4
    side = (octant_bit((GROUP, width), 0, ghosts) ^ (lax.axis_index("gx") % 2 == 1)).astype(
        jnp.float32
    )

    inputs = (
        positions.transpose(0, 1, 3, 2, 4).reshape(3, 1, atoms),
        species,
        start_block.transpose(0, 1, 2, 4, 3, 5),
        ghost_lists,
    )
    own, octants, lists = call(
        pack_kernel,
        [(high, atoms), (high, width), ((1, width), jnp.int32)],
        inputs,
        [pltpu.VMEM(x.shape, x.dtype) for x in inputs]
        + [pltpu.SemaphoreType.DMA((len(inputs),))],
        spaces=pltpu.HBM,
    )
    basis, hidden = radial_in.shape
    index, low, inward, outward, columns = call(
        functools.partial(prepare_kernel, atoms, ghosts),
        [
            ((1, edges), jnp.int32),
            ((LANES, edges), jnp.bfloat16),
            ((hidden, LANES * (-(-6 * basis // LANES))), jnp.bfloat16),
            ((2 * channels, 2 * hidden), jnp.bfloat16),
            (channels, LANES),
        ],
        (neighbors.reshape(1, -1), embedding, radial_in, radial_out.T, readout.reshape(1, -1)),
        flops=2_000_000,
    )

    def spread(level):
        if level.shape[1] == width:
            level = jnp.concatenate([level, fetch_ghosts(level, 0, ghosts)], axis=1)
        return (level,) + spread_outer(level, ghosts)

    pairs = len(pair_list(fanout))
    shared = [
        (vectors * (fanout + pairs) * GROUP, atoms),
        ((fanout + pairs) * GROUP, atoms),
        (vectors * (fanout + pairs) * GROUP, atoms),
    ]
    base_sums = 2 * fanout + pairs + fanout * fanout
    saved_shapes = [
        (high, edges),
        (GROUP, edges),
        (GROUP * (-(-base_sums // 4)), atoms),
        (pairs * GROUP, atoms),
    ] + [(channels, edges)] * 5
    results = call(
        functools.partial(first_kernel, ghosts, vectors, basis, embedding.shape[0]),
        [(high, atoms), (high, 7 * width)] + saved_shapes,
        (index, own)
        + spread(octants)
        + (low, inward, outward, columns),
        [(high, table_width), (channels, edges), (channels, LANES)]
        + shared
        + [(base_sums * GROUP, atoms)],
    )
    own_terms, ghost_terms, saved = results[0], results[1], results[2:]

    sums, beside = return_outer(ghost_terms, width, ghosts)
    if ring:
        part, packet = call(
            functools.partial(start_kernel, vectors),
            [(high, atoms), (high, 2 * width)],
            (own_terms, sums, beside, lists),
        )
        others = pair_exchange(packet, "gx", (1, 2, 3))
        first, level = call(
            functools.partial(merge_kernel, vectors),
            [(high, atoms), (high, 2 * width)],
            (side, part, packet, *others),
            [(high, atoms)],
        )
    else:
        first, level = call(
            functools.partial(middle_kernel, vectors),
            [(high, atoms), (high, width)],
            (own_terms, sums + return_ghosts(beside, 0, ghosts), lists),
        )
    own_terms, ghost_terms, edge_gram = call(
        functools.partial(second_kernel, ghosts, vectors),
        [(high, atoms), (high, 7 * width), (GROUP, LANES)],
        (index, first) + spread(level) + (low,) + tuple(saved),
        [(high, table_width)] + shared,
    )
    sums, beside = return_outer(ghost_terms, width, ghosts)
    if ring:
        part, packet = call(
            functools.partial(gram_start_kernel, vectors),
            [(high, atoms), (high, 2 * width + LANES)],
            (own, first, own_terms, sums, beside, lists, edge_gram),
        )
        others = pair_exchange(packet, "gx", (1, 2, 3))
        second, gram = call(
            functools.partial(gram_merge_kernel, vectors),
            [(high, atoms), (GROUP, LANES)],
            (side, *others[:0:-1], part, packet, others[0]),
            [(high, atoms)],
        )
        gram = sum_across(gram)
    else:
        second, gram = call(
            functools.partial(gram_kernel, vectors),
            [(high, atoms), (GROUP, LANES)],
            (own, first, own_terms, sums + return_ghosts(beside, 0, ghosts), lists),
        )
        gram = [sum_over(gram, AXES)]
    shapes = [(1, 1, 1, 3, vectors, atoms), (2, vectors, vectors), (2, vectors, vectors)]
    following, diagonal, off = call(
        functools.partial(last_kernel, vectors, scale),
        shapes,
        (own, first, second, *gram),
        shapes + [pltpu.SemaphoreType.DMA((len(shapes),))],
        out_spaces=pltpu.HBM,
    )
    return following.transpose(0, 1, 2, 4, 3, 5), diagonal, off


def solution(mesh):
    return jax.shard_map(
        on_device,
        mesh=mesh,
        in_specs=(
            P("gx", "gy", "gz", None, None),
            P("gx", "gy", "gz", None),
            P("gx", "gy", "gz", None, None, None),
            P("gx", "gy", "gz", None, None),
            P("gx", "gy", "gz", None),
            P(),
            P(),
            P(),
            P(),
        ),
        out_specs=(P("gx", "gy", "gz", None, None, None), P(), P()),
        check_vma=False,
    )
```

```python
import functools
import math

import jax
import jax.numpy as jnp
import numpy as np
from jax import lax
from jax.experimental import pallas as pl
from jax.experimental.pallas import tpu as pltpu
from jax.sharding import PartitionSpec as P

SOFTEN = 0.25
CUTOFF = 4.0
HIGHEST = lax.Precision.HIGHEST
LANES = 128
GROUP = 8
AXES = ("gx", "gy", "gz")
VMEM_BYTES = 48 * 1024 * 1024


def swap_pairs(size, distance):
    return [(i, (i + distance) % size) for i in range(size)]


def octant_bit(shape, bit, ghosts):
    lane = lax.broadcasted_iota(jnp.int32, shape, 1) % (8 * ghosts)
    return (lane // ghosts // (4 >> bit)) % 2 == 1


def pair_exchange(x, axis, distances):
    size = lax.axis_size(axis)
    return [lax.ppermute(x, axis, [(i, i ^ d) for i in range(size)]) for d in distances]


def ring_sides(x, bit):
    axis = AXES[bit]
    size = lax.axis_size(axis)
    if size == 4:
        near, far = pair_exchange(x, axis, (1, 3))
        return near, far, lax.axis_index(axis) % 2 == 1
    above = lax.ppermute(x, axis, swap_pairs(size, -1))
    below = lax.ppermute(x, axis, swap_pairs(size, 1))
    return above, below, False


def fetch_ghosts(x, bit, ghosts):
    axis = AXES[bit]
    size = lax.axis_size(axis)
    if size == 1:
        return x
    if size == 2:
        return lax.ppermute(x, axis, swap_pairs(2, 1))
    near, far, odd = ring_sides(x, bit)
    return jnp.where(octant_bit(x.shape, bit, ghosts) ^ odd, far, near)


def return_ghosts(x, bit, ghosts):
    axis = AXES[bit]
    size = lax.axis_size(axis)
    if size == 1:
        return x
    if size == 2:
        return lax.ppermute(x, axis, swap_pairs(2, 1))
    near, far, odd = ring_sides(x, bit)
    return jnp.where(octant_bit(x.shape, bit, ghosts) == odd, far, near)


def spread_outer(level, ghosts):
    second = fetch_ghosts(level, 1, ghosts)
    level = jnp.concatenate([level, second], axis=1)
    return second, fetch_ghosts(level, 2, ghosts)


def return_outer(terms, width, ghosts):
    got = return_ghosts(terms[:, 3 * width :], 2, ghosts)
    inner = got[:, :width]
    first = terms[:, :width] + got[:, width : 2 * width]
    second = terms[:, width : 3 * width] + got[:, 2 * width :]
    got = return_ghosts(second, 1, ghosts)
    return inner + got[:, :width], first + got[:, width:]


def sum_over(x, axes):
    for axis in axes:
        size = lax.axis_size(axis)
        if size & (size - 1):
            x = lax.psum(x, axis)
            continue
        step = 1
        while step < size:
            x = x + lax.ppermute(x, axis, [(i, i ^ step) for i in range(size)])
            step *= 2
    return x


def sum_across(x):
    axes = AXES[1:]
    sizes = [lax.axis_size(axis) for axis in axes]
    if sizes != [4, 2]:
        return [sum_over(x, axes)]
    x = x + pair_exchange(x, axes[0], (1,))[0]
    count = sizes[0] * sizes[1]
    terms = [
        lax.ppermute(x, axes, [(i, i ^ d) for i in range(count)])
        for d in (2 * sizes[1], 1, 2 * sizes[1] + 1)
    ]
    return [x] + terms


def rows(a):
    return slice(GROUP * a, GROUP * (a + 1))


def gather_lanes(table, index_row, group):
    lane = jnp.broadcast_to(index_row % LANES, (GROUP, LANES))
    tile = jnp.broadcast_to(index_row // LANES, (GROUP, LANES))
    out = None
    for number in range(table.shape[1] // LANES):
        source = table[rows(group), number * LANES : (number + 1) * LANES]
        picked = jnp.take_along_axis(source, lane, axis=1, mode="promise_in_bounds")
        out = picked if out is None else jnp.where(tile == number, picked, out)
    return out


def column(line):
    size = line.shape[1]
    shape = (size, size)
    same = lax.broadcasted_iota(jnp.int32, shape, 0) == lax.broadcasted_iota(jnp.int32, shape, 1)
    return jnp.sum(jnp.where(same, line, 0.0), axis=1, keepdims=True)


def split_rows(y, vectors):
    high = y.astype(jnp.bfloat16).astype(jnp.float32)
    return high + pltpu.roll(y - high, vectors, 0)


def join_rows(y, vectors):
    return y + pltpu.roll(y, GROUP - vectors, 0)


def pack_kernel(pos_hbm, spec_hbm, block_hbm, raw_hbm, own_ref, oct_ref, list_ref, *scratch):
    pos_ref, spec_ref, block_ref, raw_ref, sems = scratch
    copies = [
        pltpu.make_async_copy(source, target, sems.at[n])
        for n, (source, target) in enumerate(
            (
                (pos_hbm, pos_ref),
                (spec_hbm, spec_ref),
                (block_hbm, block_ref),
                (raw_hbm, raw_ref),
            )
        )
    ]
    for copy in copies:
        copy.start()
    for copy in copies:
        copy.wait()
    vectors = block_ref.shape[4]
    atoms = pos_ref.shape[-1]
    for a in range(3):
        parts = [block_ref[0, 0, 0, a], pos_ref[a]]
        used = vectors + 1
        if a == 0:
            parts.append(spec_ref[0, 0].astype(jnp.float32))
            used += 1
        parts.append(jnp.zeros((GROUP - used, atoms), jnp.float32))
        own_ref[rows(a), :] = jnp.concatenate(parts, axis=0)
    pieces = [raw_ref[n // 4, n // 2 % 2, n % 2 : n % 2 + 1, :] for n in range(8)]
    list_ref[...] = jnp.concatenate(pieces, axis=1)
    pick_octants(own_ref, list_ref, oct_ref)
    row = lax.broadcasted_iota(jnp.int32, (GROUP, list_ref.shape[1]), 0)
    oct_ref[rows(0), :] = jnp.where(
        row == vectors + 2, list_ref[...].astype(jnp.float32), oct_ref[rows(0), :]
    )


def prepare_kernel(
    atoms, ghosts, near_ref, emb_ref, rin_ref, rout_ref, read_ref, idx_ref, low_ref, in_ref, out_ref, col_ref
):
    index = table_index(near_ref[...], atoms, ghosts)
    idx_ref[...] = index
    low = lax.broadcasted_iota(jnp.int32, low_ref.shape, 0) == index % LANES
    low_ref[...] = jnp.where(low, 1.0, 0.0).astype(jnp.bfloat16)
    high, middle, rest = split_parts(rin_ref[...])
    stack = [high, middle, rest, high, middle, high]
    pad = in_ref.shape[1] - 6 * rin_ref.shape[0]
    stack = jnp.concatenate(stack + [jnp.zeros((pad, rin_ref.shape[1]), jnp.float32)], axis=0)
    in_ref[...] = jnp.transpose(stack).astype(jnp.bfloat16)
    high, rest, _ = split_parts(rout_ref[...])
    out_ref[...] = jnp.concatenate(
        [jnp.concatenate([high, high], axis=1), jnp.concatenate([rest, rest], axis=1)], axis=0
    ).astype(jnp.bfloat16)
    species = emb_ref.shape[0]
    lane = lax.broadcasted_iota(jnp.int32, col_ref.shape, 1)
    columns = jnp.broadcast_to(column(read_ref[...]), col_ref.shape)
    for n in range(species):
        columns = jnp.where(lane == n, column(emb_ref[n : n + 1, :]), columns)
    col_ref[...] = columns


def pick_octants(own_ref, list_ref, oct_ref):
    for j in range(list_ref.shape[1] // LANES):
        cut = slice(j * LANES, (j + 1) * LANES)
        for a in range(3):
            oct_ref[rows(a), cut] = gather_lanes(own_ref, list_ref[:, cut], a)


def add_octants(own, octants, lists, vectors):
    atoms = own.shape[1]
    width = lists.shape[1]
    keep = lax.broadcasted_iota(jnp.int32, octants.shape, 0) < vectors
    packed = split_rows(jnp.where(keep, octants, 0.0), vectors).astype(jnp.bfloat16)
    onehot = lax.broadcasted_iota(jnp.int32, (atoms, width), 0) == lists
    spread = lax.dot_general(
        packed,
        jnp.where(onehot, 1.0, 0.0).astype(jnp.bfloat16),
        (((1,), (1,)), ((), ())),
        preferred_element_type=jnp.float32,
    )
    return own + join_rows(spread, vectors)


def fill_table(table, own_ref, ghost_refs, vectors, ghosts, shifted):
    atoms = own_ref.shape[1]
    table[:, :atoms] = own_ref[...]
    width = 8 * ghosts
    places = [
        (ref, j * width) for ref in ghost_refs for j in range(ref.shape[1] // width)
    ]
    if len(ghost_refs) == 2:
        places = [places[n] for n in (0, 1, 4, 5, 2, 3, 6, 7)]
    for kind, (ref, start) in enumerate(places):
        if kind == 0:
            continue
        part = ref[:, start : start + width]
        if shifted:
            row = lax.broadcasted_iota(jnp.int32, part.shape, 0)
            for a in range(3):
                if (kind >> a) & 1:
                    move = jnp.where(octant_bit(part.shape, a, ghosts), -1.0, 1.0)
                    part = part + jnp.where(row == GROUP * a + vectors, move, 0.0)
        base = atoms + (kind - 1) * width
        table[:, base : base + width] = part


def gather_slot(table, idx_ref, k, atoms):
    pieces = [[] for _ in range(3)]
    for j in range(atoms // LANES):
        index_row = idx_ref[:, pl.ds(pl.multiple_of(k * atoms + j * LANES, LANES), LANES)]
        for a in range(3):
            pieces[a].append(gather_lanes(table, index_row, a))
    return [jnp.concatenate(p, axis=1) for p in pieces]


def pair_list(fanout):
    return [(k, l) for k in range(fanout) for l in range(k, fanout)]


def lookup(table, fanout):
    where = {pair: n for n, pair in enumerate(pair_list(fanout))}
    return lambda k, l: table[where[min(k, l), max(k, l)]]


def sum_rows(parts):
    row = lax.broadcasted_iota(jnp.int32, parts[0].shape, 0)
    if len(parts) != 4 or GROUP != 8:
        out = jnp.zeros_like(parts[0])
        for n, part in enumerate(parts):
            out = jnp.where(row == n, jnp.sum(part, axis=0, keepdims=True), out)
        return out
    fold = [part + pltpu.roll(part, 4, 0) for part in parts]
    low = row < 4
    lead = jnp.where(low, fold[0], fold[1])
    rest = jnp.where(low, fold[2], fold[3])
    both = jnp.where(row % 4 < 2, lead + pltpu.roll(lead, 6, 0), rest + pltpu.roll(rest, 2, 0))
    even = both + pltpu.roll(both, 7, 0)
    odd = both + pltpu.roll(both, 1, 0)
    return jnp.where(row % 2 == 1, pltpu.roll(odd, 4, 0), even)


def dot3(x, y):
    return x[0] * y[0] + x[1] * y[1] + x[2] * y[2]


def slot_cut(k, atoms):
    return slice(k * atoms, (k + 1) * atoms)


def tile_rows(n):
    return slice(GROUP * n, GROUP * (n + 1))


def tangents(diffs, units, invs, tn, changes, vectors):
    fanout = len(diffs)
    pairs = pair_list(fanout)
    per_vector = fanout + len(pairs)
    taus = [dot3(units[k], diffs[k]) for k in range(fanout)]
    turns = [
        [(diffs[k][a] - units[k][a] * taus[k]) * invs[k] for a in range(3)] for k in range(fanout)
    ]
    values = list(taus)
    for k, l in pairs:
        half = dot3(units[k], turns[l])
        values.append(2.0 * half if k == l else half + dot3(units[l], turns[k]))
    for n, value in enumerate(values):
        changes[tile_rows(n), :] = value
        for v in range(vectors):
            tn[tile_rows(v * per_vector + n), :] = jnp.broadcast_to(
                value[v : v + 1, :], value.shape
            )


def channel_products(f, f1, q, rp, rpp, cosine, tn, acc, lanes, fanout, vectors):
    pairs = pair_list(fanout)
    per_vector = fanout + len(pairs)
    slots = range(fanout)
    rpp_q = [rpp[k] * q[k] for k in slots]
    rpp_f = [rpp[k] * f[k] for k in slots]
    for v in range(vectors):
        base = v * per_vector

        def tangent(n):
            return tn[tile_rows(base + n), lanes]

        phi = [f1[k] * tangent(k) for k in slots]
        index = {pair: fanout + n for n, pair in enumerate(pairs)}
        dq = []
        for k in slots:
            total = None
            for l in slots:
                term = phi[l] * cosine(k, l) + f[l] * tangent(index[min(k, l), max(k, l)])
                total = term if total is None else total + term
            dq.append(total)
        y = [phi[k] * rpp_q[k] + dq[k] * rpp_f[k] for k in slots]
        w = [y[k] * f[k] + rp[k] * phi[k] for k in slots]
        for k in slots:
            total = y[k] * q[k] + rp[k] * dq[k]
            for l in slots:
                total = total + w[l] * cosine(k, l)
            acc[tile_rows(base + k), lanes] += f1[k] * total
        for n, (k, l) in enumerate(pairs):
            term = w[k] * f[l] if k == l else w[k] * f[l] + w[l] * f[k]
            acc[tile_rows(base + fanout + n), lanes] += term


def finish_product(
    idx_ref, low_ref, unit_ref, inv_ref, sums_ref, acc, changes, diffs, terms_out, vectors
):
    fanout = len(diffs)
    atoms = idx_ref.shape[1] // fanout
    tiles = terms_out.shape[1] // LANES
    pairs = pair_list(fanout)
    per_vector = fanout + len(pairs)
    slots = range(fanout)
    row = lax.broadcasted_iota(jnp.int32, (GROUP, atoms), 0)
    outs = [
        sum_rows([acc[tile_rows(v * per_vector + n), :] for v in range(vectors)])
        for n in range(per_vector)
    ]
    taus = [changes[tile_rows(k), :] for k in slots]
    turned = lookup([changes[tile_rows(fanout + n), :] for n in range(len(pairs))], fanout)
    bent = lookup(outs[fanout:], fanout)
    units = [[unit_ref[rows(a), slot_cut(k, atoms)] for a in range(3)] for k in slots]
    invs = [inv_ref[:, slot_cut(k, atoms)] for k in slots]
    turns = [
        [(diffs[k][a] - units[k][a] * taus[k]) * invs[k] for a in range(3)] for k in slots
    ]

    def base_sum(n):
        line = (n // 4) * GROUP + n % 4
        return sums_ref[line : line + 1, :]

    stretch = [base_sum(k) for k in slots]
    curve = [base_sum(fanout + k) for k in slots]
    weight = lookup([base_sum(2 * fanout + n) for n in range(len(pairs))], fanout)
    mixed = [[base_sum(2 * fanout + len(pairs) + k * fanout + l) for l in slots] for k in slots]
    center = [jnp.zeros((GROUP, atoms), jnp.float32) for _ in range(3)]
    shifted = [jnp.zeros((GROUP, atoms), jnp.float32) for _ in range(vectors)]
    left = []
    for k in slots:
        along = outs[k] + curve[k] * taus[k]
        force = [0.0, 0.0, 0.0]
        change = [0.0, 0.0, 0.0]
        for l in slots:
            along = along + turned(k, l) * mixed[k][l]
            bend = bent(k, l) + taus[l] * mixed[l][k] + taus[k] * mixed[k][l]
            pull = weight(k, l)
            if k == l:
                bend = bend + bent(k, l)
                pull = pull + pull
            for a in range(3):
                force[a] = force[a] + pull * units[l][a]
                change[a] = change[a] + bend * units[l][a] + pull * turns[l][a]
        flat = dot3(units[k], force)
        inv = invs[k]
        along = (
            along
            - (dot3(units[k], change) + dot3(turns[k], force)) * inv
            + taus[k] * flat * (inv * inv)
        )
        keep = stretch[k] - flat * inv
        packed = []
        for a in range(3):
            y = (
                along * units[k][a]
                + keep * turns[k][a]
                + (change[a] - taus[k] * inv * force[a]) * inv
            )
            y = jnp.where(row < vectors, y, 0.0)
            center[a] = center[a] - y
            for n in range(vectors):
                other = y if n == 0 else pltpu.roll(y, n, 0)
                if n:
                    other = other + pltpu.roll(y, GROUP - vectors + n, 0)
                shifted[n] = shifted[n] + other * diffs[k][a]
            packed.append(split_rows(y, vectors))
        packed = jnp.concatenate(packed, axis=0)
        tile = idx_ref[:, slot_cut(k, atoms)] // LANES
        left.append(
            jnp.concatenate(
                [jnp.where(tile == number, packed, 0.0) for number in range(tiles)], axis=0
            ).astype(jnp.bfloat16)
        )
    spread = lax.dot_general(
        jnp.concatenate(left, axis=1),
        low_ref[...],
        (((1,), (1,)), ((), ())),
        preferred_element_type=jnp.float32,
    )
    own_tiles = atoms // LANES
    for number in range(tiles):
        for a in range(3):
            value = join_rows(spread[tile_rows(number * 3 + a)], vectors)
            cut = slice(number * LANES, (number + 1) * LANES)
            if number < own_tiles:
                value = value + center[a][:, cut]
            terms_out[rows(a), cut] = value
    return shifted


def split_parts(x):
    high = x.astype(jnp.bfloat16).astype(jnp.float32)
    rest = x - high
    middle = rest.astype(jnp.bfloat16).astype(jnp.float32)
    low = (rest - middle).astype(jnp.bfloat16).astype(jnp.float32)
    return high, middle, low


def silu_slopes(x):
    sig = 0.5 + 0.5 * jnp.tanh(0.5 * x)
    anti = 1.0 - sig
    return sig, sig * (1.0 + x * anti), sig * anti * (2.0 + x * (anti - sig))


def half_turns(dist, inv, basis):
    shape = (basis, dist.shape[1])
    order = (lax.broadcasted_iota(jnp.int32, shape, 0) + 1).astype(jnp.float32)
    turns = order * (dist * (1.0 / CUTOFF))
    whole = jnp.floor(turns + 0.5)
    sign = 1.0 - 2.0 * (whole - 2.0 * jnp.floor(whole * 0.5))
    x = (turns - whole) * np.float32(np.pi)
    x2 = x * x

    def series(terms):
        value = terms[-1]
        for term in terms[-2::-1]:
            value = term + x2 * value
        return value

    sine = sign * x * series([(-1.0) ** n / math.factorial(2 * n + 1) for n in range(6)])
    cosine = sign * series([(-1.0) ** n / math.factorial(2 * n) for n in range(7)])
    omega = order * np.float32(np.pi / CUTOFF)
    b0 = sine * inv
    b1 = (omega * cosine - b0) * inv
    b2 = -(omega * omega * sine + 2.0 * b1) * inv
    return jnp.concatenate([b0, b1, b2], axis=1)


def first_kernel(
    ghosts,
    vectors,
    basis,
    species,
    idx_ref,
    own_ref,
    g1_ref,
    g2_ref,
    g3_ref,
    low_ref,
    in_ref,
    out_ref,
    col_ref,
    terms_out,
    unit_ref,
    inv_ref,
    sums_ref,
    cos_ref,
    f_ref,
    f1_ref,
    q_ref,
    rp_ref,
    rpp_ref,
    table,
    f2_ref,
    read_col,
    tn,
    changes,
    acc,
    acc2,
):
    atoms = own_ref.shape[1]
    fanout = idx_ref.shape[1] // atoms
    channels = col_ref.shape[0]
    pairs = pair_list(fanout)
    slots = range(fanout)
    embeds = [col_ref[:, n : n + 1] for n in range(species)]
    read_col[...] = jnp.broadcast_to(col_ref[:, species : species + 1], read_col.shape)
    fill_table(table, own_ref, (g1_ref, g2_ref, g3_ref), vectors, ghosts, True)

    def embed(kind):
        value = embeds[0]
        for n in range(1, species):
            value = jnp.where(kind == float(n), embeds[n], value)
        return value

    own_embed = embed(own_ref[vectors + 1 : vectors + 2, :])
    inward = in_ref[:, : 6 * basis]
    outward = out_ref[...]
    diffs, units, invs = [], [], []
    for k in slots:
        cut = slot_cut(k, atoms)
        near = gather_slot(table, idx_ref, k, atoms)
        diff = [near[a] - own_ref[rows(a), :] for a in range(3)]
        delta = [
            jnp.broadcast_to(diff[a][vectors : vectors + 1, :], (GROUP, atoms)) for a in range(3)
        ]
        dist = jnp.sqrt(dot3(delta, delta) + SOFTEN)
        inv = 1.0 / dist
        unit = [delta[a] * inv for a in range(3)]
        for a in range(3):
            unit_ref[rows(a), cut] = unit[a]
        inv_ref[:, cut] = inv
        diffs.append(diff)
        units.append(unit)
        invs.append(inv)
        one = dist[0:1]
        radii = half_turns(one, inv[0:1], basis)
        high, middle, rest = split_parts(radii)
        z = jnp.dot(
            inward,
            jnp.concatenate([high, high, high, middle, middle, rest], axis=0).astype(jnp.bfloat16),
            preferred_element_type=jnp.float32,
        )
        z0, z1, z2 = z[:, :atoms], z[:, atoms : 2 * atoms], z[:, 2 * atoms :]
        sig, slope, curve = silu_slopes(z0)
        hidden = jnp.concatenate([z0 * sig, slope * z1, curve * z1 * z1 + slope * z2], axis=1)
        high = hidden.astype(jnp.bfloat16)
        rest = (hidden - high.astype(jnp.float32)).astype(jnp.bfloat16)
        radial = jnp.dot(
            outward, jnp.concatenate([high, rest], axis=0), preferred_element_type=jnp.float32
        )
        radial = radial[:channels] + radial[channels:]
        r0, r1, r2 = radial[:, :atoms], radial[:, atoms : 2 * atoms], radial[:, 2 * atoms :]
        square = one * one
        base = 1.0 - square * (1.0 / CUTOFF**2)
        v0 = base * base
        v1 = base * one * (-4.0 / CUTOFF**2)
        v2 = -4.0 / CUTOFF**2 + square * (12.0 / CUTOFF**4)
        pair = own_embed * embed(near[0][vectors + 1 : vectors + 2, :])
        f_ref[:, cut] = pair * (r0 * v0)
        f1_ref[:, cut] = pair * (r1 * v0 + r0 * v1)
        f2_ref[:, cut] = pair * (r2 * v0 + 2.0 * (r1 * v1) + r0 * v2)
    for n, (k, l) in enumerate(pairs):
        cos_ref[tile_rows(n), :] = 1.0 + dot3(units[k], units[l])
    tangents(diffs, units, invs, tn, changes, vectors)
    acc[...] = jnp.zeros_like(acc)
    acc2[...] = jnp.zeros_like(acc2)
    share = 1.0 / fanout

    def tile(number, carry):
        here = pl.ds(pl.multiple_of(number * GROUP, GROUP), GROUP)
        for half in range(atoms // LANES):
            lanes = slice(half * LANES, (half + 1) * LANES)
            cuts = [slice(k * atoms + half * LANES, k * atoms + (half + 1) * LANES) for k in slots]
            cosine = lookup([cos_ref[tile_rows(n), lanes] for n in range(len(pairs))], fanout)
            f = [f_ref[here, cut] for cut in cuts]
            f1 = [f1_ref[here, cut] for cut in cuts]
            read = read_col[here, :] * share
            q, rp, rpp = [], [], []
            for k in slots:
                project = sum(f[l] * cosine(k, l) for l in slots)
                _, slope, curve = silu_slopes(f[k] * project * share)
                q.append(project)
                rp.append(read * slope)
                rpp.append(read * share * curve)
                q_ref[here, cuts[k]] = q[k]
                rp_ref[here, cuts[k]] = rp[k]
                rpp_ref[here, cuts[k]] = rpp[k]
            m = [rp[k] * f[k] for k in slots]
            slope = [rp[k] * q[k] + sum(m[l] * cosine(k, l) for l in slots) for k in slots]
            terms = [slope[k] * f1[k] for k in slots]
            terms += [slope[k] * f2_ref[here, cuts[k]] for k in slots]
            terms += [m[k] * f[l] if k == l else m[k] * f[l] + m[l] * f[k] for k, l in pairs]
            terms += [f1[k] * m[l] for k in slots for l in slots]
            for n, term in enumerate(terms):
                acc2[tile_rows(n), lanes] += term
            channel_products(f, f1, q, rp, rpp, cosine, tn, acc, lanes, fanout, vectors)
        return carry

    lax.fori_loop(0, channels // GROUP, tile, 0)
    count = acc2.shape[0] // GROUP
    for n in range(0, count, 4):
        parts = [acc2[tile_rows(min(n + j, count - 1)), :] for j in range(4)]
        sums_ref[tile_rows(n // 4), :] = sum_rows(parts)
    finish_product(
        idx_ref,
        low_ref,
        unit_ref,
        inv_ref,
        sums_ref,
        acc,
        changes,
        diffs,
        terms_out,
        vectors,
    )


def second_kernel(ghosts, vectors, levels, idx_ref, own_ref, *refs):
    ghost_refs, refs = refs[:levels], refs[levels:]
    low_ref, unit_ref, inv_ref, sums_ref, cos_ref, f_ref, f1_ref, q_ref, rp_ref, rpp_ref = refs[:10]
    terms_out, gram_out, table, tn, changes, acc = refs[10:]
    atoms = own_ref.shape[1]
    fanout = idx_ref.shape[1] // atoms
    channels = f_ref.shape[0]
    pairs = pair_list(fanout)
    slots = range(fanout)
    fill_table(table, own_ref, ghost_refs, vectors, ghosts, False)
    diffs = []
    for k in slots:
        near = gather_slot(table, idx_ref, k, atoms)
        diffs.append([near[a] - own_ref[rows(a), :] for a in range(3)])
    units = [[unit_ref[rows(a), slot_cut(k, atoms)] for a in range(3)] for k in slots]
    invs = [inv_ref[:, slot_cut(k, atoms)] for k in slots]
    tangents(diffs, units, invs, tn, changes, vectors)
    acc[...] = jnp.zeros_like(acc)

    def tile(number, carry):
        here = pl.ds(pl.multiple_of(number * GROUP, GROUP), GROUP)
        for half in range(atoms // LANES):
            lanes = slice(half * LANES, (half + 1) * LANES)
            cuts = [slice(k * atoms + half * LANES, k * atoms + (half + 1) * LANES) for k in slots]
            cosine = lookup([cos_ref[tile_rows(n), lanes] for n in range(len(pairs))], fanout)
            parts = [
                [ref[here, cut] for cut in cuts] for ref in (f_ref, f1_ref, q_ref, rp_ref, rpp_ref)
            ]
            channel_products(*parts, cosine, tn, acc, lanes, fanout, vectors)
        return carry

    lax.fori_loop(0, channels // GROUP, tile, 0)
    shifted = finish_product(
        idx_ref,
        low_ref,
        unit_ref,
        inv_ref,
        sums_ref,
        acc,
        changes,
        diffs,
        terms_out,
        vectors,
    )
    gram_out[...] = from_shifted(shifted, vectors)


def middle_kernel(vectors, own_ref, sums_ref, list_ref, full_ref, oct_ref):
    for a in range(3):
        full_ref[rows(a), :] = add_octants(
            own_ref[rows(a), :], sums_ref[rows(a), :], list_ref[...], vectors
        )
    pick_octants(full_ref, list_ref, oct_ref)


def inner(x, y, pad_to=LANES):
    pad = jnp.zeros((pad_to - y.shape[0], y.shape[1]), jnp.float32)
    return lax.dot_general(
        x,
        jnp.concatenate([y, pad], axis=0),
        (((1,), (1,)), ((), ())),
        precision=HIGHEST,
        preferred_element_type=jnp.float32,
    )


def only_vectors(x, vectors):
    row = lax.broadcasted_iota(jnp.int32, x.shape, 0)
    return jnp.where(row % GROUP < vectors, x, 0.0)


def pack_gram(total, edge):
    lane = lax.broadcasted_iota(jnp.int32, (GROUP, LANES), 1)
    out = total[rows(0)]
    out = jnp.where(lane >= 2 * GROUP, pltpu.roll(total[rows(1)], GROUP, 1), out)
    if edge is not None:
        out = jnp.where(lane >= 3 * GROUP, pltpu.roll(edge, 3 * GROUP, 1), out)
    return jnp.where(lane >= 4 * GROUP, pltpu.roll(total[rows(2)], 2 * GROUP, 1), out)


def gram_kernel(vectors, start_ref, first_ref, own_ref, sums_ref, list_ref, full_ref, gram_ref):
    total = jnp.zeros((3 * GROUP, LANES), jnp.float32)
    for a in range(3):
        second = add_octants(own_ref[rows(a), :], sums_ref[rows(a), :], list_ref[...], vectors)
        full_ref[rows(a), :] = second
        stack = jnp.concatenate([start_ref[rows(a), :], first_ref[rows(a), :], second], axis=0)
        stack = only_vectors(stack, vectors)
        total += inner(stack, stack)
    gram_ref[...] = pack_gram(total, None)


def packet_start(vectors, own_ref, sums_ref, ghost_ref, list_ref, part_ref, packet_ref):
    width = list_ref.shape[1]
    for a in range(3):
        part_ref[rows(a), :] = add_octants(
            own_ref[rows(a), :], sums_ref[rows(a), :], list_ref[...], vectors
        )
    mark = vectors + 1
    for j in range(width // LANES):
        cut = slice(j * LANES, (j + 1) * LANES)
        for a in range(3):
            value = gather_lanes(part_ref, list_ref[:, cut], a)
            if a == 0:
                row = lax.broadcasted_iota(jnp.int32, value.shape, 0)
                value = jnp.where(row == mark, list_ref[:, cut].astype(jnp.float32), value)
            packet_ref[rows(a), cut] = value
    packet_ref[:, width : 2 * width] = ghost_ref[...]


def arriving(side, packets, n, a, width):
    cut = slice(width, 2 * width)
    after, before = packets[(n + 1) % 4], packets[(n + 3) % 4]
    return jnp.where(side > 0.5, after[rows(a), cut], before[rows(a), cut])


def packet_lists(packet, vectors, width):
    mark = vectors + 1
    return packet[mark : mark + 1, :width].astype(jnp.int32)


def start_kernel(vectors, own_ref, sums_ref, ghost_ref, list_ref, part_ref, packet_ref):
    packet_start(vectors, own_ref, sums_ref, ghost_ref, list_ref, part_ref, packet_ref)


def merge_kernel(
    vectors, side_ref, part_ref, p0_ref, p1_ref, p2_ref, p3_ref, full_ref, level_ref, spread
):
    width = p0_ref.shape[1] // 2
    side = side_ref[...]
    packets = (p0_ref, p1_ref, p2_ref, p3_ref)
    lists = [packet_lists(p, vectors, width) for p in packets]
    for a in range(3):
        full_ref[rows(a), :] = add_octants(
            part_ref[rows(a), :], arriving(side, packets, 0, a, width), lists[0], vectors
        )
    near = []
    for n in (1, 3):
        for a in range(3):
            zero = jnp.zeros((GROUP, part_ref.shape[1]), jnp.float32)
            spread[rows(a), :] = add_octants(
                zero, arriving(side, packets, n, a, width), lists[n], vectors
            )
        values = []
        for a in range(3):
            pieces = [
                gather_lanes(spread, lists[n][:, j * LANES : (j + 1) * LANES], a)
                for j in range(width // LANES)
            ]
            values.append(packets[n][rows(a), :width] + jnp.concatenate(pieces, axis=1))
        near.append(values)
    for a in range(3):
        for j in range(width // LANES):
            cut = slice(j * LANES, (j + 1) * LANES)
            level_ref[rows(a), cut] = gather_lanes(full_ref, lists[0][:, cut], a)
        level_ref[rows(a), width : 2 * width] = jnp.where(side > 0.5, near[1][a], near[0][a])


def gram_start_kernel(
    vectors,
    start_ref,
    first_ref,
    own_ref,
    sums_ref,
    ghost_ref,
    list_ref,
    edge_ref,
    part_ref,
    packet_ref,
):
    packet_start(vectors, own_ref, sums_ref, ghost_ref, list_ref, part_ref, packet_ref)
    width = list_ref.shape[1]
    total = jnp.zeros((3 * GROUP, LANES), jnp.float32)
    for a in range(3):
        stack = jnp.concatenate(
            [start_ref[rows(a), :], first_ref[rows(a), :], part_ref[rows(a), :]], axis=0
        )
        stack = only_vectors(stack, vectors)
        total += inner(stack, stack)
    cut = slice(2 * width, 2 * width + LANES)
    packet_ref[rows(0), cut] = pack_gram(total, edge_ref[...])
    packet_ref[GROUP : 3 * GROUP, cut] = jnp.zeros((2 * GROUP, LANES), jnp.float32)


def shifted_products(x, y, vectors):
    return [x * (pltpu.roll(y, n, 0) if n else y) for n in range(vectors)]


def from_shifted(shifted, vectors):
    shape = (GROUP, LANES)
    row = lax.broadcasted_iota(jnp.int32, shape, 0)
    lane = lax.broadcasted_iota(jnp.int32, shape, 1)
    total = jnp.zeros(shape, jnp.float32)
    for n in range(vectors):
        value = jnp.sum(shifted[n], axis=1, keepdims=True)
        total = jnp.where(lane == (row + vectors - n) % vectors, value, total)
    return jnp.where((row < vectors) & (lane < vectors), total, 0.0)


def gram_merge_kernel(
    vectors, side_ref, p3_ref, p2_ref, part_ref, p0_ref, p1_ref, full_ref, gram_ref, spread
):
    width = (p0_ref.shape[1] - LANES) // 2
    atoms = part_ref.shape[1]
    side = side_ref[...]
    packets = (p0_ref, p1_ref, p2_ref, p3_ref)
    shares = []
    for n in range(4):
        lists = packet_lists(packets[n], vectors, width)
        terms = [only_vectors(arriving(side, packets, n, a, width), vectors) for a in range(3)]
        packed = jnp.concatenate([split_rows(t, vectors) for t in terms], axis=0)
        onehot = lax.broadcasted_iota(jnp.int32, (atoms, width), 0) == lists
        placed = lax.dot_general(
            packed.astype(jnp.bfloat16),
            jnp.where(onehot, 1.0, 0.0).astype(jnp.bfloat16),
            (((1,), (1,)), ((), ())),
            preferred_element_type=jnp.float32,
        )
        total = None
        for a in range(3):
            value = join_rows(placed[rows(a)], vectors)
            spread[rows(a), :] = value
            if n == 0:
                full_ref[rows(a), :] = part_ref[rows(a), :] + value
            at = only_vectors(packets[n][rows(a), :width], vectors)
            at = at + pltpu.roll(at, vectors, 0)
            back = jnp.concatenate(
                [
                    gather_lanes(spread, lists[:, j * LANES : (j + 1) * LANES], a)
                    for j in range(width // LANES)
                ],
                axis=1,
            )
            found = shifted_products(terms[a], at + at + back, vectors)
            total = found if total is None else [x + y for x, y in zip(total, found)]
        shares.append([packets[n][rows(0), 2 * width : 2 * width + LANES]] + total)

    def add(x, y):
        return [p + q for p, q in zip(x, y)]

    total = add(add(shares[0], shares[1]), add(shares[2], shares[3]))
    gram_ref[...] = total[0] + pltpu.roll(from_shifted(total[1:], vectors), 4 * GROUP, 1)


def pair_sums(mine, other, got, width, atoms):
    def tile(ref, kind, a):
        start = atoms + (kind - 1) * width
        return ref[rows(a), start : start + width]

    def back(n, a):
        return got[rows(a), n * width : (n + 1) * width]

    def pick(first, second, n):
        return (
            [first[rows(a), :atoms] for a in range(3)],
            [tile(second, 4, a) + back(n, a) for a in range(3)],
            [tile(first, 1, a) + tile(second, 5, a) + back(n + 1, a) for a in range(3)],
        )

    return pick(mine, other, 0), pick(other, mine, 2)


def pair_packet(vectors, mine, other, got, lists, parts, packet, ghosts_width):
    atoms = parts[0].shape[1]
    mark = vectors + 1
    for n, (own, sums, beside) in enumerate(pair_sums(mine, other, got, ghosts_width, atoms)):
        base = 2 * n * ghosts_width
        for a in range(3):
            parts[n][rows(a), :] = add_octants(own[a], sums[a], lists[n], vectors)
        for a in range(3):
            packet[rows(a), base + ghosts_width : base + 2 * ghosts_width] = beside[a]
            for j in range(ghosts_width // LANES):
                cut = slice(j * LANES, (j + 1) * LANES)
                value = gather_lanes(parts[n], lists[n][:, cut], a)
                if a == 0:
                    row = lax.broadcasted_iota(jnp.int32, value.shape, 0)
                    value = jnp.where(row == mark, lists[n][:, cut].astype(jnp.float32), value)
                packet[rows(a), base + j * LANES : base + (j + 1) * LANES] = value


def pair_lists(vectors, list_ref, beyond_ref):
    row = vectors + 2
    width = list_ref.shape[1]
    return list_ref[...], beyond_ref[row : row + 1, :width].astype(jnp.int32)


def pair_start_kernel(
    vectors, mine, other, got, list_ref, beyond_ref, part_ref, packet_ref, beyond_part
):
    pair_packet(
        vectors,
        mine,
        other,
        got,
        pair_lists(vectors, list_ref, beyond_ref),
        (part_ref, beyond_part),
        packet_ref,
        list_ref.shape[1],
    )


def placed_terms(side, packets, n, half, lists, atoms, width, vectors):
    start = (2 * half + 1) * width
    after, before = packets[(n + 1) % 4], packets[(n + 3) % 4]
    terms = [
        only_vectors(
            jnp.where(
                side > 0.5,
                after[rows(a), start : start + width],
                before[rows(a), start : start + width],
            ),
            vectors,
        )
        for a in range(3)
    ]
    packed = jnp.concatenate([split_rows(t, vectors) for t in terms], axis=0)
    onehot = lax.broadcasted_iota(jnp.int32, (atoms, width), 0) == lists
    placed = lax.dot_general(
        packed.astype(jnp.bfloat16),
        jnp.where(onehot, 1.0, 0.0).astype(jnp.bfloat16),
        (((1,), (1,)), ((), ())),
        preferred_element_type=jnp.float32,
    )
    return terms, [join_rows(placed[rows(a)], vectors) for a in range(3)]


def read_back(ref, lists, a):
    pieces = [
        gather_lanes(ref, lists[:, j * LANES : (j + 1) * LANES], a)
        for j in range(lists.shape[1] // LANES)
    ]
    return jnp.concatenate(pieces, axis=1)


def packet_row(packet, half, vectors, width):
    mark = vectors + 1
    start = 2 * half * width
    return packet[mark : mark + 1, start : start + width].astype(jnp.int32)


def pair_merge_kernel(
    vectors,
    width,
    side_ref,
    part_ref,
    p0_ref,
    p1_ref,
    p2_ref,
    p3_ref,
    start_ref,
    full_ref,
    level_ref,
    gram_ref,
    spread,
):
    atoms = part_ref.shape[1]
    side = side_ref[...]
    packets = (p0_ref, p1_ref, p2_ref, p3_ref)
    for half in range(2):
        found = []
        for slot, n in enumerate((0, 1, 3)):
            lists = packet_row(packets[n], half, vectors, width)
            _, placed = placed_terms(side, packets, n, half, lists, atoms, width, vectors)
            spread_here = spread.at[half * 3 + slot]
            for a in range(3):
                spread_here[rows(a), :] = placed[a]
                if n == 0 and half == 0:
                    full_ref[rows(a), :] = part_ref[rows(a), :] + placed[a]
            start = 2 * half * width
            found.append(
                [
                    packets[n][rows(a), start : start + width] + read_back(spread_here, lists, a)
                    for a in range(3)
                ]
            )
        for a in range(3):
            start = 2 * half * width
            level_ref[rows(a), start : start + width] = found[0][a]
            level_ref[rows(a), start + width : start + 2 * width] = jnp.where(
                side > 0.5, found[2][a], found[1][a]
            )
    total = jnp.zeros((2 * GROUP, LANES), jnp.float32)
    for a in range(3):
        stack = jnp.concatenate([start_ref[rows(a), :], full_ref[rows(a), :]], axis=0)
        stack = only_vectors(stack, vectors)
        total += inner(stack, stack)
    gram_ref[...] = pack_gram(
        jnp.concatenate([total, jnp.zeros((GROUP, LANES), jnp.float32)], axis=0),
        jnp.zeros((GROUP, LANES), jnp.float32),
    )


def repeat_rows(x, vectors):
    x = only_vectors(x, vectors)
    return x + pltpu.roll(x, vectors, 0)


def pair_gram_start_kernel(
    vectors,
    mine,
    other,
    got,
    list_ref,
    beyond_ref,
    gram_ref,
    beyond_gram,
    part_ref,
    packet_ref,
    beyond_part,
):
    width = list_ref.shape[1]
    parts = (part_ref, beyond_part)
    pair_packet(
        vectors,
        mine,
        other,
        got,
        pair_lists(vectors, list_ref, beyond_ref),
        parts,
        packet_ref,
        width,
    )
    squares = []
    for part in parts:
        total = None
        for a in range(3):
            value = repeat_rows(part[rows(a), :], vectors)
            found = shifted_products(value, value, vectors)
            total = found if total is None else [x + y for x, y in zip(total, found)]
        squares.append(from_shifted(total, vectors))
    gram = gram_ref[...] + beyond_gram[...]
    cut = slice(4 * width, 4 * width + LANES)
    packet_ref[rows(0), cut] = gram + pltpu.roll(squares[0] + squares[1], 4 * GROUP, 1)
    packet_ref[GROUP : 3 * GROUP, cut] = jnp.zeros((2 * GROUP, LANES), jnp.float32)


def pair_gram_merge_kernel(
    vectors,
    width,
    side_ref,
    p3_ref,
    p2_ref,
    part_ref,
    p0_ref,
    p1_ref,
    full_ref,
    gram_ref,
    spread,
):
    atoms = part_ref.shape[1]
    side = side_ref[...]
    packets = (p0_ref, p1_ref, p2_ref, p3_ref)
    shares = []
    for n in range(4):
        total = []
        for half in range(2):
            lists = packet_row(packets[n], half, vectors, width)
            terms, placed = placed_terms(side, packets, n, half, lists, atoms, width, vectors)
            spread_here = spread.at[2 * n + half]
            found = None
            for a in range(3):
                spread_here[rows(a), :] = placed[a]
                if n == 0 and half == 0:
                    full_ref[rows(a), :] = part_ref[rows(a), :] + placed[a]
                start = 2 * half * width
                at = repeat_rows(packets[n][rows(a), start : start + width], vectors)
                products = shifted_products(
                    terms[a], at + at + read_back(spread_here, lists, a), vectors
                )
                found = products if found is None else [x + y for x, y in zip(found, products)]
            total.append(found)
        share = packets[n][rows(0), 4 * width : 4 * width + LANES]
        shares.append([share] + [x + y for x, y in zip(*total)])

    def add(x, y):
        return [p + q for p, q in zip(x, y)]

    total = add(add(shares[0], shares[1]), add(shares[2], shares[3]))
    gram_ref[...] = total[0] + pltpu.roll(from_shifted(total[1:], vectors), 4 * GROUP, 1)


def last_kernel(vectors, scale, start_ref, first_ref, second_ref, *refs):
    gram_refs, refs = refs[:-7], refs[-7:]
    next_hbm, diag_hbm, off_hbm, next_ref, diag_ref, off_ref, sems = refs
    shape = (GROUP, LANES)
    row = lax.broadcasted_iota(jnp.int32, shape, 0)
    lane = lax.broadcasted_iota(jnp.int32, shape, 1)
    levels = [ref[...] for ref in gram_refs]
    while len(levels) > 1:
        levels = [sum(levels[n : n + 2]) for n in range(0, len(levels), 2)]
    gram = levels[0] * scale
    size = range(vectors)

    def block(n):
        return [
            [
                jnp.broadcast_to(gram[i : i + 1, GROUP * n + j : GROUP * n + j + 1], shape)
                for j in size
            ]
            for i in size
        ]

    def total(terms):
        terms = [t for t in terms if t is not None]
        out = terms[0] if terms else None
        for term in terms[1:]:
            out = out + term
        return out

    def times(x, y):
        return None if x is None or y is None else x * y

    def mul(x, y):
        return [[total([times(x[i][k], y[k][j]) for k in size]) for j in size] for i in size]

    def even(x):
        return [[x[min(i, j)][max(i, j)] for j in size] for i in size]

    def mul_even(x, y):
        upper = [
            [total([times(x[i][k], y[k][j]) for k in size]) if j >= i else None for j in size]
            for i in size
        ]
        return even(upper)

    def add(x, y, sign=1.0):
        def join(p, q):
            if p is None or q is None:
                return (q if sign > 0 else None if q is None else -q) if p is None else p
            return p + q if sign > 0 else p - q

        return [[join(p, q) for p, q in zip(u, v)] for u, v in zip(x, y)]

    def flip(x):
        return [[x[j][i] for j in size] for i in size]

    def factor(m):
        m = [list(line) for line in m]
        lower = [[None] * vectors for _ in size]
        inverse = [[jnp.ones(shape, jnp.float32) if i == j else None for j in size] for i in size]
        for j in size:
            pivot = lax.rsqrt(m[j][j])
            for i in range(j, vectors):
                lower[i][j] = m[i][j] * pivot
            inverse[j] = [times(x, pivot) for x in inverse[j]]
            for i in range(j + 1, vectors):
                for k in range(j + 1, i + 1):
                    m[i][k] = m[i][k] - lower[i][j] * lower[k][j]
                for k in range(j + 1):
                    step = times(lower[i][j], inverse[j][k])
                    if step is not None:
                        old = inverse[i][k]
                        inverse[i][k] = -step if old is None else old - step
        return lower, inverse

    ss, su, uu, uq, qq = (block(n) for n in range(5))
    qq = [[0.5 * (qq[i][j] + qq[j][i]) for j in size] for i in size]
    _, p0 = factor(ss)
    p0t = flip(p0)
    a1 = mul_even(mul(p0, su), p0t)
    l1, p1 = factor(add(mul_even(mul(p0, uu), p0t), mul_even(a1, a1), -1.0))
    b = mul(p1, p0)
    a = [[-x for x in line] for line in mul(p1, mul(a1, p0))]
    at, bt, up1 = flip(a), flip(b), flip(l1)
    right_s = add(mul(su, at), mul(uu, bt))
    right_u = add(mul(uu, at), mul(uq, bt))
    right_q = add(mul(uq, at), mul(qq, bt))
    a2 = even(add(mul_even(a, right_s), mul_even(b, right_u)))
    ww = add(mul_even(a, right_u), mul_even(b, right_q))
    l2, p2 = factor(add(add(ww, mul_even(a2, a2), -1.0), mul_even(up1, l1), -1.0))
    up2 = flip(l2)
    weights = (
        [[-x for x in line] for line in mul(p2, add(mul(a2, a), mul(up1, p0)))],
        mul(p2, add(a, mul(a2, b), -1.0)),
        mul(p2, b),
    )

    def tile(x):
        out = jnp.zeros(shape, jnp.float32)
        for i in size:
            for j in size:
                if x[i][j] is not None:
                    out = jnp.where((row == i) & (lane == j), x[i][j], out)
        return out[:vectors, :vectors]

    def stacked(x, j):
        out = jnp.zeros(shape, jnp.float32)
        for i in size:
            if x[i][j] is not None:
                out = jnp.where(row == i, x[i][j], out)
        return jnp.concatenate([out] * (start_ref.shape[1] // LANES), axis=1)

    diag_ref[0] = tile(a1)
    diag_ref[1] = tile(a2)
    off_ref[0] = tile(up1)
    off_ref[1] = tile(up2)
    copies = [
        pltpu.make_async_copy(diag_ref, diag_hbm, sems.at[0]),
        pltpu.make_async_copy(off_ref, off_hbm, sems.at[1]),
    ]
    for copy in copies:
        copy.start()
    columns = [[stacked(weight, w) for w in size] for weight in weights]
    for comp in range(3):
        value = None
        for n, ref in enumerate((start_ref, first_ref, second_ref)):
            for w in size:
                line = GROUP * comp + w
                term = columns[n][w] * ref[line : line + 1, :]
                value = term if value is None else value + term
        next_ref[0, 0, 0, comp] = value[:vectors]
    copies.append(pltpu.make_async_copy(next_ref, next_hbm, sems.at[2]))
    copies[-1].start()
    for copy in copies:
        copy.wait()


def call(body, outs, args, scratch=(), flops=0, spaces=pltpu.VMEM, out_spaces=pltpu.VMEM):
    outs = [shape if isinstance(shape[0], tuple) else (shape, jnp.float32) for shape in outs]
    return pl.pallas_call(
        body,
        out_shape=[jax.ShapeDtypeStruct(shape, kind) for shape, kind in outs],
        in_specs=[pl.BlockSpec(memory_space=spaces)] * len(args),
        out_specs=[pl.BlockSpec(memory_space=out_spaces)] * len(outs),
        scratch_shapes=[
            pltpu.VMEM(shape, jnp.float32) if isinstance(shape, tuple) else shape
            for shape in scratch
        ],
        cost_estimate=pl.CostEstimate(flops=flops, bytes_accessed=0, transcendentals=0)
        if flops
        else None,
        compiler_params=pltpu.CompilerParams(vmem_limit_bytes=VMEM_BYTES),
    )(*args)


def table_index(neighbors, atoms, ghosts):
    entry = neighbors - atoms
    cell = entry // ghosts
    number = cell
    kept = [n for n in range(64) if not all(m in (1, 2) for m in (n // 16, n // 4 % 4, n % 4))]
    previous = -1
    for position, n in enumerate(kept):
        if n - previous > 1:
            number = number + jnp.where(cell >= position, n - previous - 1, 0)
        previous = n
    member = (number // 16, number // 4 % 4, number % 4)
    kind = 0
    octant = 0
    for bit, m in enumerate(member):
        kind = kind + jnp.where((m == 0) | (m == 3), 1 << bit, 0)
        octant = 2 * octant + (m + 1) % 2
    place = atoms + (kind - 1) * (8 * ghosts) + octant * ghosts + entry % ghosts
    return jnp.where(neighbors < atoms, neighbors, place)


def on_device(
    positions,
    species,
    start_block,
    neighbors,
    ghost_lists,
    embedding,
    radial_in,
    radial_out,
    readout,
):
    atoms = positions.shape[-1]
    ghosts = ghost_lists.shape[-1]
    vectors = start_block.shape[3]
    fanout = neighbors.shape[3]
    channels = embedding.shape[1]
    devices = lax.axis_size("gx") * lax.axis_size("gy") * lax.axis_size("gz")
    scale = 1.0 / (3.0 * atoms * devices)
    width = 8 * ghosts
    high = 3 * GROUP
    edges = fanout * atoms
    table_width = atoms + 7 * width
    ring = lax.axis_size("gx") == 4
    side = (octant_bit((GROUP, width), 0, ghosts) ^ (lax.axis_index("gx") % 2 == 1)).astype(
        jnp.float32
    )

    inputs = (
        positions.transpose(0, 1, 3, 2, 4).reshape(3, 1, atoms),
        species,
        start_block.transpose(0, 1, 2, 4, 3, 5),
        ghost_lists,
    )
    own, octants, lists = call(
        pack_kernel,
        [(high, atoms), (high, width), ((1, width), jnp.int32)],
        inputs,
        [pltpu.VMEM(x.shape, x.dtype) for x in inputs]
        + [pltpu.SemaphoreType.DMA((len(inputs),))],
        spaces=pltpu.HBM,
    )
    basis, hidden = radial_in.shape
    index, low, inward, outward, columns = call(
        functools.partial(prepare_kernel, atoms, ghosts),
        [
            ((1, edges), jnp.int32),
            ((LANES, edges), jnp.bfloat16),
            ((hidden, LANES * (-(-6 * basis // LANES))), jnp.bfloat16),
            ((2 * channels, 2 * hidden), jnp.bfloat16),
            (channels, LANES),
        ],
        (neighbors.reshape(1, -1), embedding, radial_in, radial_out.T, readout.reshape(1, -1)),
        flops=2_000_000,
    )

    def spread(level):
        if level.shape[1] == width:
            level = jnp.concatenate([level, fetch_ghosts(level, 0, ghosts)], axis=1)
        return (level,) + spread_outer(level, ghosts)

    pairs = len(pair_list(fanout))
    shared = [
        (vectors * (fanout + pairs) * GROUP, atoms),
        ((fanout + pairs) * GROUP, atoms),
        (vectors * (fanout + pairs) * GROUP, atoms),
    ]
    base_sums = 2 * fanout + pairs + fanout * fanout
    saved_shapes = [
        (high, edges),
        (GROUP, edges),
        (GROUP * (-(-base_sums // 4)), atoms),
        (pairs * GROUP, atoms),
    ] + [(channels, edges)] * 5
    ghost_levels = spread(octants)
    results = call(
        functools.partial(first_kernel, ghosts, vectors, basis, embedding.shape[0]),
        [(high, table_width)] + saved_shapes,
        (index, own) + ghost_levels + (low, inward, outward, columns),
        [(high, table_width), (channels, edges), (channels, LANES)]
        + shared
        + [(base_sums * GROUP, atoms)],
    )
    terms, saved = results[0], results[1:]
    lifted = ring and lax.axis_size("gz") == 2

    def second_product(first, levels):
        return call(
            functools.partial(second_kernel, ghosts, vectors, len(levels)),
            [(high, table_width), (GROUP, LANES)],
            (index, first) + levels + (low,) + tuple(saved),
            [(high, table_width)] + shared,
        )

    if lifted:
        beyond = ghost_levels[2]

        def exchange(terms):
            other = lax.ppermute(terms, "gz", swap_pairs(2, 1))
            cut = [atoms + (kind - 1) * width for kind in range(9)]
            both = [
                x[:, cut[2] : cut[4]] + y[:, cut[6] : cut[8]]
                for x, y in ((terms, other), (other, terms))
            ]
            return other, return_ghosts(jnp.concatenate(both, axis=1), 1, ghosts)

        other, got = exchange(terms)
        part, packet = call(
            functools.partial(pair_start_kernel, vectors),
            [(high, atoms), (high, 4 * width)],
            (terms, other, got, lists, beyond),
            [(high, atoms)],
        )
        others = pair_exchange(packet, "gx", (1, 2, 3))
        first, level, gram = call(
            functools.partial(pair_merge_kernel, vectors, width),
            [(high, atoms), (high, 4 * width), (GROUP, LANES)],
            (side, part, packet, *others, own),
            [(6, high, atoms)],
        )
        terms, edge_gram = second_product(first, (level, fetch_ghosts(level, 1, ghosts)))
        gram = gram + jnp.roll(edge_gram, 3 * GROUP, axis=1)
        sent = jnp.concatenate([terms, jnp.pad(gram, ((0, high - GROUP), (0, 0)))], axis=1)
        other, got = exchange(sent)
        part, packet = call(
            functools.partial(pair_gram_start_kernel, vectors),
            [(high, atoms), (high, 4 * width + LANES)],
            (sent, other, got, lists, beyond, gram, other[:GROUP, table_width:]),
            [(high, atoms)],
        )
        others = pair_exchange(packet, "gx", (1, 2, 3))
        second, gram = call(
            functools.partial(pair_gram_merge_kernel, vectors, width),
            [(high, atoms), (GROUP, LANES)],
            (side, *others[:0:-1], part, packet, others[0]),
            [(8, high, atoms)],
        )
        gram = [sum_over(gram, AXES[1:2])]
    else:
        own_terms, ghost_terms = terms[:, :atoms], terms[:, atoms:]
        sums, beside = return_outer(ghost_terms, width, ghosts)
        if ring:
            part, packet = call(
                functools.partial(start_kernel, vectors),
                [(high, atoms), (high, 2 * width)],
                (own_terms, sums, beside, lists),
            )
            others = pair_exchange(packet, "gx", (1, 2, 3))
            first, level = call(
                functools.partial(merge_kernel, vectors),
                [(high, atoms), (high, 2 * width)],
                (side, part, packet, *others),
                [(high, atoms)],
            )
        else:
            first, level = call(
                functools.partial(middle_kernel, vectors),
                [(high, atoms), (high, width)],
                (own_terms, sums + return_ghosts(beside, 0, ghosts), lists),
            )
        terms, edge_gram = second_product(first, spread(level))
        own_terms, ghost_terms = terms[:, :atoms], terms[:, atoms:]
        sums, beside = return_outer(ghost_terms, width, ghosts)
        if ring:
            part, packet = call(
                functools.partial(gram_start_kernel, vectors),
                [(high, atoms), (high, 2 * width + LANES)],
                (own, first, own_terms, sums, beside, lists, edge_gram),
            )
            others = pair_exchange(packet, "gx", (1, 2, 3))
            second, gram = call(
                functools.partial(gram_merge_kernel, vectors),
                [(high, atoms), (GROUP, LANES)],
                (side, *others[:0:-1], part, packet, others[0]),
                [(high, atoms)],
            )
            gram = sum_across(gram)
        else:
            second, gram = call(
                functools.partial(gram_kernel, vectors),
                [(high, atoms), (GROUP, LANES)],
                (own, first, own_terms, sums + return_ghosts(beside, 0, ghosts), lists),
            )
            gram = [sum_over(gram, AXES)]
    shapes = [(1, 1, 1, 3, vectors, atoms), (2, vectors, vectors), (2, vectors, vectors)]
    following, diagonal, off = call(
        functools.partial(last_kernel, vectors, scale),
        shapes,
        (own, first, second, *gram),
        shapes + [pltpu.SemaphoreType.DMA((len(shapes),))],
        out_spaces=pltpu.HBM,
    )
    return following.transpose(0, 1, 2, 4, 3, 5), diagonal, off


def solution(mesh):
    return jax.shard_map(
        on_device,
        mesh=mesh,
        in_specs=(
            P("gx", "gy", "gz", None, None),
            P("gx", "gy", "gz", None),
            P("gx", "gy", "gz", None, None, None),
            P("gx", "gy", "gz", None, None),
            P("gx", "gy", "gz", None),
            P(),
            P(),
            P(),
            P(),
        ),
        out_specs=(P("gx", "gy", "gz", None, None, None), P(), P()),
        check_vma=False,
    )
```

```python
import functools
import math

import jax
import jax.numpy as jnp
import numpy as np
from jax import lax
from jax.experimental import pallas as pl
from jax.experimental.pallas import tpu as pltpu
from jax.sharding import PartitionSpec as P

SOFTEN = 0.25
CUTOFF = 4.0
HIGHEST = lax.Precision.HIGHEST
LANES = 128
GROUP = 8
AXES = ("gx", "gy", "gz")
VMEM_BYTES = 48 * 1024 * 1024


def swap_pairs(size, distance):
    return [(i, (i + distance) % size) for i in range(size)]


def octant_bit(shape, bit, ghosts):
    lane = lax.broadcasted_iota(jnp.int32, shape, 1) % (8 * ghosts)
    return (lane // ghosts // (4 >> bit)) % 2 == 1


def pair_exchange(x, axis, distances):
    size = lax.axis_size(axis)
    return [lax.ppermute(x, axis, [(i, i ^ d) for i in range(size)]) for d in distances]


def ring_sides(x, bit):
    axis = AXES[bit]
    size = lax.axis_size(axis)
    if size == 4:
        near, far = pair_exchange(x, axis, (1, 3))
        return near, far, lax.axis_index(axis) % 2 == 1
    above = lax.ppermute(x, axis, swap_pairs(size, -1))
    below = lax.ppermute(x, axis, swap_pairs(size, 1))
    return above, below, False


def fetch_ghosts(x, bit, ghosts):
    axis = AXES[bit]
    size = lax.axis_size(axis)
    if size == 1:
        return x
    if size == 2:
        return lax.ppermute(x, axis, swap_pairs(2, 1))
    near, far, odd = ring_sides(x, bit)
    return jnp.where(octant_bit(x.shape, bit, ghosts) ^ odd, far, near)


def return_ghosts(x, bit, ghosts):
    axis = AXES[bit]
    size = lax.axis_size(axis)
    if size == 1:
        return x
    if size == 2:
        return lax.ppermute(x, axis, swap_pairs(2, 1))
    near, far, odd = ring_sides(x, bit)
    return jnp.where(octant_bit(x.shape, bit, ghosts) == odd, far, near)


def spread_outer(level, ghosts):
    second = fetch_ghosts(level, 1, ghosts)
    level = jnp.concatenate([level, second], axis=1)
    return second, fetch_ghosts(level, 2, ghosts)


def return_outer(terms, width, ghosts):
    got = return_ghosts(terms[:, 3 * width :], 2, ghosts)
    inner = got[:, :width]
    first = terms[:, :width] + got[:, width : 2 * width]
    second = terms[:, width : 3 * width] + got[:, 2 * width :]
    got = return_ghosts(second, 1, ghosts)
    return inner + got[:, :width], first + got[:, width:]


def sum_over(x, axes):
    for axis in axes:
        size = lax.axis_size(axis)
        if size & (size - 1):
            x = lax.psum(x, axis)
            continue
        step = 1
        while step < size:
            x = x + lax.ppermute(x, axis, [(i, i ^ step) for i in range(size)])
            step *= 2
    return x


def sum_across(x):
    axes = AXES[1:]
    sizes = [lax.axis_size(axis) for axis in axes]
    if sizes != [4, 2]:
        return [sum_over(x, axes)]
    x = x + pair_exchange(x, axes[0], (1,))[0]
    count = sizes[0] * sizes[1]
    terms = [
        lax.ppermute(x, axes, [(i, i ^ d) for i in range(count)])
        for d in (2 * sizes[1], 1, 2 * sizes[1] + 1)
    ]
    return [x] + terms


def rows(a):
    return slice(GROUP * a, GROUP * (a + 1))


def gather_lanes(table, index_row, group):
    lane = jnp.broadcast_to(index_row % LANES, (GROUP, LANES))
    tile = jnp.broadcast_to(index_row // LANES, (GROUP, LANES))
    out = None
    for number in range(table.shape[1] // LANES):
        source = table[rows(group), number * LANES : (number + 1) * LANES]
        picked = jnp.take_along_axis(source, lane, axis=1, mode="promise_in_bounds")
        out = picked if out is None else jnp.where(tile == number, picked, out)
    return out


def column(line):
    size = line.shape[1]
    shape = (size, size)
    same = lax.broadcasted_iota(jnp.int32, shape, 0) == lax.broadcasted_iota(jnp.int32, shape, 1)
    return jnp.sum(jnp.where(same, line, 0.0), axis=1, keepdims=True)


def split_rows(y, vectors):
    high = y.astype(jnp.bfloat16).astype(jnp.float32)
    return high + pltpu.roll(y - high, vectors, 0)


def join_rows(y, vectors):
    return y + pltpu.roll(y, GROUP - vectors, 0)


def pack_rows(values, vectors):
    row = lax.broadcasted_iota(jnp.int32, values[0].shape, 0)
    return jnp.where(row < vectors, values[0], pltpu.roll(values[1], vectors, 0)), values[2]


def unpack_rows(ref, lanes, vectors):
    both = ref[rows(0), lanes]
    return [both, pltpu.roll(both, GROUP - vectors, 0), ref[rows(1), lanes]]


def pack_kernel(vectors, own_ref, oct_ref, list_ref):
    mark = vectors + 2
    width = oct_ref.shape[1]
    list_ref[...] = own_ref[mark : mark + 1, :width].astype(jnp.int32)
    pick_octants(own_ref, list_ref, oct_ref)
    row = lax.broadcasted_iota(jnp.int32, (GROUP, width), 0)
    oct_ref[rows(0), :] = jnp.where(
        row == mark, own_ref[mark : mark + 1, :width], oct_ref[rows(0), :]
    )


def prepare_kernel(
    atoms, ghosts, near_ref, emb_ref, rin_ref, rout_ref, read_ref, idx_ref, low_ref, in_ref, out_ref, col_ref
):
    index = table_index(near_ref[...], atoms, ghosts)
    idx_ref[...] = index
    low = lax.broadcasted_iota(jnp.int32, low_ref.shape, 0) == index % LANES
    low_ref[...] = jnp.where(low, 1.0, 0.0).astype(jnp.bfloat16)
    high, middle, rest = split_parts(rin_ref[...])
    stack = [high, middle, rest, high, middle, high]
    pad = in_ref.shape[1] - 6 * rin_ref.shape[0]
    stack = jnp.concatenate(stack + [jnp.zeros((pad, rin_ref.shape[1]), jnp.float32)], axis=0)
    in_ref[...] = jnp.transpose(stack).astype(jnp.bfloat16)
    high, rest, _ = split_parts(rout_ref[...])
    out_ref[...] = jnp.concatenate(
        [jnp.concatenate([high, high], axis=1), jnp.concatenate([rest, rest], axis=1)], axis=0
    ).astype(jnp.bfloat16)
    species = emb_ref.shape[0]
    lane = lax.broadcasted_iota(jnp.int32, col_ref.shape, 1)
    columns = jnp.broadcast_to(column(read_ref[...]), col_ref.shape)
    for n in range(species):
        columns = jnp.where(lane == n, column(emb_ref[n : n + 1, :]), columns)
    col_ref[...] = columns


def pick_octants(own_ref, list_ref, oct_ref):
    for j in range(list_ref.shape[1] // LANES):
        cut = slice(j * LANES, (j + 1) * LANES)
        for a in range(3):
            oct_ref[rows(a), cut] = gather_lanes(own_ref, list_ref[:, cut], a)


def add_octants(own, octants, lists, vectors):
    atoms = own.shape[1]
    width = lists.shape[1]
    keep = lax.broadcasted_iota(jnp.int32, octants.shape, 0) < vectors
    packed = split_rows(jnp.where(keep, octants, 0.0), vectors).astype(jnp.bfloat16)
    onehot = lax.broadcasted_iota(jnp.int32, (atoms, width), 0) == lists
    spread = lax.dot_general(
        packed,
        jnp.where(onehot, 1.0, 0.0).astype(jnp.bfloat16),
        (((1,), (1,)), ((), ())),
        preferred_element_type=jnp.float32,
    )
    return own + join_rows(spread, vectors)


def fill_table(table, own_ref, ghost_refs, vectors, ghosts, shifted):
    atoms = own_ref.shape[1]
    table[:, :atoms] = own_ref[...]
    width = 8 * ghosts
    places = [
        (ref, j * width) for ref in ghost_refs for j in range(ref.shape[1] // width)
    ]
    if len(ghost_refs) == 2:
        places = [places[n] for n in (0, 1, 4, 5, 2, 3, 6, 7)]
    for kind, (ref, start) in enumerate(places):
        if kind == 0:
            continue
        base = atoms + (kind - 1) * width
        if len(ghost_refs) == 2:
            for a, part in enumerate(unpack_rows(ref, slice(start, start + width), vectors)):
                table[rows(a), base : base + width] = part
            continue
        part = ref[:, start : start + width]
        if shifted:
            row = lax.broadcasted_iota(jnp.int32, part.shape, 0)
            for a in range(3):
                if (kind >> a) & 1:
                    move = jnp.where(octant_bit(part.shape, a, ghosts), -1.0, 1.0)
                    part = part + jnp.where(row == GROUP * a + vectors, move, 0.0)
        table[:, base : base + width] = part


def gather_slot(table, idx_ref, k, atoms):
    pieces = [[] for _ in range(3)]
    for j in range(atoms // LANES):
        index_row = idx_ref[:, pl.ds(pl.multiple_of(k * atoms + j * LANES, LANES), LANES)]
        for a in range(3):
            pieces[a].append(gather_lanes(table, index_row, a))
    return [jnp.concatenate(p, axis=1) for p in pieces]


def pair_list(fanout):
    return [(k, l) for k in range(fanout) for l in range(k, fanout)]


def lookup(table, fanout):
    where = {pair: n for n, pair in enumerate(pair_list(fanout))}
    return lambda k, l: table[where[min(k, l), max(k, l)]]


def sum_rows(parts):
    row = lax.broadcasted_iota(jnp.int32, parts[0].shape, 0)
    if len(parts) != 4 or GROUP != 8:
        out = jnp.zeros_like(parts[0])
        for n, part in enumerate(parts):
            out = jnp.where(row == n, jnp.sum(part, axis=0, keepdims=True), out)
        return out
    fold = [part + pltpu.roll(part, 4, 0) for part in parts]
    low = row < 4
    lead = jnp.where(low, fold[0], fold[1])
    rest = jnp.where(low, fold[2], fold[3])
    both = jnp.where(row % 4 < 2, lead + pltpu.roll(lead, 6, 0), rest + pltpu.roll(rest, 2, 0))
    even = both + pltpu.roll(both, 7, 0)
    odd = both + pltpu.roll(both, 1, 0)
    return jnp.where(row % 2 == 1, pltpu.roll(odd, 4, 0), even)


def dot3(x, y):
    return x[0] * y[0] + x[1] * y[1] + x[2] * y[2]


def slot_cut(k, atoms):
    return slice(k * atoms, (k + 1) * atoms)


def tile_rows(n):
    return slice(GROUP * n, GROUP * (n + 1))


def tangents(diffs, units, invs, tn, changes, vectors):
    fanout = len(diffs)
    pairs = pair_list(fanout)
    per_vector = fanout + len(pairs)
    taus = [dot3(units[k], diffs[k]) for k in range(fanout)]
    turns = [
        [(diffs[k][a] - units[k][a] * taus[k]) * invs[k] for a in range(3)] for k in range(fanout)
    ]
    values = list(taus)
    for k, l in pairs:
        half = dot3(units[k], turns[l])
        values.append(2.0 * half if k == l else half + dot3(units[l], turns[k]))
    for n, value in enumerate(values):
        changes[tile_rows(n), :] = value
        for v in range(vectors):
            tn[tile_rows(v * per_vector + n), :] = jnp.broadcast_to(
                value[v : v + 1, :], value.shape
            )


def channel_products(f, f1, q, rp, rpp, cosine, tn, acc, lanes, fanout, vectors):
    pairs = pair_list(fanout)
    per_vector = fanout + len(pairs)
    slots = range(fanout)
    rpp_q = [rpp[k] * q[k] for k in slots]
    rpp_f = [rpp[k] * f[k] for k in slots]
    for v in range(vectors):
        base = v * per_vector

        def tangent(n):
            return tn[tile_rows(base + n), lanes]

        phi = [f1[k] * tangent(k) for k in slots]
        index = {pair: fanout + n for n, pair in enumerate(pairs)}
        dq = []
        for k in slots:
            total = None
            for l in slots:
                term = phi[l] * cosine(k, l) + f[l] * tangent(index[min(k, l), max(k, l)])
                total = term if total is None else total + term
            dq.append(total)
        y = [phi[k] * rpp_q[k] + dq[k] * rpp_f[k] for k in slots]
        w = [y[k] * f[k] + rp[k] * phi[k] for k in slots]
        for k in slots:
            total = y[k] * q[k] + rp[k] * dq[k]
            for l in slots:
                total = total + w[l] * cosine(k, l)
            acc[tile_rows(base + k), lanes] += f1[k] * total
        for n, (k, l) in enumerate(pairs):
            term = w[k] * f[l] if k == l else w[k] * f[l] + w[l] * f[k]
            acc[tile_rows(base + fanout + n), lanes] += term


def finish_product(
    idx_ref, low_ref, unit_ref, inv_ref, sums_ref, acc, changes, diffs, terms_out, vectors
):
    fanout = len(diffs)
    atoms = idx_ref.shape[1] // fanout
    tiles = terms_out.shape[1] // LANES
    pairs = pair_list(fanout)
    per_vector = fanout + len(pairs)
    slots = range(fanout)
    row = lax.broadcasted_iota(jnp.int32, (GROUP, atoms), 0)
    outs = [
        sum_rows([acc[tile_rows(v * per_vector + n), :] for v in range(vectors)])
        for n in range(per_vector)
    ]
    taus = [changes[tile_rows(k), :] for k in slots]
    turned = lookup([changes[tile_rows(fanout + n), :] for n in range(len(pairs))], fanout)
    bent = lookup(outs[fanout:], fanout)
    units = [[unit_ref[rows(a), slot_cut(k, atoms)] for a in range(3)] for k in slots]
    invs = [inv_ref[:, slot_cut(k, atoms)] for k in slots]
    turns = [
        [(diffs[k][a] - units[k][a] * taus[k]) * invs[k] for a in range(3)] for k in slots
    ]

    def base_sum(n):
        line = (n // 4) * GROUP + n % 4
        return sums_ref[line : line + 1, :]

    stretch = [base_sum(k) for k in slots]
    curve = [base_sum(fanout + k) for k in slots]
    weight = lookup([base_sum(2 * fanout + n) for n in range(len(pairs))], fanout)
    mixed = [[base_sum(2 * fanout + len(pairs) + k * fanout + l) for l in slots] for k in slots]
    center = [jnp.zeros((GROUP, atoms), jnp.float32) for _ in range(3)]
    shifted = [jnp.zeros((GROUP, atoms), jnp.float32) for _ in range(vectors)]
    left = []
    for k in slots:
        along = outs[k] + curve[k] * taus[k]
        force = [0.0, 0.0, 0.0]
        change = [0.0, 0.0, 0.0]
        for l in slots:
            along = along + turned(k, l) * mixed[k][l]
            bend = bent(k, l) + taus[l] * mixed[l][k] + taus[k] * mixed[k][l]
            pull = weight(k, l)
            if k == l:
                bend = bend + bent(k, l)
                pull = pull + pull
            for a in range(3):
                force[a] = force[a] + pull * units[l][a]
                change[a] = change[a] + bend * units[l][a] + pull * turns[l][a]
        flat = dot3(units[k], force)
        inv = invs[k]
        along = (
            along
            - (dot3(units[k], change) + dot3(turns[k], force)) * inv
            + taus[k] * flat * (inv * inv)
        )
        keep = stretch[k] - flat * inv
        packed = []
        for a in range(3):
            y = (
                along * units[k][a]
                + keep * turns[k][a]
                + (change[a] - taus[k] * inv * force[a]) * inv
            )
            y = jnp.where(row < vectors, y, 0.0)
            center[a] = center[a] - y
            for n in range(vectors):
                other = y if n == 0 else pltpu.roll(y, n, 0)
                if n:
                    other = other + pltpu.roll(y, GROUP - vectors + n, 0)
                shifted[n] = shifted[n] + other * diffs[k][a]
            packed.append(split_rows(y, vectors))
        packed = jnp.concatenate(packed, axis=0)
        tile = idx_ref[:, slot_cut(k, atoms)] // LANES
        left.append(
            jnp.concatenate(
                [jnp.where(tile == number, packed, 0.0) for number in range(tiles)], axis=0
            ).astype(jnp.bfloat16)
        )
    spread = lax.dot_general(
        jnp.concatenate(left, axis=1),
        low_ref[...],
        (((1,), (1,)), ((), ())),
        preferred_element_type=jnp.float32,
    )
    own_tiles = atoms // LANES
    for number in range(tiles):
        cut = slice(number * LANES, (number + 1) * LANES)
        values = []
        for a in range(3):
            value = join_rows(spread[tile_rows(number * 3 + a)], vectors)
            if number < own_tiles:
                value = value + center[a][:, cut]
            values.append(value)
        terms_out[rows(0), cut], terms_out[rows(1), cut] = pack_rows(values, vectors)
    return shifted


def split_parts(x):
    high = x.astype(jnp.bfloat16).astype(jnp.float32)
    rest = x - high
    middle = rest.astype(jnp.bfloat16).astype(jnp.float32)
    low = (rest - middle).astype(jnp.bfloat16).astype(jnp.float32)
    return high, middle, low


def silu_slopes(x):
    sig = 0.5 + 0.5 * jnp.tanh(0.5 * x)
    anti = 1.0 - sig
    return sig, sig * (1.0 + x * anti), sig * anti * (2.0 + x * (anti - sig))


def half_turns(dist, inv, basis):
    shape = (basis, dist.shape[1])
    order = (lax.broadcasted_iota(jnp.int32, shape, 0) + 1).astype(jnp.float32)
    turns = order * (dist * (1.0 / CUTOFF))
    whole = jnp.floor(turns + 0.5)
    sign = 1.0 - 2.0 * (whole - 2.0 * jnp.floor(whole * 0.5))
    x = (turns - whole) * np.float32(np.pi)
    x2 = x * x

    def series(terms):
        value = terms[-1]
        for term in terms[-2::-1]:
            value = term + x2 * value
        return value

    sine = sign * x * series([(-1.0) ** n / math.factorial(2 * n + 1) for n in range(6)])
    cosine = sign * series([(-1.0) ** n / math.factorial(2 * n) for n in range(7)])
    omega = order * np.float32(np.pi / CUTOFF)
    b0 = sine * inv
    b1 = (omega * cosine - b0) * inv
    b2 = -(omega * omega * sine + 2.0 * b1) * inv
    return jnp.concatenate([b0, b1, b2], axis=1)


def first_kernel(
    ghosts,
    vectors,
    basis,
    species,
    idx_ref,
    own_ref,
    g1_ref,
    g2_ref,
    g3_ref,
    low_ref,
    in_ref,
    out_ref,
    col_ref,
    terms_out,
    unit_ref,
    inv_ref,
    sums_ref,
    cos_ref,
    f_ref,
    f1_ref,
    q_ref,
    rp_ref,
    rpp_ref,
    table,
    f2_ref,
    read_col,
    tn,
    changes,
    acc,
    acc2,
):
    atoms = own_ref.shape[1]
    fanout = idx_ref.shape[1] // atoms
    channels = col_ref.shape[0]
    pairs = pair_list(fanout)
    slots = range(fanout)
    embeds = [col_ref[:, n : n + 1] for n in range(species)]
    read_col[...] = jnp.broadcast_to(col_ref[:, species : species + 1], read_col.shape)
    fill_table(table, own_ref, (g1_ref, g2_ref, g3_ref), vectors, ghosts, True)

    def embed(kind):
        value = embeds[0]
        for n in range(1, species):
            value = jnp.where(kind == float(n), embeds[n], value)
        return value

    own_embed = embed(own_ref[vectors + 1 : vectors + 2, :])
    inward = in_ref[:, : 6 * basis]
    outward = out_ref[...]
    diffs, units, invs = [], [], []
    for k in slots:
        cut = slot_cut(k, atoms)
        near = gather_slot(table, idx_ref, k, atoms)
        diff = [near[a] - own_ref[rows(a), :] for a in range(3)]
        delta = [
            jnp.broadcast_to(diff[a][vectors : vectors + 1, :], (GROUP, atoms)) for a in range(3)
        ]
        dist = jnp.sqrt(dot3(delta, delta) + SOFTEN)
        inv = 1.0 / dist
        unit = [delta[a] * inv for a in range(3)]
        for a in range(3):
            unit_ref[rows(a), cut] = unit[a]
        inv_ref[:, cut] = inv
        diffs.append(diff)
        units.append(unit)
        invs.append(inv)
        one = dist[0:1]
        radii = half_turns(one, inv[0:1], basis)
        high, middle, rest = split_parts(radii)
        z = jnp.dot(
            inward,
            jnp.concatenate([high, high, high, middle, middle, rest], axis=0).astype(jnp.bfloat16),
            preferred_element_type=jnp.float32,
        )
        z0, z1, z2 = z[:, :atoms], z[:, atoms : 2 * atoms], z[:, 2 * atoms :]
        sig, slope, curve = silu_slopes(z0)
        hidden = jnp.concatenate([z0 * sig, slope * z1, curve * z1 * z1 + slope * z2], axis=1)
        high = hidden.astype(jnp.bfloat16)
        rest = (hidden - high.astype(jnp.float32)).astype(jnp.bfloat16)
        radial = jnp.dot(
            outward, jnp.concatenate([high, rest], axis=0), preferred_element_type=jnp.float32
        )
        radial = radial[:channels] + radial[channels:]
        r0, r1, r2 = radial[:, :atoms], radial[:, atoms : 2 * atoms], radial[:, 2 * atoms :]
        square = one * one
        base = 1.0 - square * (1.0 / CUTOFF**2)
        v0 = base * base
        v1 = base * one * (-4.0 / CUTOFF**2)
        v2 = -4.0 / CUTOFF**2 + square * (12.0 / CUTOFF**4)
        pair = own_embed * embed(near[0][vectors + 1 : vectors + 2, :])
        f_ref[:, cut] = pair * (r0 * v0)
        f1_ref[:, cut] = pair * (r1 * v0 + r0 * v1)
        f2_ref[:, cut] = pair * (r2 * v0 + 2.0 * (r1 * v1) + r0 * v2)
    for n, (k, l) in enumerate(pairs):
        cos_ref[tile_rows(n), :] = 1.0 + dot3(units[k], units[l])
    tangents(diffs, units, invs, tn, changes, vectors)
    acc[...] = jnp.zeros_like(acc)
    acc2[...] = jnp.zeros_like(acc2)
    share = 1.0 / fanout

    def tile(number, carry):
        here = pl.ds(pl.multiple_of(number * GROUP, GROUP), GROUP)
        for half in range(atoms // LANES):
            lanes = slice(half * LANES, (half + 1) * LANES)
            cuts = [slice(k * atoms + half * LANES, k * atoms + (half + 1) * LANES) for k in slots]
            cosine = lookup([cos_ref[tile_rows(n), lanes] for n in range(len(pairs))], fanout)
            f = [f_ref[here, cut] for cut in cuts]
            f1 = [f1_ref[here, cut] for cut in cuts]
            read = read_col[here, :] * share
            q, rp, rpp = [], [], []
            for k in slots:
                project = sum(f[l] * cosine(k, l) for l in slots)
                _, slope, curve = silu_slopes(f[k] * project * share)
                q.append(project)
                rp.append(read * slope)
                rpp.append(read * share * curve)
                q_ref[here, cuts[k]] = q[k]
                rp_ref[here, cuts[k]] = rp[k]
                rpp_ref[here, cuts[k]] = rpp[k]
            m = [rp[k] * f[k] for k in slots]
            slope = [rp[k] * q[k] + sum(m[l] * cosine(k, l) for l in slots) for k in slots]
            terms = [slope[k] * f1[k] for k in slots]
            terms += [slope[k] * f2_ref[here, cuts[k]] for k in slots]
            terms += [m[k] * f[l] if k == l else m[k] * f[l] + m[l] * f[k] for k, l in pairs]
            terms += [f1[k] * m[l] for k in slots for l in slots]
            for n, term in enumerate(terms):
                acc2[tile_rows(n), lanes] += term
            channel_products(f, f1, q, rp, rpp, cosine, tn, acc, lanes, fanout, vectors)
        return carry

    lax.fori_loop(0, channels // GROUP, tile, 0)
    count = acc2.shape[0] // GROUP
    for n in range(0, count, 4):
        parts = [acc2[tile_rows(min(n + j, count - 1)), :] for j in range(4)]
        sums_ref[tile_rows(n // 4), :] = sum_rows(parts)
    finish_product(
        idx_ref,
        low_ref,
        unit_ref,
        inv_ref,
        sums_ref,
        acc,
        changes,
        diffs,
        terms_out,
        vectors,
    )


def second_kernel(ghosts, vectors, levels, idx_ref, own_ref, *refs):
    ghost_refs, refs = refs[:levels], refs[levels:]
    low_ref, unit_ref, inv_ref, sums_ref, cos_ref, f_ref, f1_ref, q_ref, rp_ref, rpp_ref = refs[:10]
    terms_out, gram_out, table, tn, changes, acc = refs[10:]
    atoms = own_ref.shape[1]
    fanout = idx_ref.shape[1] // atoms
    channels = f_ref.shape[0]
    pairs = pair_list(fanout)
    slots = range(fanout)
    fill_table(table, own_ref, ghost_refs, vectors, ghosts, False)
    diffs = []
    for k in slots:
        near = gather_slot(table, idx_ref, k, atoms)
        diffs.append([near[a] - own_ref[rows(a), :] for a in range(3)])
    units = [[unit_ref[rows(a), slot_cut(k, atoms)] for a in range(3)] for k in slots]
    invs = [inv_ref[:, slot_cut(k, atoms)] for k in slots]
    tangents(diffs, units, invs, tn, changes, vectors)
    acc[...] = jnp.zeros_like(acc)

    def tile(number, carry):
        here = pl.ds(pl.multiple_of(number * GROUP, GROUP), GROUP)
        for half in range(atoms // LANES):
            lanes = slice(half * LANES, (half + 1) * LANES)
            cuts = [slice(k * atoms + half * LANES, k * atoms + (half + 1) * LANES) for k in slots]
            cosine = lookup([cos_ref[tile_rows(n), lanes] for n in range(len(pairs))], fanout)
            parts = [
                [ref[here, cut] for cut in cuts] for ref in (f_ref, f1_ref, q_ref, rp_ref, rpp_ref)
            ]
            channel_products(*parts, cosine, tn, acc, lanes, fanout, vectors)
        return carry

    lax.fori_loop(0, channels // GROUP, tile, 0)
    shifted = finish_product(
        idx_ref,
        low_ref,
        unit_ref,
        inv_ref,
        sums_ref,
        acc,
        changes,
        diffs,
        terms_out,
        vectors,
    )
    gram_out[...] = from_shifted(shifted, vectors)


def middle_kernel(vectors, own_ref, sums_ref, list_ref, full_ref, oct_ref):
    for a in range(3):
        full_ref[rows(a), :] = add_octants(
            own_ref[rows(a), :], sums_ref[rows(a), :], list_ref[...], vectors
        )
    pick_octants(full_ref, list_ref, oct_ref)


def inner(x, y, pad_to=LANES):
    pad = jnp.zeros((pad_to - y.shape[0], y.shape[1]), jnp.float32)
    return lax.dot_general(
        x,
        jnp.concatenate([y, pad], axis=0),
        (((1,), (1,)), ((), ())),
        precision=HIGHEST,
        preferred_element_type=jnp.float32,
    )


def only_vectors(x, vectors):
    row = lax.broadcasted_iota(jnp.int32, x.shape, 0)
    return jnp.where(row % GROUP < vectors, x, 0.0)


def pack_gram(total, edge):
    lane = lax.broadcasted_iota(jnp.int32, (GROUP, LANES), 1)
    out = total[rows(0)]
    out = jnp.where(lane >= 2 * GROUP, pltpu.roll(total[rows(1)], GROUP, 1), out)
    if edge is not None:
        out = jnp.where(lane >= 3 * GROUP, pltpu.roll(edge, 3 * GROUP, 1), out)
    return jnp.where(lane >= 4 * GROUP, pltpu.roll(total[rows(2)], 2 * GROUP, 1), out)


def gram_kernel(vectors, start_ref, first_ref, own_ref, sums_ref, list_ref, full_ref, gram_ref):
    total = jnp.zeros((3 * GROUP, LANES), jnp.float32)
    for a in range(3):
        second = add_octants(own_ref[rows(a), :], sums_ref[rows(a), :], list_ref[...], vectors)
        full_ref[rows(a), :] = second
        stack = jnp.concatenate([start_ref[rows(a), :], first_ref[rows(a), :], second], axis=0)
        stack = only_vectors(stack, vectors)
        total += inner(stack, stack)
    gram_ref[...] = pack_gram(total, None)


def packet_start(vectors, own_ref, sums_ref, ghost_ref, list_ref, part_ref, packet_ref):
    width = list_ref.shape[1]
    for a in range(3):
        part_ref[rows(a), :] = add_octants(
            own_ref[rows(a), :], sums_ref[rows(a), :], list_ref[...], vectors
        )
    mark = vectors + 1
    for j in range(width // LANES):
        cut = slice(j * LANES, (j + 1) * LANES)
        for a in range(3):
            value = gather_lanes(part_ref, list_ref[:, cut], a)
            if a == 0:
                row = lax.broadcasted_iota(jnp.int32, value.shape, 0)
                value = jnp.where(row == mark, list_ref[:, cut].astype(jnp.float32), value)
            packet_ref[rows(a), cut] = value
    packet_ref[:, width : 2 * width] = ghost_ref[...]


def arriving(side, packets, n, a, width):
    cut = slice(width, 2 * width)
    after, before = packets[(n + 1) % 4], packets[(n + 3) % 4]
    return jnp.where(side > 0.5, after[rows(a), cut], before[rows(a), cut])


def packet_lists(packet, vectors, width):
    mark = vectors + 1
    return packet[mark : mark + 1, :width].astype(jnp.int32)


def start_kernel(vectors, own_ref, sums_ref, ghost_ref, list_ref, part_ref, packet_ref):
    packet_start(vectors, own_ref, sums_ref, ghost_ref, list_ref, part_ref, packet_ref)


def merge_kernel(
    vectors, side_ref, part_ref, p0_ref, p1_ref, p2_ref, p3_ref, full_ref, level_ref, spread
):
    width = p0_ref.shape[1] // 2
    side = side_ref[...]
    packets = (p0_ref, p1_ref, p2_ref, p3_ref)
    lists = [packet_lists(p, vectors, width) for p in packets]
    for a in range(3):
        full_ref[rows(a), :] = add_octants(
            part_ref[rows(a), :], arriving(side, packets, 0, a, width), lists[0], vectors
        )
    near = []
    for n in (1, 3):
        for a in range(3):
            zero = jnp.zeros((GROUP, part_ref.shape[1]), jnp.float32)
            spread[rows(a), :] = add_octants(
                zero, arriving(side, packets, n, a, width), lists[n], vectors
            )
        values = []
        for a in range(3):
            pieces = [
                gather_lanes(spread, lists[n][:, j * LANES : (j + 1) * LANES], a)
                for j in range(width // LANES)
            ]
            values.append(packets[n][rows(a), :width] + jnp.concatenate(pieces, axis=1))
        near.append(values)
    for a in range(3):
        for j in range(width // LANES):
            cut = slice(j * LANES, (j + 1) * LANES)
            level_ref[rows(a), cut] = gather_lanes(full_ref, lists[0][:, cut], a)
        level_ref[rows(a), width : 2 * width] = jnp.where(side > 0.5, near[1][a], near[0][a])


def gram_start_kernel(
    vectors,
    start_ref,
    first_ref,
    own_ref,
    sums_ref,
    ghost_ref,
    list_ref,
    edge_ref,
    part_ref,
    packet_ref,
):
    packet_start(vectors, own_ref, sums_ref, ghost_ref, list_ref, part_ref, packet_ref)
    width = list_ref.shape[1]
    total = jnp.zeros((3 * GROUP, LANES), jnp.float32)
    for a in range(3):
        stack = jnp.concatenate(
            [start_ref[rows(a), :], first_ref[rows(a), :], part_ref[rows(a), :]], axis=0
        )
        stack = only_vectors(stack, vectors)
        total += inner(stack, stack)
    cut = slice(2 * width, 2 * width + LANES)
    packet_ref[rows(0), cut] = pack_gram(total, edge_ref[...])
    packet_ref[GROUP : 3 * GROUP, cut] = jnp.zeros((2 * GROUP, LANES), jnp.float32)


def shifted_products(x, y, vectors):
    return [x * (pltpu.roll(y, n, 0) if n else y) for n in range(vectors)]


def from_shifted(shifted, vectors):
    shape = (GROUP, LANES)
    row = lax.broadcasted_iota(jnp.int32, shape, 0)
    lane = lax.broadcasted_iota(jnp.int32, shape, 1)
    total = jnp.zeros(shape, jnp.float32)
    for n in range(vectors):
        value = jnp.sum(shifted[n], axis=1, keepdims=True)
        total = jnp.where(lane == (row + vectors - n) % vectors, value, total)
    return jnp.where((row < vectors) & (lane < vectors), total, 0.0)


def gram_merge_kernel(
    vectors, side_ref, p3_ref, p2_ref, part_ref, p0_ref, p1_ref, full_ref, gram_ref, spread
):
    width = (p0_ref.shape[1] - LANES) // 2
    atoms = part_ref.shape[1]
    side = side_ref[...]
    packets = (p0_ref, p1_ref, p2_ref, p3_ref)
    shares = []
    for n in range(4):
        lists = packet_lists(packets[n], vectors, width)
        terms = [only_vectors(arriving(side, packets, n, a, width), vectors) for a in range(3)]
        packed = jnp.concatenate([split_rows(t, vectors) for t in terms], axis=0)
        onehot = lax.broadcasted_iota(jnp.int32, (atoms, width), 0) == lists
        placed = lax.dot_general(
            packed.astype(jnp.bfloat16),
            jnp.where(onehot, 1.0, 0.0).astype(jnp.bfloat16),
            (((1,), (1,)), ((), ())),
            preferred_element_type=jnp.float32,
        )
        total = None
        for a in range(3):
            value = join_rows(placed[rows(a)], vectors)
            spread[rows(a), :] = value
            if n == 0:
                full_ref[rows(a), :] = part_ref[rows(a), :] + value
            at = only_vectors(packets[n][rows(a), :width], vectors)
            at = at + pltpu.roll(at, vectors, 0)
            back = jnp.concatenate(
                [
                    gather_lanes(spread, lists[:, j * LANES : (j + 1) * LANES], a)
                    for j in range(width // LANES)
                ],
                axis=1,
            )
            found = shifted_products(terms[a], at + at + back, vectors)
            total = found if total is None else [x + y for x, y in zip(total, found)]
        shares.append([packets[n][rows(0), 2 * width : 2 * width + LANES]] + total)

    def add(x, y):
        return [p + q for p, q in zip(x, y)]

    total = add(add(shares[0], shares[1]), add(shares[2], shares[3]))
    gram_ref[...] = total[0] + pltpu.roll(from_shifted(total[1:], vectors), 4 * GROUP, 1)


def pair_sums(mine, other, got, width, atoms, vectors):
    def tile(ref, kind):
        start = atoms + (kind - 1) * width
        return ref[:, start : start + width]

    def back(n):
        return got[:, n * width : (n + 1) * width]

    def pick(first, second, n):
        return (
            unpack_rows(first, slice(0, atoms), vectors),
            tile(second, 4) + back(n),
            tile(first, 1) + tile(second, 5) + back(n + 1),
        )

    return pick(mine, other, 0), pick(other, mine, 2)


def pair_packet(vectors, mine, other, got, lists, parts, packet, width):
    atoms = parts[0].shape[1]
    for n, (own, sums, beside) in enumerate(pair_sums(mine, other, got, width, atoms, vectors)):
        base = 2 * n * width
        for a, value in enumerate(unpack_rows(sums, slice(0, width), vectors)):
            parts[n][rows(a), :] = add_octants(own[a], value, lists[n], vectors)
        packet[:, base + width : base + 2 * width] = beside
        first, last = pack_rows([read_back(parts[n], lists[n], a) for a in range(3)], vectors)
        row = lax.broadcasted_iota(jnp.int32, last.shape, 0)
        packet[rows(0), base : base + width] = first
        packet[rows(1), base : base + width] = jnp.where(
            row == vectors, lists[n].astype(jnp.float32), last
        )


def pair_lists(vectors, list_ref, beyond_ref):
    row = vectors + 2
    width = list_ref.shape[1]
    return list_ref[...], beyond_ref[row : row + 1, :width].astype(jnp.int32)


def pair_start_kernel(
    vectors, mine, other, got, list_ref, beyond_ref, part_ref, packet_ref, beyond_part
):
    pair_packet(
        vectors,
        mine,
        other,
        got,
        pair_lists(vectors, list_ref, beyond_ref),
        (part_ref, beyond_part),
        packet_ref,
        list_ref.shape[1],
    )


def placed_terms(side, packets, n, half, lists, atoms, width, vectors):
    start = (2 * half + 1) * width
    after, before = packets[(n + 1) % 4], packets[(n + 3) % 4]
    cut = slice(start, start + width)
    arrived = jnp.where(
        jnp.concatenate([side, side], axis=0) > 0.5, after[:, cut], before[:, cut]
    )
    terms = [
        only_vectors(t, vectors) for t in unpack_rows(arrived, slice(0, width), vectors)
    ]
    packed = jnp.concatenate([split_rows(t, vectors) for t in terms], axis=0)
    onehot = lax.broadcasted_iota(jnp.int32, (atoms, width), 0) == lists
    placed = lax.dot_general(
        packed.astype(jnp.bfloat16),
        jnp.where(onehot, 1.0, 0.0).astype(jnp.bfloat16),
        (((1,), (1,)), ((), ())),
        preferred_element_type=jnp.float32,
    )
    return terms, [join_rows(placed[rows(a)], vectors) for a in range(3)]


def read_back(ref, lists, a):
    pieces = [
        gather_lanes(ref, lists[:, j * LANES : (j + 1) * LANES], a)
        for j in range(lists.shape[1] // LANES)
    ]
    return jnp.concatenate(pieces, axis=1)


def packet_row(packet, half, vectors, width):
    mark = GROUP + vectors
    start = 2 * half * width
    return packet[mark : mark + 1, start : start + width].astype(jnp.int32)


def pair_merge_kernel(
    vectors,
    width,
    side_ref,
    part_ref,
    p0_ref,
    p1_ref,
    p2_ref,
    p3_ref,
    start_ref,
    full_ref,
    level_ref,
    gram_ref,
    spread,
):
    atoms = part_ref.shape[1]
    side = side_ref[...]
    packets = (p0_ref, p1_ref, p2_ref, p3_ref)
    for half in range(2):
        found = []
        for slot, n in enumerate((0, 1, 3)):
            lists = packet_row(packets[n], half, vectors, width)
            _, placed = placed_terms(side, packets, n, half, lists, atoms, width, vectors)
            spread_here = spread.at[half * 3 + slot]
            for a in range(3):
                spread_here[rows(a), :] = placed[a]
                if n == 0 and half == 0:
                    full_ref[rows(a), :] = part_ref[rows(a), :] + placed[a]
            start = 2 * half * width
            change = pack_rows([read_back(spread_here, lists, a) for a in range(3)], vectors)
            found.append(
                [packets[n][rows(g), start : start + width] + change[g] for g in range(2)]
            )
        for g in range(2):
            start = 2 * half * width
            level_ref[rows(g), start : start + width] = found[0][g]
            level_ref[rows(g), start + width : start + 2 * width] = jnp.where(
                side > 0.5, found[2][g], found[1][g]
            )
    total = jnp.zeros((2 * GROUP, LANES), jnp.float32)
    for a in range(3):
        stack = jnp.concatenate([start_ref[rows(a), :], full_ref[rows(a), :]], axis=0)
        stack = only_vectors(stack, vectors)
        total += inner(stack, stack)
    gram_ref[...] = pack_gram(
        jnp.concatenate([total, jnp.zeros((GROUP, LANES), jnp.float32)], axis=0),
        jnp.zeros((GROUP, LANES), jnp.float32),
    )


def repeat_rows(x, vectors):
    x = only_vectors(x, vectors)
    return x + pltpu.roll(x, vectors, 0)


def pair_gram_start_kernel(
    vectors,
    mine,
    other,
    got,
    list_ref,
    beyond_ref,
    gram_ref,
    beyond_gram,
    part_ref,
    packet_ref,
    beyond_part,
):
    width = list_ref.shape[1]
    parts = (part_ref, beyond_part)
    pair_packet(
        vectors,
        mine,
        other,
        got,
        pair_lists(vectors, list_ref, beyond_ref),
        parts,
        packet_ref,
        width,
    )
    squares = []
    for part in parts:
        total = None
        for a in range(3):
            value = repeat_rows(part[rows(a), :], vectors)
            found = shifted_products(value, value, vectors)
            total = found if total is None else [x + y for x, y in zip(total, found)]
        squares.append(from_shifted(total, vectors))
    gram = gram_ref[...] + beyond_gram[...]
    cut = slice(4 * width, 4 * width + LANES)
    packet_ref[rows(0), cut] = gram + pltpu.roll(squares[0] + squares[1], 4 * GROUP, 1)
    packet_ref[rows(1), cut] = jnp.zeros((GROUP, LANES), jnp.float32)


def pair_gram_merge_kernel(
    vectors,
    width,
    side_ref,
    p3_ref,
    p2_ref,
    part_ref,
    p0_ref,
    p1_ref,
    full_ref,
    gram_ref,
    spread,
):
    atoms = part_ref.shape[1]
    side = side_ref[...]
    packets = (p0_ref, p1_ref, p2_ref, p3_ref)
    shares = []
    for n in range(4):
        total = []
        for half in range(2):
            lists = packet_row(packets[n], half, vectors, width)
            terms, placed = placed_terms(side, packets, n, half, lists, atoms, width, vectors)
            spread_here = spread.at[2 * n + half]
            found = None
            start = 2 * half * width
            values = unpack_rows(packets[n], slice(start, start + width), vectors)
            for a in range(3):
                spread_here[rows(a), :] = placed[a]
                if n == 0 and half == 0:
                    full_ref[rows(a), :] = part_ref[rows(a), :] + placed[a]
                at = repeat_rows(values[a], vectors)
                products = shifted_products(
                    terms[a], at + at + read_back(spread_here, lists, a), vectors
                )
                found = products if found is None else [x + y for x, y in zip(found, products)]
            total.append(found)
        share = packets[n][rows(0), 4 * width : 4 * width + LANES]
        shares.append([share] + [x + y for x, y in zip(*total)])

    def add(x, y):
        return [p + q for p, q in zip(x, y)]

    total = add(add(shares[0], shares[1]), add(shares[2], shares[3]))
    gram_ref[...] = total[0] + pltpu.roll(from_shifted(total[1:], vectors), 4 * GROUP, 1)


def last_kernel(vectors, scale, start_ref, first_ref, second_ref, *refs):
    gram_refs, refs = refs[:-7], refs[-7:]
    next_hbm, diag_hbm, off_hbm, next_ref, diag_ref, off_ref, sems = refs
    shape = (GROUP, LANES)
    row = lax.broadcasted_iota(jnp.int32, shape, 0)
    lane = lax.broadcasted_iota(jnp.int32, shape, 1)
    levels = [ref[...] for ref in gram_refs]
    while len(levels) > 1:
        levels = [sum(levels[n : n + 2]) for n in range(0, len(levels), 2)]
    gram = levels[0] * scale
    size = range(vectors)

    def block(n):
        return [
            [
                jnp.broadcast_to(gram[i : i + 1, GROUP * n + j : GROUP * n + j + 1], shape)
                for j in size
            ]
            for i in size
        ]

    def total(terms):
        terms = [t for t in terms if t is not None]
        out = terms[0] if terms else None
        for term in terms[1:]:
            out = out + term
        return out

    def times(x, y):
        return None if x is None or y is None else x * y

    def mul(x, y):
        return [[total([times(x[i][k], y[k][j]) for k in size]) for j in size] for i in size]

    def even(x):
        return [[x[min(i, j)][max(i, j)] for j in size] for i in size]

    def mul_even(x, y):
        upper = [
            [total([times(x[i][k], y[k][j]) for k in size]) if j >= i else None for j in size]
            for i in size
        ]
        return even(upper)

    def add(x, y, sign=1.0):
        def join(p, q):
            if p is None or q is None:
                return (q if sign > 0 else None if q is None else -q) if p is None else p
            return p + q if sign > 0 else p - q

        return [[join(p, q) for p, q in zip(u, v)] for u, v in zip(x, y)]

    def flip(x):
        return [[x[j][i] for j in size] for i in size]

    def factor(m):
        m = [list(line) for line in m]
        lower = [[None] * vectors for _ in size]
        inverse = [[jnp.ones(shape, jnp.float32) if i == j else None for j in size] for i in size]
        for j in size:
            pivot = lax.rsqrt(m[j][j])
            for i in range(j, vectors):
                lower[i][j] = m[i][j] * pivot
            inverse[j] = [times(x, pivot) for x in inverse[j]]
            for i in range(j + 1, vectors):
                for k in range(j + 1, i + 1):
                    m[i][k] = m[i][k] - lower[i][j] * lower[k][j]
                for k in range(j + 1):
                    step = times(lower[i][j], inverse[j][k])
                    if step is not None:
                        old = inverse[i][k]
                        inverse[i][k] = -step if old is None else old - step
        return lower, inverse

    ss, su, uu, uq, qq = (block(n) for n in range(5))
    qq = [[0.5 * (qq[i][j] + qq[j][i]) for j in size] for i in size]
    _, p0 = factor(ss)
    p0t = flip(p0)
    a1 = mul_even(mul(p0, su), p0t)
    l1, p1 = factor(add(mul_even(mul(p0, uu), p0t), mul_even(a1, a1), -1.0))
    b = mul(p1, p0)
    a = [[-x for x in line] for line in mul(p1, mul(a1, p0))]
    at, bt, up1 = flip(a), flip(b), flip(l1)
    right_s = add(mul(su, at), mul(uu, bt))
    right_u = add(mul(uu, at), mul(uq, bt))
    right_q = add(mul(uq, at), mul(qq, bt))
    a2 = even(add(mul_even(a, right_s), mul_even(b, right_u)))
    ww = add(mul_even(a, right_u), mul_even(b, right_q))
    l2, p2 = factor(add(add(ww, mul_even(a2, a2), -1.0), mul_even(up1, l1), -1.0))
    up2 = flip(l2)
    weights = (
        [[-x for x in line] for line in mul(p2, add(mul(a2, a), mul(up1, p0)))],
        mul(p2, add(a, mul(a2, b), -1.0)),
        mul(p2, b),
    )

    def tile(x):
        out = jnp.zeros(shape, jnp.float32)
        for i in size:
            for j in size:
                if x[i][j] is not None:
                    out = jnp.where((row == i) & (lane == j), x[i][j], out)
        return out[:vectors, :vectors]

    def stacked(x, j):
        out = jnp.zeros(shape, jnp.float32)
        for i in size:
            if x[i][j] is not None:
                out = jnp.where(row == i, x[i][j], out)
        return jnp.concatenate([out] * (start_ref.shape[1] // LANES), axis=1)

    diag_ref[0] = tile(a1)
    diag_ref[1] = tile(a2)
    off_ref[0] = tile(up1)
    off_ref[1] = tile(up2)
    copies = [
        pltpu.make_async_copy(diag_ref, diag_hbm, sems.at[0]),
        pltpu.make_async_copy(off_ref, off_hbm, sems.at[1]),
    ]
    for copy in copies:
        copy.start()
    columns = [[stacked(weight, w) for w in size] for weight in weights]
    for comp in range(3):
        value = None
        for n, ref in enumerate((start_ref, first_ref, second_ref)):
            for w in size:
                line = GROUP * comp + w
                term = columns[n][w] * ref[line : line + 1, :]
                value = term if value is None else value + term
        next_ref[0, 0, 0, comp] = value[:vectors]
    copies.append(pltpu.make_async_copy(next_ref, next_hbm, sems.at[2]))
    copies[-1].start()
    for copy in copies:
        copy.wait()


def call(body, outs, args, scratch=(), flops=0, spaces=pltpu.VMEM, out_spaces=pltpu.VMEM):
    outs = [shape if isinstance(shape[0], tuple) else (shape, jnp.float32) for shape in outs]
    return pl.pallas_call(
        body,
        out_shape=[jax.ShapeDtypeStruct(shape, kind) for shape, kind in outs],
        in_specs=[pl.BlockSpec(memory_space=spaces)] * len(args),
        out_specs=[pl.BlockSpec(memory_space=out_spaces)] * len(outs),
        scratch_shapes=[
            pltpu.VMEM(shape, jnp.float32) if isinstance(shape, tuple) else shape
            for shape in scratch
        ],
        cost_estimate=pl.CostEstimate(flops=flops, bytes_accessed=0, transcendentals=0)
        if flops
        else None,
        compiler_params=pltpu.CompilerParams(vmem_limit_bytes=VMEM_BYTES),
    )(*args)


def table_index(neighbors, atoms, ghosts):
    entry = neighbors - atoms
    cell = entry // ghosts
    number = cell
    kept = [n for n in range(64) if not all(m in (1, 2) for m in (n // 16, n // 4 % 4, n % 4))]
    previous = -1
    for position, n in enumerate(kept):
        if n - previous > 1:
            number = number + jnp.where(cell >= position, n - previous - 1, 0)
        previous = n
    member = (number // 16, number // 4 % 4, number % 4)
    kind = 0
    octant = 0
    for bit, m in enumerate(member):
        kind = kind + jnp.where((m == 0) | (m == 3), 1 << bit, 0)
        octant = 2 * octant + (m + 1) % 2
    place = atoms + (kind - 1) * (8 * ghosts) + octant * ghosts + entry % ghosts
    return jnp.where(neighbors < atoms, neighbors, place)


def on_device(
    positions,
    species,
    start_block,
    neighbors,
    ghost_lists,
    embedding,
    radial_in,
    radial_out,
    readout,
):
    atoms = positions.shape[-1]
    ghosts = ghost_lists.shape[-1]
    vectors = start_block.shape[3]
    fanout = neighbors.shape[3]
    channels = embedding.shape[1]
    devices = lax.axis_size("gx") * lax.axis_size("gy") * lax.axis_size("gz")
    scale = 1.0 / (3.0 * atoms * devices)
    width = 8 * ghosts
    high = 3 * GROUP
    edges = fanout * atoms
    table_width = atoms + 7 * width
    ring = lax.axis_size("gx") == 4
    side = (octant_bit((GROUP, width), 0, ghosts) ^ (lax.axis_index("gx") % 2 == 1)).astype(
        jnp.float32
    )

    block = start_block[0, 0, 0]
    blank = jnp.zeros((GROUP - vectors - 1, atoms), jnp.float32)
    extra = jnp.concatenate(
        [
            species[0, 0].astype(jnp.float32),
            jnp.pad(ghost_lists.reshape(1, width).astype(jnp.float32), ((0, 0), (0, atoms - width))),
            blank[2:],
        ],
        axis=0,
    )
    own = jnp.concatenate(
        [
            part
            for a in range(3)
            for part in (block[:, a], positions[0, 0, 0, a : a + 1], extra if a == 0 else blank)
        ],
        axis=0,
    )
    octants, lists = call(
        functools.partial(pack_kernel, vectors),
        [(high, width), ((1, width), jnp.int32)],
        (own,),
    )
    basis, hidden = radial_in.shape
    index, low, inward, outward, columns = call(
        functools.partial(prepare_kernel, atoms, ghosts),
        [
            ((1, edges), jnp.int32),
            ((LANES, edges), jnp.bfloat16),
            ((hidden, LANES * (-(-6 * basis // LANES))), jnp.bfloat16),
            ((2 * channels, 2 * hidden), jnp.bfloat16),
            (channels, LANES),
        ],
        (neighbors.reshape(1, -1), embedding, radial_in, radial_out.T, readout.reshape(1, -1)),
        flops=2_000_000,
    )

    def spread(level):
        if level.shape[1] == width:
            level = jnp.concatenate([level, fetch_ghosts(level, 0, ghosts)], axis=1)
        return (level,) + spread_outer(level, ghosts)

    pairs = len(pair_list(fanout))
    shared = [
        (vectors * (fanout + pairs) * GROUP, atoms),
        ((fanout + pairs) * GROUP, atoms),
        (vectors * (fanout + pairs) * GROUP, atoms),
    ]
    base_sums = 2 * fanout + pairs + fanout * fanout
    saved_shapes = [
        (high, edges),
        (GROUP, edges),
        (GROUP * (-(-base_sums // 4)), atoms),
        (pairs * GROUP, atoms),
    ] + [(channels, edges)] * 5
    ghost_levels = spread(octants)
    results = call(
        functools.partial(first_kernel, ghosts, vectors, basis, embedding.shape[0]),
        [(2 * GROUP, table_width)] + saved_shapes,
        (index, own) + ghost_levels + (low, inward, outward, columns),
        [(high, table_width), (channels, edges), (channels, LANES)]
        + shared
        + [(base_sums * GROUP, atoms)],
    )
    terms, saved = results[0], results[1:]
    lifted = ring and lax.axis_size("gz") == 2

    def second_product(first, levels):
        return call(
            functools.partial(second_kernel, ghosts, vectors, len(levels)),
            [(2 * GROUP, table_width), (GROUP, LANES)],
            (index, first) + levels + (low,) + tuple(saved),
            [(high, table_width)] + shared,
        )

    def loose(terms):
        parts = [terms[GROUP // 2 * n : GROUP // 2 * (n + 1)] for n in range(3)]
        rest = jnp.zeros_like(parts[0])
        return jnp.concatenate([x for part in parts for x in (part, rest)], axis=0)

    if lifted:
        beyond = ghost_levels[2]

        def exchange(terms):
            other = lax.ppermute(terms, "gz", swap_pairs(2, 1))
            cut = [atoms + (kind - 1) * width for kind in range(9)]
            both = [
                x[:, cut[2] : cut[4]] + y[:, cut[6] : cut[8]]
                for x, y in ((terms, other), (other, terms))
            ]
            return other, return_ghosts(jnp.concatenate(both, axis=1), 1, ghosts)

        other, got = exchange(terms)
        part, packet = call(
            functools.partial(pair_start_kernel, vectors),
            [(high, atoms), (2 * GROUP, 4 * width)],
            (terms, other, got, lists, beyond),
            [(high, atoms)],
        )
        others = pair_exchange(packet, "gx", (1, 2, 3))
        first, level, gram = call(
            functools.partial(pair_merge_kernel, vectors, width),
            [(high, atoms), (2 * GROUP, 4 * width), (GROUP, LANES)],
            (side, part, packet, *others, own),
            [(6, high, atoms)],
        )
        terms, edge_gram = second_product(first, (level, fetch_ghosts(level, 1, ghosts)))
        gram = gram + jnp.roll(edge_gram, 3 * GROUP, axis=1)
        sent = jnp.concatenate([terms, jnp.pad(gram, ((0, GROUP), (0, 0)))], axis=1)
        other, got = exchange(sent)
        part, packet = call(
            functools.partial(pair_gram_start_kernel, vectors),
            [(high, atoms), (2 * GROUP, 4 * width + LANES)],
            (sent, other, got, lists, beyond, gram, other[:GROUP, table_width:]),
            [(high, atoms)],
        )
        others = pair_exchange(packet, "gx", (1, 2, 3))
        second, gram = call(
            functools.partial(pair_gram_merge_kernel, vectors, width),
            [(high, atoms), (GROUP, LANES)],
            (side, *others[:0:-1], part, packet, others[0]),
            [(8, high, atoms)],
        )
        gram = [sum_over(gram, AXES[1:2])]
    else:
        terms = loose(terms)
        own_terms, ghost_terms = terms[:, :atoms], terms[:, atoms:]
        sums, beside = return_outer(ghost_terms, width, ghosts)
        if ring:
            part, packet = call(
                functools.partial(start_kernel, vectors),
                [(high, atoms), (high, 2 * width)],
                (own_terms, sums, beside, lists),
            )
            others = pair_exchange(packet, "gx", (1, 2, 3))
            first, level = call(
                functools.partial(merge_kernel, vectors),
                [(high, atoms), (high, 2 * width)],
                (side, part, packet, *others),
                [(high, atoms)],
            )
        else:
            first, level = call(
                functools.partial(middle_kernel, vectors),
                [(high, atoms), (high, width)],
                (own_terms, sums + return_ghosts(beside, 0, ghosts), lists),
            )
        terms, edge_gram = second_product(first, spread(level))
        terms = loose(terms)
        own_terms, ghost_terms = terms[:, :atoms], terms[:, atoms:]
        sums, beside = return_outer(ghost_terms, width, ghosts)
        if ring:
            part, packet = call(
                functools.partial(gram_start_kernel, vectors),
                [(high, atoms), (high, 2 * width + LANES)],
                (own, first, own_terms, sums, beside, lists, edge_gram),
            )
            others = pair_exchange(packet, "gx", (1, 2, 3))
            second, gram = call(
                functools.partial(gram_merge_kernel, vectors),
                [(high, atoms), (GROUP, LANES)],
                (side, *others[:0:-1], part, packet, others[0]),
                [(high, atoms)],
            )
            gram = sum_across(gram)
        else:
            second, gram = call(
                functools.partial(gram_kernel, vectors),
                [(high, atoms), (GROUP, LANES)],
                (own, first, own_terms, sums + return_ghosts(beside, 0, ghosts), lists),
            )
            gram = [sum_over(gram, AXES)]
    shapes = [(1, 1, 1, 3, vectors, atoms), (2, vectors, vectors), (2, vectors, vectors)]
    following, diagonal, off = call(
        functools.partial(last_kernel, vectors, scale),
        shapes,
        (own, first, second, *gram),
        shapes + [pltpu.SemaphoreType.DMA((len(shapes),))],
        out_spaces=pltpu.HBM,
    )
    return following.transpose(0, 1, 2, 4, 3, 5), diagonal, off


def solution(mesh):
    return jax.shard_map(
        on_device,
        mesh=mesh,
        in_specs=(
            P("gx", "gy", "gz", None, None),
            P("gx", "gy", "gz", None),
            P("gx", "gy", "gz", None, None, None),
            P("gx", "gy", "gz", None, None),
            P("gx", "gy", "gz", None),
            P(),
            P(),
            P(),
            P(),
        ),
        out_specs=(P("gx", "gy", "gz", None, None, None), P(), P()),
        check_vma=False,
    )
```

```python
import functools
import math

import jax
import jax.numpy as jnp
import numpy as np
from jax import lax
from jax.experimental import pallas as pl
from jax.experimental.pallas import tpu as pltpu
from jax.sharding import PartitionSpec as P

SOFTEN = 0.25
CUTOFF = 4.0
HIGHEST = lax.Precision.HIGHEST
LANES = 128
GROUP = 8
AXES = ("gx", "gy", "gz")
VMEM_BYTES = 48 * 1024 * 1024


def swap_pairs(size, distance):
    return [(i, (i + distance) % size) for i in range(size)]


def octant_bit(shape, bit, ghosts):
    lane = lax.broadcasted_iota(jnp.int32, shape, 1) % (8 * ghosts)
    return (lane // ghosts // (4 >> bit)) % 2 == 1


def pair_exchange(x, axis, distances):
    size = lax.axis_size(axis)
    return [lax.ppermute(x, axis, [(i, i ^ d) for i in range(size)]) for d in distances]


def ring_sides(x, bit):
    axis = AXES[bit]
    size = lax.axis_size(axis)
    if size == 4:
        near, far = pair_exchange(x, axis, (1, 3))
        return near, far, lax.axis_index(axis) % 2 == 1
    above = lax.ppermute(x, axis, swap_pairs(size, -1))
    below = lax.ppermute(x, axis, swap_pairs(size, 1))
    return above, below, False


def fetch_ghosts(x, bit, ghosts):
    axis = AXES[bit]
    size = lax.axis_size(axis)
    if size == 1:
        return x
    if size == 2:
        return lax.ppermute(x, axis, swap_pairs(2, 1))
    near, far, odd = ring_sides(x, bit)
    return jnp.where(octant_bit(x.shape, bit, ghosts) ^ odd, far, near)


def return_ghosts(x, bit, ghosts):
    axis = AXES[bit]
    size = lax.axis_size(axis)
    if size == 1:
        return x
    if size == 2:
        return lax.ppermute(x, axis, swap_pairs(2, 1))
    near, far, odd = ring_sides(x, bit)
    return jnp.where(octant_bit(x.shape, bit, ghosts) == odd, far, near)


def spread_outer(level, ghosts):
    second = fetch_ghosts(level, 1, ghosts)
    level = jnp.concatenate([level, second], axis=1)
    return second, fetch_ghosts(level, 2, ghosts)


def return_outer(terms, width, ghosts):
    got = return_ghosts(terms[:, 3 * width :], 2, ghosts)
    inner = got[:, :width]
    first = terms[:, :width] + got[:, width : 2 * width]
    second = terms[:, width : 3 * width] + got[:, 2 * width :]
    got = return_ghosts(second, 1, ghosts)
    return inner + got[:, :width], first + got[:, width:]


def sum_over(x, axes):
    for axis in axes:
        size = lax.axis_size(axis)
        if size & (size - 1):
            x = lax.psum(x, axis)
            continue
        step = 1
        while step < size:
            x = x + lax.ppermute(x, axis, [(i, i ^ step) for i in range(size)])
            step *= 2
    return x


def sum_across(x):
    axes = AXES[1:]
    sizes = [lax.axis_size(axis) for axis in axes]
    if sizes != [4, 2]:
        return [sum_over(x, axes)]
    x = x + pair_exchange(x, axes[0], (1,))[0]
    count = sizes[0] * sizes[1]
    terms = [
        lax.ppermute(x, axes, [(i, i ^ d) for i in range(count)])
        for d in (2 * sizes[1], 1, 2 * sizes[1] + 1)
    ]
    return [x] + terms


def rows(a):
    return slice(GROUP * a, GROUP * (a + 1))


def gather_lanes(table, index_row, group):
    lane = jnp.broadcast_to(index_row % LANES, (GROUP, LANES))
    tile = jnp.broadcast_to(index_row // LANES, (GROUP, LANES))
    out = None
    for number in range(table.shape[1] // LANES):
        source = table[rows(group), number * LANES : (number + 1) * LANES]
        picked = jnp.take_along_axis(source, lane, axis=1, mode="promise_in_bounds")
        out = picked if out is None else jnp.where(tile == number, picked, out)
    return out


def column(line):
    size = line.shape[1]
    shape = (size, size)
    same = lax.broadcasted_iota(jnp.int32, shape, 0) == lax.broadcasted_iota(jnp.int32, shape, 1)
    return jnp.sum(jnp.where(same, line, 0.0), axis=1, keepdims=True)


def split_rows(y, vectors):
    high = y.astype(jnp.bfloat16).astype(jnp.float32)
    return high + pltpu.roll(y - high, vectors, 0)


def join_rows(y, vectors):
    return y + pltpu.roll(y, GROUP - vectors, 0)


def pack_rows(values, vectors):
    row = lax.broadcasted_iota(jnp.int32, values[0].shape, 0)
    return jnp.where(row < vectors, values[0], pltpu.roll(values[1], vectors, 0)), values[2]


def unpack_rows(ref, lanes, vectors):
    both = ref[rows(0), lanes]
    return [both, pltpu.roll(both, GROUP - vectors, 0), ref[rows(1), lanes]]


def pack_kernel(vectors, own_ref, oct_ref, list_ref):
    mark = vectors + 2
    width = oct_ref.shape[1]
    list_ref[...] = own_ref[mark : mark + 1, :width].astype(jnp.int32)
    pick_octants(own_ref, list_ref, oct_ref)
    row = lax.broadcasted_iota(jnp.int32, (GROUP, width), 0)
    oct_ref[rows(0), :] = jnp.where(
        row == mark, own_ref[mark : mark + 1, :width], oct_ref[rows(0), :]
    )


def prepare_kernel(
    atoms, ghosts, near_ref, emb_ref, rin_ref, rout_ref, read_ref, idx_ref, low_ref, in_ref, out_ref, col_ref
):
    index = table_index(near_ref[...], atoms, ghosts)
    idx_ref[...] = index
    low = lax.broadcasted_iota(jnp.int32, low_ref.shape, 0) == index % LANES
    low_ref[...] = jnp.where(low, 1.0, 0.0).astype(jnp.bfloat16)
    high, middle, rest = split_parts(rin_ref[...])
    stack = [high, middle, rest, high, middle, high]
    pad = in_ref.shape[1] - 6 * rin_ref.shape[0]
    stack = jnp.concatenate(stack + [jnp.zeros((pad, rin_ref.shape[1]), jnp.float32)], axis=0)
    in_ref[...] = jnp.transpose(stack).astype(jnp.bfloat16)
    high, rest, _ = split_parts(rout_ref[...])
    out_ref[...] = jnp.concatenate(
        [jnp.concatenate([high, high], axis=1), jnp.concatenate([rest, rest], axis=1)], axis=0
    ).astype(jnp.bfloat16)
    species = emb_ref.shape[0]
    lane = lax.broadcasted_iota(jnp.int32, col_ref.shape, 1)
    columns = jnp.broadcast_to(column(read_ref[...]), col_ref.shape)
    for n in range(species):
        columns = jnp.where(lane == n, column(emb_ref[n : n + 1, :]), columns)
    col_ref[...] = columns


def pick_octants(own_ref, list_ref, oct_ref):
    for j in range(list_ref.shape[1] // LANES):
        cut = slice(j * LANES, (j + 1) * LANES)
        for a in range(3):
            oct_ref[rows(a), cut] = gather_lanes(own_ref, list_ref[:, cut], a)


def add_octants(own, octants, lists, vectors):
    atoms = own.shape[1]
    width = lists.shape[1]
    keep = lax.broadcasted_iota(jnp.int32, octants.shape, 0) < vectors
    packed = split_rows(jnp.where(keep, octants, 0.0), vectors).astype(jnp.bfloat16)
    onehot = lax.broadcasted_iota(jnp.int32, (atoms, width), 0) == lists
    spread = lax.dot_general(
        packed,
        jnp.where(onehot, 1.0, 0.0).astype(jnp.bfloat16),
        (((1,), (1,)), ((), ())),
        preferred_element_type=jnp.float32,
    )
    return own + join_rows(spread, vectors)


def fill_table(table, own_ref, ghost_refs, vectors, ghosts, shifted):
    atoms = own_ref.shape[1]
    table[:, :atoms] = own_ref[...]
    width = 8 * ghosts
    places = [
        (ref, j * width) for ref in ghost_refs for j in range(ref.shape[1] // width)
    ]
    if len(ghost_refs) == 2:
        places = [places[n] for n in (0, 1, 4, 5, 2, 3, 6, 7)]
    for kind, (ref, start) in enumerate(places):
        if kind == 0:
            continue
        base = atoms + (kind - 1) * width
        if len(ghost_refs) == 2:
            for a, part in enumerate(unpack_rows(ref, slice(start, start + width), vectors)):
                table[rows(a), base : base + width] = part
            continue
        part = ref[:, start : start + width]
        if shifted:
            row = lax.broadcasted_iota(jnp.int32, part.shape, 0)
            for a in range(3):
                if (kind >> a) & 1:
                    move = jnp.where(octant_bit(part.shape, a, ghosts), -1.0, 1.0)
                    part = part + jnp.where(row == GROUP * a + vectors, move, 0.0)
        table[:, base : base + width] = part


def gather_slot(table, idx_ref, k, atoms):
    pieces = [[] for _ in range(3)]
    for j in range(atoms // LANES):
        index_row = idx_ref[:, pl.ds(pl.multiple_of(k * atoms + j * LANES, LANES), LANES)]
        for a in range(3):
            pieces[a].append(gather_lanes(table, index_row, a))
    return [jnp.concatenate(p, axis=1) for p in pieces]


def pair_list(fanout):
    return [(k, l) for k in range(fanout) for l in range(k, fanout)]


def lookup(table, fanout):
    where = {pair: n for n, pair in enumerate(pair_list(fanout))}
    return lambda k, l: table[where[min(k, l), max(k, l)]]


def sum_rows(parts):
    row = lax.broadcasted_iota(jnp.int32, parts[0].shape, 0)
    if len(parts) != 4 or GROUP != 8:
        out = jnp.zeros_like(parts[0])
        for n, part in enumerate(parts):
            out = jnp.where(row == n, jnp.sum(part, axis=0, keepdims=True), out)
        return out
    fold = [part + pltpu.roll(part, 4, 0) for part in parts]
    low = row < 4
    lead = jnp.where(low, fold[0], fold[1])
    rest = jnp.where(low, fold[2], fold[3])
    both = jnp.where(row % 4 < 2, lead + pltpu.roll(lead, 6, 0), rest + pltpu.roll(rest, 2, 0))
    even = both + pltpu.roll(both, 7, 0)
    odd = both + pltpu.roll(both, 1, 0)
    return jnp.where(row % 2 == 1, pltpu.roll(odd, 4, 0), even)


def dot3(x, y):
    return x[0] * y[0] + x[1] * y[1] + x[2] * y[2]


def slot_cut(k, atoms):
    return slice(k * atoms, (k + 1) * atoms)


def tile_rows(n):
    return slice(GROUP * n, GROUP * (n + 1))


def tangents(diffs, units, invs, tn, changes, vectors):
    fanout = len(diffs)
    pairs = pair_list(fanout)
    per_vector = fanout + len(pairs)
    taus = [dot3(units[k], diffs[k]) for k in range(fanout)]
    turns = [
        [(diffs[k][a] - units[k][a] * taus[k]) * invs[k] for a in range(3)] for k in range(fanout)
    ]
    values = list(taus)
    for k, l in pairs:
        half = dot3(units[k], turns[l])
        values.append(2.0 * half if k == l else half + dot3(units[l], turns[k]))
    for n, value in enumerate(values):
        changes[tile_rows(n), :] = value
        for v in range(vectors):
            tn[tile_rows(v * per_vector + n), :] = jnp.broadcast_to(
                value[v : v + 1, :], value.shape
            )


def channel_products(f, f1, q, rp, rpp, cosine, tn, acc, lanes, fanout, vectors):
    pairs = pair_list(fanout)
    per_vector = fanout + len(pairs)
    slots = range(fanout)
    rpp_q = [rpp[k] * q[k] for k in slots]
    rpp_f = [rpp[k] * f[k] for k in slots]
    for v in range(vectors):
        base = v * per_vector

        def tangent(n):
            return tn[tile_rows(base + n), lanes]

        phi = [f1[k] * tangent(k) for k in slots]
        index = {pair: fanout + n for n, pair in enumerate(pairs)}
        dq = []
        for k in slots:
            total = None
            for l in slots:
                term = phi[l] * cosine(k, l) + f[l] * tangent(index[min(k, l), max(k, l)])
                total = term if total is None else total + term
            dq.append(total)
        y = [phi[k] * rpp_q[k] + dq[k] * rpp_f[k] for k in slots]
        w = [y[k] * f[k] + rp[k] * phi[k] for k in slots]
        for k in slots:
            total = y[k] * q[k] + rp[k] * dq[k]
            for l in slots:
                total = total + w[l] * cosine(k, l)
            acc[tile_rows(base + k), lanes] += f1[k] * total
        for n, (k, l) in enumerate(pairs):
            term = w[k] * f[l] if k == l else w[k] * f[l] + w[l] * f[k]
            acc[tile_rows(base + fanout + n), lanes] += term


def finish_product(
    idx_ref, low_ref, unit_ref, inv_ref, sums_ref, acc, changes, diffs, terms_out, vectors
):
    fanout = len(diffs)
    atoms = idx_ref.shape[1] // fanout
    tiles = terms_out.shape[1] // LANES
    pairs = pair_list(fanout)
    per_vector = fanout + len(pairs)
    slots = range(fanout)
    row = lax.broadcasted_iota(jnp.int32, (GROUP, atoms), 0)
    outs = [
        sum_rows([acc[tile_rows(v * per_vector + n), :] for v in range(vectors)])
        for n in range(per_vector)
    ]
    taus = [changes[tile_rows(k), :] for k in slots]
    turned = lookup([changes[tile_rows(fanout + n), :] for n in range(len(pairs))], fanout)
    bent = lookup(outs[fanout:], fanout)
    units = [[unit_ref[rows(a), slot_cut(k, atoms)] for a in range(3)] for k in slots]
    invs = [inv_ref[:, slot_cut(k, atoms)] for k in slots]
    turns = [
        [(diffs[k][a] - units[k][a] * taus[k]) * invs[k] for a in range(3)] for k in slots
    ]

    def base_sum(n):
        line = (n // 4) * GROUP + n % 4
        return sums_ref[line : line + 1, :]

    stretch = [base_sum(k) for k in slots]
    curve = [base_sum(fanout + k) for k in slots]
    weight = lookup([base_sum(2 * fanout + n) for n in range(len(pairs))], fanout)
    mixed = [[base_sum(2 * fanout + len(pairs) + k * fanout + l) for l in slots] for k in slots]
    center = [jnp.zeros((GROUP, atoms), jnp.float32) for _ in range(3)]
    shifted = [jnp.zeros((GROUP, atoms), jnp.float32) for _ in range(vectors)]
    left = []
    for k in slots:
        along = outs[k] + curve[k] * taus[k]
        force = [0.0, 0.0, 0.0]
        change = [0.0, 0.0, 0.0]
        for l in slots:
            along = along + turned(k, l) * mixed[k][l]
            bend = bent(k, l) + taus[l] * mixed[l][k] + taus[k] * mixed[k][l]
            pull = weight(k, l)
            if k == l:
                bend = bend + bent(k, l)
                pull = pull + pull
            for a in range(3):
                force[a] = force[a] + pull * units[l][a]
                change[a] = change[a] + bend * units[l][a] + pull * turns[l][a]
        flat = dot3(units[k], force)
        inv = invs[k]
        along = (
            along
            - (dot3(units[k], change) + dot3(turns[k], force)) * inv
            + taus[k] * flat * (inv * inv)
        )
        keep = stretch[k] - flat * inv
        packed = []
        for a in range(3):
            y = (
                along * units[k][a]
                + keep * turns[k][a]
                + (change[a] - taus[k] * inv * force[a]) * inv
            )
            y = jnp.where(row < vectors, y, 0.0)
            center[a] = center[a] - y
            for n in range(vectors):
                other = y if n == 0 else pltpu.roll(y, n, 0)
                if n:
                    other = other + pltpu.roll(y, GROUP - vectors + n, 0)
                shifted[n] = shifted[n] + other * diffs[k][a]
            packed.append(split_rows(y, vectors))
        packed = jnp.concatenate(packed, axis=0)
        tile = idx_ref[:, slot_cut(k, atoms)] // LANES
        left.append(
            jnp.concatenate(
                [jnp.where(tile == number, packed, 0.0) for number in range(tiles)], axis=0
            ).astype(jnp.bfloat16)
        )
    spread = lax.dot_general(
        jnp.concatenate(left, axis=1),
        low_ref[...],
        (((1,), (1,)), ((), ())),
        preferred_element_type=jnp.float32,
    )
    own_tiles = atoms // LANES
    for number in range(tiles):
        cut = slice(number * LANES, (number + 1) * LANES)
        values = []
        for a in range(3):
            value = join_rows(spread[tile_rows(number * 3 + a)], vectors)
            if number < own_tiles:
                value = value + center[a][:, cut]
            values.append(value)
        terms_out[rows(0), cut], terms_out[rows(1), cut] = pack_rows(values, vectors)
    return shifted


def split_parts(x):
    high = x.astype(jnp.bfloat16).astype(jnp.float32)
    rest = x - high
    middle = rest.astype(jnp.bfloat16).astype(jnp.float32)
    low = (rest - middle).astype(jnp.bfloat16).astype(jnp.float32)
    return high, middle, low


def silu_slopes(x):
    sig = 0.5 + 0.5 * jnp.tanh(0.5 * x)
    anti = 1.0 - sig
    return sig, sig * (1.0 + x * anti), sig * anti * (2.0 + x * (anti - sig))


def half_turns(dist, inv, basis):
    shape = (basis, dist.shape[1])
    order = (lax.broadcasted_iota(jnp.int32, shape, 0) + 1).astype(jnp.float32)
    turns = order * (dist * (1.0 / CUTOFF))
    whole = jnp.floor(turns + 0.5)
    sign = 1.0 - 2.0 * (whole - 2.0 * jnp.floor(whole * 0.5))
    x = (turns - whole) * np.float32(np.pi)
    x2 = x * x

    def series(terms):
        value = terms[-1]
        for term in terms[-2::-1]:
            value = term + x2 * value
        return value

    sine = sign * x * series([(-1.0) ** n / math.factorial(2 * n + 1) for n in range(6)])
    cosine = sign * series([(-1.0) ** n / math.factorial(2 * n) for n in range(7)])
    omega = order * np.float32(np.pi / CUTOFF)
    b0 = sine * inv
    b1 = (omega * cosine - b0) * inv
    b2 = -(omega * omega * sine + 2.0 * b1) * inv
    return jnp.concatenate([b0, b1, b2], axis=1)


def first_kernel(
    ghosts,
    vectors,
    basis,
    species,
    idx_ref,
    own_ref,
    g1_ref,
    g2_ref,
    g3_ref,
    low_ref,
    in_ref,
    out_ref,
    col_ref,
    terms_out,
    unit_ref,
    inv_ref,
    sums_ref,
    cos_ref,
    f_ref,
    f1_ref,
    q_ref,
    rp_ref,
    rpp_ref,
    table,
    f2_ref,
    read_col,
    tn,
    changes,
    acc,
    acc2,
):
    atoms = own_ref.shape[1]
    fanout = idx_ref.shape[1] // atoms
    channels = col_ref.shape[0]
    pairs = pair_list(fanout)
    slots = range(fanout)
    embeds = [col_ref[:, n : n + 1] for n in range(species)]
    read_col[...] = jnp.broadcast_to(col_ref[:, species : species + 1], read_col.shape)
    fill_table(table, own_ref, (g1_ref, g2_ref, g3_ref), vectors, ghosts, True)

    def embed(kind):
        value = embeds[0]
        for n in range(1, species):
            value = jnp.where(kind == float(n), embeds[n], value)
        return value

    own_embed = embed(own_ref[vectors + 1 : vectors + 2, :])
    inward = in_ref[:, : 6 * basis]
    outward = out_ref[...]
    diffs, units, invs = [], [], []
    for k in slots:
        cut = slot_cut(k, atoms)
        near = gather_slot(table, idx_ref, k, atoms)
        diff = [near[a] - own_ref[rows(a), :] for a in range(3)]
        delta = [
            jnp.broadcast_to(diff[a][vectors : vectors + 1, :], (GROUP, atoms)) for a in range(3)
        ]
        dist = jnp.sqrt(dot3(delta, delta) + SOFTEN)
        inv = 1.0 / dist
        unit = [delta[a] * inv for a in range(3)]
        for a in range(3):
            unit_ref[rows(a), cut] = unit[a]
        inv_ref[:, cut] = inv
        diffs.append(diff)
        units.append(unit)
        invs.append(inv)
        one = dist[0:1]
        radii = half_turns(one, inv[0:1], basis)
        high, middle, rest = split_parts(radii)
        z = jnp.dot(
            inward,
            jnp.concatenate([high, high, high, middle, middle, rest], axis=0).astype(jnp.bfloat16),
            preferred_element_type=jnp.float32,
        )
        z0, z1, z2 = z[:, :atoms], z[:, atoms : 2 * atoms], z[:, 2 * atoms :]
        sig, slope, curve = silu_slopes(z0)
        hidden = jnp.concatenate([z0 * sig, slope * z1, curve * z1 * z1 + slope * z2], axis=1)
        high = hidden.astype(jnp.bfloat16)
        rest = (hidden - high.astype(jnp.float32)).astype(jnp.bfloat16)
        radial = jnp.dot(
            outward, jnp.concatenate([high, rest], axis=0), preferred_element_type=jnp.float32
        )
        radial = radial[:channels] + radial[channels:]
        r0, r1, r2 = radial[:, :atoms], radial[:, atoms : 2 * atoms], radial[:, 2 * atoms :]
        square = one * one
        base = 1.0 - square * (1.0 / CUTOFF**2)
        v0 = base * base
        v1 = base * one * (-4.0 / CUTOFF**2)
        v2 = -4.0 / CUTOFF**2 + square * (12.0 / CUTOFF**4)
        pair = own_embed * embed(near[0][vectors + 1 : vectors + 2, :])
        f_ref[:, cut] = pair * (r0 * v0)
        f1_ref[:, cut] = pair * (r1 * v0 + r0 * v1)
        f2_ref[:, cut] = pair * (r2 * v0 + 2.0 * (r1 * v1) + r0 * v2)
    for n, (k, l) in enumerate(pairs):
        cos_ref[tile_rows(n), :] = 1.0 + dot3(units[k], units[l])
    tangents(diffs, units, invs, tn, changes, vectors)
    acc[...] = jnp.zeros_like(acc)
    acc2[...] = jnp.zeros_like(acc2)
    share = 1.0 / fanout

    def tile(number, carry):
        here = pl.ds(pl.multiple_of(number * GROUP, GROUP), GROUP)
        for half in range(atoms // LANES):
            lanes = slice(half * LANES, (half + 1) * LANES)
            cuts = [slice(k * atoms + half * LANES, k * atoms + (half + 1) * LANES) for k in slots]
            cosine = lookup([cos_ref[tile_rows(n), lanes] for n in range(len(pairs))], fanout)
            f = [f_ref[here, cut] for cut in cuts]
            f1 = [f1_ref[here, cut] for cut in cuts]
            read = read_col[here, :] * share
            q, rp, rpp = [], [], []
            for k in slots:
                project = sum(f[l] * cosine(k, l) for l in slots)
                _, slope, curve = silu_slopes(f[k] * project * share)
                q.append(project)
                rp.append(read * slope)
                rpp.append(read * share * curve)
                q_ref[here, cuts[k]] = q[k]
                rp_ref[here, cuts[k]] = rp[k]
                rpp_ref[here, cuts[k]] = rpp[k]
            m = [rp[k] * f[k] for k in slots]
            slope = [rp[k] * q[k] + sum(m[l] * cosine(k, l) for l in slots) for k in slots]
            terms = [slope[k] * f1[k] for k in slots]
            terms += [slope[k] * f2_ref[here, cuts[k]] for k in slots]
            terms += [m[k] * f[l] if k == l else m[k] * f[l] + m[l] * f[k] for k, l in pairs]
            terms += [f1[k] * m[l] for k in slots for l in slots]
            for n, term in enumerate(terms):
                acc2[tile_rows(n), lanes] += term
            channel_products(f, f1, q, rp, rpp, cosine, tn, acc, lanes, fanout, vectors)
        return carry

    lax.fori_loop(0, channels // GROUP, tile, 0, unroll=2)
    count = acc2.shape[0] // GROUP
    for n in range(0, count, 4):
        parts = [acc2[tile_rows(min(n + j, count - 1)), :] for j in range(4)]
        sums_ref[tile_rows(n // 4), :] = sum_rows(parts)
    finish_product(
        idx_ref,
        low_ref,
        unit_ref,
        inv_ref,
        sums_ref,
        acc,
        changes,
        diffs,
        terms_out,
        vectors,
    )


def second_kernel(ghosts, vectors, levels, idx_ref, own_ref, *refs):
    ghost_refs, refs = refs[:levels], refs[levels:]
    low_ref, unit_ref, inv_ref, sums_ref, cos_ref, f_ref, f1_ref, q_ref, rp_ref, rpp_ref = refs[:10]
    terms_out, gram_out, table, tn, changes, acc = refs[10:]
    atoms = own_ref.shape[1]
    fanout = idx_ref.shape[1] // atoms
    channels = f_ref.shape[0]
    pairs = pair_list(fanout)
    slots = range(fanout)
    fill_table(table, own_ref, ghost_refs, vectors, ghosts, False)
    diffs = []
    for k in slots:
        near = gather_slot(table, idx_ref, k, atoms)
        diffs.append([near[a] - own_ref[rows(a), :] for a in range(3)])
    units = [[unit_ref[rows(a), slot_cut(k, atoms)] for a in range(3)] for k in slots]
    invs = [inv_ref[:, slot_cut(k, atoms)] for k in slots]
    tangents(diffs, units, invs, tn, changes, vectors)
    acc[...] = jnp.zeros_like(acc)

    def tile(number, carry):
        here = pl.ds(pl.multiple_of(number * GROUP, GROUP), GROUP)
        for half in range(atoms // LANES):
            lanes = slice(half * LANES, (half + 1) * LANES)
            cuts = [slice(k * atoms + half * LANES, k * atoms + (half + 1) * LANES) for k in slots]
            cosine = lookup([cos_ref[tile_rows(n), lanes] for n in range(len(pairs))], fanout)
            parts = [
                [ref[here, cut] for cut in cuts] for ref in (f_ref, f1_ref, q_ref, rp_ref, rpp_ref)
            ]
            channel_products(*parts, cosine, tn, acc, lanes, fanout, vectors)
        return carry

    lax.fori_loop(0, channels // GROUP, tile, 0, unroll=2)
    shifted = finish_product(
        idx_ref,
        low_ref,
        unit_ref,
        inv_ref,
        sums_ref,
        acc,
        changes,
        diffs,
        terms_out,
        vectors,
    )
    gram_out[...] = from_shifted(shifted, vectors)


def middle_kernel(vectors, own_ref, sums_ref, list_ref, full_ref, oct_ref):
    for a in range(3):
        full_ref[rows(a), :] = add_octants(
            own_ref[rows(a), :], sums_ref[rows(a), :], list_ref[...], vectors
        )
    pick_octants(full_ref, list_ref, oct_ref)


def inner(x, y, pad_to=LANES):
    pad = jnp.zeros((pad_to - y.shape[0], y.shape[1]), jnp.float32)
    return lax.dot_general(
        x,
        jnp.concatenate([y, pad], axis=0),
        (((1,), (1,)), ((), ())),
        precision=HIGHEST,
        preferred_element_type=jnp.float32,
    )


def only_vectors(x, vectors):
    row = lax.broadcasted_iota(jnp.int32, x.shape, 0)
    return jnp.where(row % GROUP < vectors, x, 0.0)


def pack_gram(total, edge):
    lane = lax.broadcasted_iota(jnp.int32, (GROUP, LANES), 1)
    out = total[rows(0)]
    out = jnp.where(lane >= 2 * GROUP, pltpu.roll(total[rows(1)], GROUP, 1), out)
    if edge is not None:
        out = jnp.where(lane >= 3 * GROUP, pltpu.roll(edge, 3 * GROUP, 1), out)
    return jnp.where(lane >= 4 * GROUP, pltpu.roll(total[rows(2)], 2 * GROUP, 1), out)


def gram_kernel(vectors, start_ref, first_ref, own_ref, sums_ref, list_ref, full_ref, gram_ref):
    total = jnp.zeros((3 * GROUP, LANES), jnp.float32)
    for a in range(3):
        second = add_octants(own_ref[rows(a), :], sums_ref[rows(a), :], list_ref[...], vectors)
        full_ref[rows(a), :] = second
        stack = jnp.concatenate([start_ref[rows(a), :], first_ref[rows(a), :], second], axis=0)
        stack = only_vectors(stack, vectors)
        total += inner(stack, stack)
    gram_ref[...] = pack_gram(total, None)


def packet_start(vectors, own_ref, sums_ref, ghost_ref, list_ref, part_ref, packet_ref):
    width = list_ref.shape[1]
    for a in range(3):
        part_ref[rows(a), :] = add_octants(
            own_ref[rows(a), :], sums_ref[rows(a), :], list_ref[...], vectors
        )
    mark = vectors + 1
    for j in range(width // LANES):
        cut = slice(j * LANES, (j + 1) * LANES)
        for a in range(3):
            value = gather_lanes(part_ref, list_ref[:, cut], a)
            if a == 0:
                row = lax.broadcasted_iota(jnp.int32, value.shape, 0)
                value = jnp.where(row == mark, list_ref[:, cut].astype(jnp.float32), value)
            packet_ref[rows(a), cut] = value
    packet_ref[:, width : 2 * width] = ghost_ref[...]


def arriving(side, packets, n, a, width):
    cut = slice(width, 2 * width)
    after, before = packets[(n + 1) % 4], packets[(n + 3) % 4]
    return jnp.where(side > 0.5, after[rows(a), cut], before[rows(a), cut])


def packet_lists(packet, vectors, width):
    mark = vectors + 1
    return packet[mark : mark + 1, :width].astype(jnp.int32)


def start_kernel(vectors, own_ref, sums_ref, ghost_ref, list_ref, part_ref, packet_ref):
    packet_start(vectors, own_ref, sums_ref, ghost_ref, list_ref, part_ref, packet_ref)


def merge_kernel(
    vectors, side_ref, part_ref, p0_ref, p1_ref, p2_ref, p3_ref, full_ref, level_ref, spread
):
    width = p0_ref.shape[1] // 2
    side = side_ref[...]
    packets = (p0_ref, p1_ref, p2_ref, p3_ref)
    lists = [packet_lists(p, vectors, width) for p in packets]
    for a in range(3):
        full_ref[rows(a), :] = add_octants(
            part_ref[rows(a), :], arriving(side, packets, 0, a, width), lists[0], vectors
        )
    near = []
    for n in (1, 3):
        for a in range(3):
            zero = jnp.zeros((GROUP, part_ref.shape[1]), jnp.float32)
            spread[rows(a), :] = add_octants(
                zero, arriving(side, packets, n, a, width), lists[n], vectors
            )
        values = []
        for a in range(3):
            pieces = [
                gather_lanes(spread, lists[n][:, j * LANES : (j + 1) * LANES], a)
                for j in range(width // LANES)
            ]
            values.append(packets[n][rows(a), :width] + jnp.concatenate(pieces, axis=1))
        near.append(values)
    for a in range(3):
        for j in range(width // LANES):
            cut = slice(j * LANES, (j + 1) * LANES)
            level_ref[rows(a), cut] = gather_lanes(full_ref, lists[0][:, cut], a)
        level_ref[rows(a), width : 2 * width] = jnp.where(side > 0.5, near[1][a], near[0][a])


def gram_start_kernel(
    vectors,
    start_ref,
    first_ref,
    own_ref,
    sums_ref,
    ghost_ref,
    list_ref,
    edge_ref,
    part_ref,
    packet_ref,
):
    packet_start(vectors, own_ref, sums_ref, ghost_ref, list_ref, part_ref, packet_ref)
    width = list_ref.shape[1]
    total = jnp.zeros((3 * GROUP, LANES), jnp.float32)
    for a in range(3):
        stack = jnp.concatenate(
            [start_ref[rows(a), :], first_ref[rows(a), :], part_ref[rows(a), :]], axis=0
        )
        stack = only_vectors(stack, vectors)
        total += inner(stack, stack)
    cut = slice(2 * width, 2 * width + LANES)
    packet_ref[rows(0), cut] = pack_gram(total, edge_ref[...])
    packet_ref[GROUP : 3 * GROUP, cut] = jnp.zeros((2 * GROUP, LANES), jnp.float32)


def shifted_products(x, y, vectors):
    return [x * (pltpu.roll(y, n, 0) if n else y) for n in range(vectors)]


def from_shifted(shifted, vectors):
    shape = (GROUP, LANES)
    row = lax.broadcasted_iota(jnp.int32, shape, 0)
    lane = lax.broadcasted_iota(jnp.int32, shape, 1)
    total = jnp.zeros(shape, jnp.float32)
    for n in range(vectors):
        value = jnp.sum(shifted[n], axis=1, keepdims=True)
        total = jnp.where(lane == (row + vectors - n) % vectors, value, total)
    return jnp.where((row < vectors) & (lane < vectors), total, 0.0)


def gram_merge_kernel(
    vectors, side_ref, p3_ref, p2_ref, part_ref, p0_ref, p1_ref, full_ref, gram_ref, spread
):
    width = (p0_ref.shape[1] - LANES) // 2
    atoms = part_ref.shape[1]
    side = side_ref[...]
    packets = (p0_ref, p1_ref, p2_ref, p3_ref)
    shares = []
    for n in range(4):
        lists = packet_lists(packets[n], vectors, width)
        terms = [only_vectors(arriving(side, packets, n, a, width), vectors) for a in range(3)]
        packed = jnp.concatenate([split_rows(t, vectors) for t in terms], axis=0)
        onehot = lax.broadcasted_iota(jnp.int32, (atoms, width), 0) == lists
        placed = lax.dot_general(
            packed.astype(jnp.bfloat16),
            jnp.where(onehot, 1.0, 0.0).astype(jnp.bfloat16),
            (((1,), (1,)), ((), ())),
            preferred_element_type=jnp.float32,
        )
        total = None
        for a in range(3):
            value = join_rows(placed[rows(a)], vectors)
            spread[rows(a), :] = value
            if n == 0:
                full_ref[rows(a), :] = part_ref[rows(a), :] + value
            at = only_vectors(packets[n][rows(a), :width], vectors)
            at = at + pltpu.roll(at, vectors, 0)
            back = jnp.concatenate(
                [
                    gather_lanes(spread, lists[:, j * LANES : (j + 1) * LANES], a)
                    for j in range(width // LANES)
                ],
                axis=1,
            )
            found = shifted_products(terms[a], at + at + back, vectors)
            total = found if total is None else [x + y for x, y in zip(total, found)]
        shares.append([packets[n][rows(0), 2 * width : 2 * width + LANES]] + total)

    def add(x, y):
        return [p + q for p, q in zip(x, y)]

    total = add(add(shares[0], shares[1]), add(shares[2], shares[3]))
    gram_ref[...] = total[0] + pltpu.roll(from_shifted(total[1:], vectors), 4 * GROUP, 1)


def pair_sums(mine, other, got, width, atoms, vectors):
    def tile(ref, kind):
        start = atoms + (kind - 1) * width
        return ref[:, start : start + width]

    def back(n):
        return got[:, n * width : (n + 1) * width]

    def pick(first, second, n):
        return (
            unpack_rows(first, slice(0, atoms), vectors),
            tile(second, 4) + back(n),
            tile(first, 1) + tile(second, 5) + back(n + 1),
        )

    return pick(mine, other, 0), pick(other, mine, 2)


def pair_packet(vectors, mine, other, got, lists, parts, packet, width):
    atoms = parts[0].shape[1]
    for n, (own, sums, beside) in enumerate(pair_sums(mine, other, got, width, atoms, vectors)):
        base = 2 * n * width
        for a, value in enumerate(unpack_rows(sums, slice(0, width), vectors)):
            parts[n][rows(a), :] = add_octants(own[a], value, lists[n], vectors)
        packet[:, base + width : base + 2 * width] = beside
        first, last = pack_rows([read_back(parts[n], lists[n], a) for a in range(3)], vectors)
        row = lax.broadcasted_iota(jnp.int32, last.shape, 0)
        packet[rows(0), base : base + width] = first
        packet[rows(1), base : base + width] = jnp.where(
            row == vectors, lists[n].astype(jnp.float32), last
        )


def pair_lists(vectors, list_ref, beyond_ref):
    row = vectors + 2
    width = list_ref.shape[1]
    return list_ref[...], beyond_ref[row : row + 1, :width].astype(jnp.int32)


def pair_start_kernel(
    vectors, mine, other, got, list_ref, beyond_ref, part_ref, packet_ref, beyond_part
):
    pair_packet(
        vectors,
        mine,
        other,
        got,
        pair_lists(vectors, list_ref, beyond_ref),
        (part_ref, beyond_part),
        packet_ref,
        list_ref.shape[1],
    )


def placed_terms(side, packets, n, half, lists, atoms, width, vectors):
    start = (2 * half + 1) * width
    after, before = packets[(n + 1) % 4], packets[(n + 3) % 4]
    cut = slice(start, start + width)
    arrived = jnp.where(
        jnp.concatenate([side, side], axis=0) > 0.5, after[:, cut], before[:, cut]
    )
    terms = [
        only_vectors(t, vectors) for t in unpack_rows(arrived, slice(0, width), vectors)
    ]
    packed = jnp.concatenate([split_rows(t, vectors) for t in terms], axis=0)
    onehot = lax.broadcasted_iota(jnp.int32, (atoms, width), 0) == lists
    placed = lax.dot_general(
        packed.astype(jnp.bfloat16),
        jnp.where(onehot, 1.0, 0.0).astype(jnp.bfloat16),
        (((1,), (1,)), ((), ())),
        preferred_element_type=jnp.float32,
    )
    return terms, [join_rows(placed[rows(a)], vectors) for a in range(3)]


def read_back(ref, lists, a):
    pieces = [
        gather_lanes(ref, lists[:, j * LANES : (j + 1) * LANES], a)
        for j in range(lists.shape[1] // LANES)
    ]
    return jnp.concatenate(pieces, axis=1)


def packet_row(packet, half, vectors, width):
    mark = GROUP + vectors
    start = 2 * half * width
    return packet[mark : mark + 1, start : start + width].astype(jnp.int32)


def pair_merge_kernel(
    vectors,
    width,
    side_ref,
    part_ref,
    p0_ref,
    p1_ref,
    p2_ref,
    p3_ref,
    start_ref,
    full_ref,
    level_ref,
    gram_ref,
    spread,
):
    atoms = part_ref.shape[1]
    side = side_ref[...]
    packets = (p0_ref, p1_ref, p2_ref, p3_ref)
    for half in range(2):
        found = []
        for slot, n in enumerate((0, 1, 3)):
            lists = packet_row(packets[n], half, vectors, width)
            _, placed = placed_terms(side, packets, n, half, lists, atoms, width, vectors)
            spread_here = spread.at[half * 3 + slot]
            for a in range(3):
                spread_here[rows(a), :] = placed[a]
                if n == 0 and half == 0:
                    full_ref[rows(a), :] = part_ref[rows(a), :] + placed[a]
            start = 2 * half * width
            change = pack_rows([read_back(spread_here, lists, a) for a in range(3)], vectors)
            found.append(
                [packets[n][rows(g), start : start + width] + change[g] for g in range(2)]
            )
        for g in range(2):
            start = 2 * half * width
            level_ref[rows(g), start : start + width] = found[0][g]
            level_ref[rows(g), start + width : start + 2 * width] = jnp.where(
                side > 0.5, found[2][g], found[1][g]
            )
    total = jnp.zeros((2 * GROUP, LANES), jnp.float32)
    for a in range(3):
        stack = jnp.concatenate([start_ref[rows(a), :], full_ref[rows(a), :]], axis=0)
        stack = only_vectors(stack, vectors)
        total += inner(stack, stack)
    gram_ref[...] = pack_gram(
        jnp.concatenate([total, jnp.zeros((GROUP, LANES), jnp.float32)], axis=0),
        jnp.zeros((GROUP, LANES), jnp.float32),
    )


def repeat_rows(x, vectors):
    x = only_vectors(x, vectors)
    return x + pltpu.roll(x, vectors, 0)


def pair_gram_start_kernel(
    vectors,
    mine,
    other,
    got,
    list_ref,
    beyond_ref,
    gram_ref,
    beyond_gram,
    part_ref,
    packet_ref,
    beyond_part,
):
    width = list_ref.shape[1]
    parts = (part_ref, beyond_part)
    pair_packet(
        vectors,
        mine,
        other,
        got,
        pair_lists(vectors, list_ref, beyond_ref),
        parts,
        packet_ref,
        width,
    )
    squares = []
    for part in parts:
        total = None
        for a in range(3):
            value = repeat_rows(part[rows(a), :], vectors)
            found = shifted_products(value, value, vectors)
            total = found if total is None else [x + y for x, y in zip(total, found)]
        squares.append(from_shifted(total, vectors))
    gram = gram_ref[...] + beyond_gram[...]
    cut = slice(4 * width, 4 * width + LANES)
    packet_ref[rows(0), cut] = gram + pltpu.roll(squares[0] + squares[1], 4 * GROUP, 1)
    packet_ref[rows(1), cut] = jnp.zeros((GROUP, LANES), jnp.float32)


def pair_gram_merge_kernel(
    vectors,
    width,
    side_ref,
    p3_ref,
    p2_ref,
    part_ref,
    p0_ref,
    p1_ref,
    full_ref,
    gram_ref,
    spread,
):
    atoms = part_ref.shape[1]
    side = side_ref[...]
    packets = (p0_ref, p1_ref, p2_ref, p3_ref)
    shares = []
    for n in range(4):
        total = []
        for half in range(2):
            lists = packet_row(packets[n], half, vectors, width)
            terms, placed = placed_terms(side, packets, n, half, lists, atoms, width, vectors)
            spread_here = spread.at[2 * n + half]
            found = None
            start = 2 * half * width
            values = unpack_rows(packets[n], slice(start, start + width), vectors)
            for a in range(3):
                spread_here[rows(a), :] = placed[a]
                if n == 0 and half == 0:
                    full_ref[rows(a), :] = part_ref[rows(a), :] + placed[a]
                at = repeat_rows(values[a], vectors)
                products = shifted_products(
                    terms[a], at + at + read_back(spread_here, lists, a), vectors
                )
                found = products if found is None else [x + y for x, y in zip(found, products)]
            total.append(found)
        share = packets[n][rows(0), 4 * width : 4 * width + LANES]
        shares.append([share] + [x + y for x, y in zip(*total)])

    def add(x, y):
        return [p + q for p, q in zip(x, y)]

    total = add(add(shares[0], shares[1]), add(shares[2], shares[3]))
    gram_ref[...] = total[0] + pltpu.roll(from_shifted(total[1:], vectors), 4 * GROUP, 1)


def last_kernel(vectors, scale, start_ref, first_ref, second_ref, *refs):
    gram_refs, refs = refs[:-7], refs[-7:]
    next_hbm, diag_hbm, off_hbm, next_ref, diag_ref, off_ref, sems = refs
    shape = (GROUP, LANES)
    row = lax.broadcasted_iota(jnp.int32, shape, 0)
    lane = lax.broadcasted_iota(jnp.int32, shape, 1)
    levels = [ref[...] for ref in gram_refs]
    while len(levels) > 1:
        levels = [sum(levels[n : n + 2]) for n in range(0, len(levels), 2)]
    gram = levels[0] * scale
    size = range(vectors)

    def block(n):
        return [
            [
                jnp.broadcast_to(gram[i : i + 1, GROUP * n + j : GROUP * n + j + 1], shape)
                for j in size
            ]
            for i in size
        ]

    def total(terms):
        terms = [t for t in terms if t is not None]
        out = terms[0] if terms else None
        for term in terms[1:]:
            out = out + term
        return out

    def times(x, y):
        return None if x is None or y is None else x * y

    def mul(x, y):
        return [[total([times(x[i][k], y[k][j]) for k in size]) for j in size] for i in size]

    def even(x):
        return [[x[min(i, j)][max(i, j)] for j in size] for i in size]

    def mul_even(x, y):
        upper = [
            [total([times(x[i][k], y[k][j]) for k in size]) if j >= i else None for j in size]
            for i in size
        ]
        return even(upper)

    def add(x, y, sign=1.0):
        def join(p, q):
            if p is None or q is None:
                return (q if sign > 0 else None if q is None else -q) if p is None else p
            return p + q if sign > 0 else p - q

        return [[join(p, q) for p, q in zip(u, v)] for u, v in zip(x, y)]

    def flip(x):
        return [[x[j][i] for j in size] for i in size]

    def factor(m):
        m = [list(line) for line in m]
        lower = [[None] * vectors for _ in size]
        inverse = [[jnp.ones(shape, jnp.float32) if i == j else None for j in size] for i in size]
        for j in size:
            pivot = lax.rsqrt(m[j][j])
            for i in range(j, vectors):
                lower[i][j] = m[i][j] * pivot
            inverse[j] = [times(x, pivot) for x in inverse[j]]
            for i in range(j + 1, vectors):
                for k in range(j + 1, i + 1):
                    m[i][k] = m[i][k] - lower[i][j] * lower[k][j]
                for k in range(j + 1):
                    step = times(lower[i][j], inverse[j][k])
                    if step is not None:
                        old = inverse[i][k]
                        inverse[i][k] = -step if old is None else old - step
        return lower, inverse

    ss, su, uu, uq, qq = (block(n) for n in range(5))
    qq = [[0.5 * (qq[i][j] + qq[j][i]) for j in size] for i in size]
    _, p0 = factor(ss)
    p0t = flip(p0)
    a1 = mul_even(mul(p0, su), p0t)
    l1, p1 = factor(add(mul_even(mul(p0, uu), p0t), mul_even(a1, a1), -1.0))
    b = mul(p1, p0)
    a = [[-x for x in line] for line in mul(p1, mul(a1, p0))]
    at, bt, up1 = flip(a), flip(b), flip(l1)
    right_s = add(mul(su, at), mul(uu, bt))
    right_u = add(mul(uu, at), mul(uq, bt))
    right_q = add(mul(uq, at), mul(qq, bt))
    a2 = even(add(mul_even(a, right_s), mul_even(b, right_u)))
    ww = add(mul_even(a, right_u), mul_even(b, right_q))
    l2, p2 = factor(add(add(ww, mul_even(a2, a2), -1.0), mul_even(up1, l1), -1.0))
    up2 = flip(l2)
    weights = (
        [[-x for x in line] for line in mul(p2, add(mul(a2, a), mul(up1, p0)))],
        mul(p2, add(a, mul(a2, b), -1.0)),
        mul(p2, b),
    )

    def tile(x):
        out = jnp.zeros(shape, jnp.float32)
        for i in size:
            for j in size:
                if x[i][j] is not None:
                    out = jnp.where((row == i) & (lane == j), x[i][j], out)
        return out[:vectors, :vectors]

    def stacked(x, j):
        out = jnp.zeros(shape, jnp.float32)
        for i in size:
            if x[i][j] is not None:
                out = jnp.where(row == i, x[i][j], out)
        return jnp.concatenate([out] * (start_ref.shape[1] // LANES), axis=1)

    diag_ref[0] = tile(a1)
    diag_ref[1] = tile(a2)
    off_ref[0] = tile(up1)
    off_ref[1] = tile(up2)
    copies = [
        pltpu.make_async_copy(diag_ref, diag_hbm, sems.at[0]),
        pltpu.make_async_copy(off_ref, off_hbm, sems.at[1]),
    ]
    for copy in copies:
        copy.start()
    columns = [[stacked(weight, w) for w in size] for weight in weights]
    for comp in range(3):
        value = None
        for n, ref in enumerate((start_ref, first_ref, second_ref)):
            for w in size:
                line = GROUP * comp + w
                term = columns[n][w] * ref[line : line + 1, :]
                value = term if value is None else value + term
        next_ref[0, 0, 0, comp] = value[:vectors]
    copies.append(pltpu.make_async_copy(next_ref, next_hbm, sems.at[2]))
    copies[-1].start()
    for copy in copies:
        copy.wait()


def call(body, outs, args, scratch=(), flops=0, spaces=pltpu.VMEM, out_spaces=pltpu.VMEM):
    outs = [shape if isinstance(shape[0], tuple) else (shape, jnp.float32) for shape in outs]
    return pl.pallas_call(
        body,
        out_shape=[jax.ShapeDtypeStruct(shape, kind) for shape, kind in outs],
        in_specs=[pl.BlockSpec(memory_space=spaces)] * len(args),
        out_specs=[pl.BlockSpec(memory_space=out_spaces)] * len(outs),
        scratch_shapes=[
            pltpu.VMEM(shape, jnp.float32) if isinstance(shape, tuple) else shape
            for shape in scratch
        ],
        cost_estimate=pl.CostEstimate(flops=flops, bytes_accessed=0, transcendentals=0)
        if flops
        else None,
        compiler_params=pltpu.CompilerParams(vmem_limit_bytes=VMEM_BYTES),
    )(*args)


def table_index(neighbors, atoms, ghosts):
    entry = neighbors - atoms
    cell = entry // ghosts
    number = cell
    kept = [n for n in range(64) if not all(m in (1, 2) for m in (n // 16, n // 4 % 4, n % 4))]
    previous = -1
    for position, n in enumerate(kept):
        if n - previous > 1:
            number = number + jnp.where(cell >= position, n - previous - 1, 0)
        previous = n
    member = (number // 16, number // 4 % 4, number % 4)
    kind = 0
    octant = 0
    for bit, m in enumerate(member):
        kind = kind + jnp.where((m == 0) | (m == 3), 1 << bit, 0)
        octant = 2 * octant + (m + 1) % 2
    place = atoms + (kind - 1) * (8 * ghosts) + octant * ghosts + entry % ghosts
    return jnp.where(neighbors < atoms, neighbors, place)


def on_device(
    positions,
    species,
    start_block,
    neighbors,
    ghost_lists,
    embedding,
    radial_in,
    radial_out,
    readout,
):
    atoms = positions.shape[-1]
    ghosts = ghost_lists.shape[-1]
    vectors = start_block.shape[3]
    fanout = neighbors.shape[3]
    channels = embedding.shape[1]
    devices = lax.axis_size("gx") * lax.axis_size("gy") * lax.axis_size("gz")
    scale = 1.0 / (3.0 * atoms * devices)
    width = 8 * ghosts
    high = 3 * GROUP
    edges = fanout * atoms
    table_width = atoms + 7 * width
    ring = lax.axis_size("gx") == 4
    side = (octant_bit((GROUP, width), 0, ghosts) ^ (lax.axis_index("gx") % 2 == 1)).astype(
        jnp.float32
    )

    block = start_block[0, 0, 0]
    blank = jnp.zeros((GROUP - vectors - 1, atoms), jnp.float32)
    extra = jnp.concatenate(
        [
            species[0, 0].astype(jnp.float32),
            jnp.pad(ghost_lists.reshape(1, width).astype(jnp.float32), ((0, 0), (0, atoms - width))),
            blank[2:],
        ],
        axis=0,
    )
    own = jnp.concatenate(
        [
            part
            for a in range(3)
            for part in (block[:, a], positions[0, 0, 0, a : a + 1], extra if a == 0 else blank)
        ],
        axis=0,
    )
    octants, lists = call(
        functools.partial(pack_kernel, vectors),
        [(high, width), ((1, width), jnp.int32)],
        (own,),
    )
    basis, hidden = radial_in.shape
    index, low, inward, outward, columns = call(
        functools.partial(prepare_kernel, atoms, ghosts),
        [
            ((1, edges), jnp.int32),
            ((LANES, edges), jnp.bfloat16),
            ((hidden, LANES * (-(-6 * basis // LANES))), jnp.bfloat16),
            ((2 * channels, 2 * hidden), jnp.bfloat16),
            (channels, LANES),
        ],
        (neighbors.reshape(1, -1), embedding, radial_in, radial_out.T, readout.reshape(1, -1)),
        flops=2_000_000,
    )

    def spread(level):
        if level.shape[1] == width:
            level = jnp.concatenate([level, fetch_ghosts(level, 0, ghosts)], axis=1)
        return (level,) + spread_outer(level, ghosts)

    pairs = len(pair_list(fanout))
    shared = [
        (vectors * (fanout + pairs) * GROUP, atoms),
        ((fanout + pairs) * GROUP, atoms),
        (vectors * (fanout + pairs) * GROUP, atoms),
    ]
    base_sums = 2 * fanout + pairs + fanout * fanout
    saved_shapes = [
        (high, edges),
        (GROUP, edges),
        (GROUP * (-(-base_sums // 4)), atoms),
        (pairs * GROUP, atoms),
    ] + [(channels, edges)] * 5
    ghost_levels = spread(octants)
    results = call(
        functools.partial(first_kernel, ghosts, vectors, basis, embedding.shape[0]),
        [(2 * GROUP, table_width)] + saved_shapes,
        (index, own) + ghost_levels + (low, inward, outward, columns),
        [(high, table_width), (channels, edges), (channels, LANES)]
        + shared
        + [(base_sums * GROUP, atoms)],
    )
    terms, saved = results[0], results[1:]
    lifted = ring and lax.axis_size("gz") == 2

    def second_product(first, levels):
        return call(
            functools.partial(second_kernel, ghosts, vectors, len(levels)),
            [(2 * GROUP, table_width), (GROUP, LANES)],
            (index, first) + levels + (low,) + tuple(saved),
            [(high, table_width)] + shared,
        )

    def loose(terms):
        parts = [terms[GROUP // 2 * n : GROUP // 2 * (n + 1)] for n in range(3)]
        rest = jnp.zeros_like(parts[0])
        return jnp.concatenate([x for part in parts for x in (part, rest)], axis=0)

    if lifted:
        beyond = ghost_levels[2]

        def exchange(terms):
            other = lax.ppermute(terms, "gz", swap_pairs(2, 1))
            cut = [atoms + (kind - 1) * width for kind in range(9)]
            both = [
                x[:, cut[2] : cut[4]] + y[:, cut[6] : cut[8]]
                for x, y in ((terms, other), (other, terms))
            ]
            return other, return_ghosts(jnp.concatenate(both, axis=1), 1, ghosts)

        other, got = exchange(terms)
        part, packet = call(
            functools.partial(pair_start_kernel, vectors),
            [(high, atoms), (2 * GROUP, 4 * width)],
            (terms, other, got, lists, beyond),
            [(high, atoms)],
        )
        others = pair_exchange(packet, "gx", (1, 2, 3))
        first, level, gram = call(
            functools.partial(pair_merge_kernel, vectors, width),
            [(high, atoms), (2 * GROUP, 4 * width), (GROUP, LANES)],
            (side, part, packet, *others, own),
            [(6, high, atoms)],
        )
        terms, edge_gram = second_product(first, (level, fetch_ghosts(level, 1, ghosts)))
        gram = gram + jnp.roll(edge_gram, 3 * GROUP, axis=1)
        sent = jnp.concatenate([terms, jnp.pad(gram, ((0, GROUP), (0, 0)))], axis=1)
        other, got = exchange(sent)
        part, packet = call(
            functools.partial(pair_gram_start_kernel, vectors),
            [(high, atoms), (2 * GROUP, 4 * width + LANES)],
            (sent, other, got, lists, beyond, gram, other[:GROUP, table_width:]),
            [(high, atoms)],
        )
        others = pair_exchange(packet, "gx", (1, 2, 3))
        second, gram = call(
            functools.partial(pair_gram_merge_kernel, vectors, width),
            [(high, atoms), (GROUP, LANES)],
            (side, *others[:0:-1], part, packet, others[0]),
            [(8, high, atoms)],
        )
        gram = [sum_over(gram, AXES[1:2])]
    else:
        terms = loose(terms)
        own_terms, ghost_terms = terms[:, :atoms], terms[:, atoms:]
        sums, beside = return_outer(ghost_terms, width, ghosts)
        if ring:
            part, packet = call(
                functools.partial(start_kernel, vectors),
                [(high, atoms), (high, 2 * width)],
                (own_terms, sums, beside, lists),
            )
            others = pair_exchange(packet, "gx", (1, 2, 3))
            first, level = call(
                functools.partial(merge_kernel, vectors),
                [(high, atoms), (high, 2 * width)],
                (side, part, packet, *others),
                [(high, atoms)],
            )
        else:
            first, level = call(
                functools.partial(middle_kernel, vectors),
                [(high, atoms), (high, width)],
                (own_terms, sums + return_ghosts(beside, 0, ghosts), lists),
            )
        terms, edge_gram = second_product(first, spread(level))
        terms = loose(terms)
        own_terms, ghost_terms = terms[:, :atoms], terms[:, atoms:]
        sums, beside = return_outer(ghost_terms, width, ghosts)
        if ring:
            part, packet = call(
                functools.partial(gram_start_kernel, vectors),
                [(high, atoms), (high, 2 * width + LANES)],
                (own, first, own_terms, sums, beside, lists, edge_gram),
            )
            others = pair_exchange(packet, "gx", (1, 2, 3))
            second, gram = call(
                functools.partial(gram_merge_kernel, vectors),
                [(high, atoms), (GROUP, LANES)],
                (side, *others[:0:-1], part, packet, others[0]),
                [(high, atoms)],
            )
            gram = sum_across(gram)
        else:
            second, gram = call(
                functools.partial(gram_kernel, vectors),
                [(high, atoms), (GROUP, LANES)],
                (own, first, own_terms, sums + return_ghosts(beside, 0, ghosts), lists),
            )
            gram = [sum_over(gram, AXES)]
    shapes = [(1, 1, 1, 3, vectors, atoms), (2, vectors, vectors), (2, vectors, vectors)]
    following, diagonal, off = call(
        functools.partial(last_kernel, vectors, scale),
        shapes,
        (own, first, second, *gram),
        shapes + [pltpu.SemaphoreType.DMA((len(shapes),))],
        out_spaces=pltpu.HBM,
    )
    return following.transpose(0, 1, 2, 4, 3, 5), diagonal, off


def solution(mesh):
    return jax.shard_map(
        on_device,
        mesh=mesh,
        in_specs=(
            P("gx", "gy", "gz", None, None),
            P("gx", "gy", "gz", None),
            P("gx", "gy", "gz", None, None, None),
            P("gx", "gy", "gz", None, None),
            P("gx", "gy", "gz", None),
            P(),
            P(),
            P(),
            P(),
        ),
        out_specs=(P("gx", "gy", "gz", None, None, None), P(), P()),
        check_vma=False,
    )
```
